32 devices in a mesh: dp: 2 (over x), context: 4 (over y, core), expert: 4 (over z).
Axes of the slice: x: 2, y: 2, z: 4, core: 2. Of those that a mesh axis runs over, the one named last changes fastest.
Arguments:
- prompt_in: bfloat16 [8, 1024, 768], P(('dp', 'expert'), 'context'), may hold values from -6 to 6
- cont_in: bfloat16 [8, 2, 512, 768], P(('dp', 'expert'), None, 'context'), may hold values from -6 to 6
- prompt_route: int32 [8, 1024, 2], P(('dp', 'expert'), 'context'), may hold values from 0 to 3, all different within a row
- cont_route: int32 [8, 2, 512, 2], P(('dp', 'expert'), None, 'context'), may hold values from 0 to 3, all different within a row
- order: int32 [8, 4, 512], P(('dp', 'expert'), 'context'), may hold values from 0 to 511, each once within a row
- buckets: int32 [1536], replicated, may hold values from 0 to 31
- attn_gain: float32 [768], replicated, may hold values from 0.1 to 1.9
- w_query: bfloat16 [768, 768], replicated, may hold values from -0.21875 to 0.21875
- w_key: bfloat16 [768, 768], replicated, may hold values from -0.21875 to 0.21875
- w_value: bfloat16 [768, 768], replicated, may hold values from -0.21875 to 0.21875
- w_attn_out: bfloat16 [768, 768], replicated, may hold values from -0.625 to 0.625
- rel_bias: float32 [32, 12], replicated, may hold values from -4 to 4
- ffn_gain: float32 [768], replicated, may hold values from 0.1 to 1.9
- router: bfloat16 [768, 4], replicated, may hold values from -0.109375 to 0.109375
- w_in: bfloat16 [4, 768, 3072], P('expert'), may hold values from -0.21875 to 0.21875
- w_out: bfloat16 [4, 3072, 768], P('expert'), may hold values from -0.21875 to 0.21875
- prompt_cot: bfloat16 [8, 1024, 768], P(('dp', 'expert'), 'context'), may hold values from -6 to 6
- cont_cot: bfloat16 [8, 2, 512, 768], P(('dp', 'expert'), None, 'context'), may hold values from -6 to 6
Outputs:
- prompt_out: bfloat16 [8, 1024, 768], P(('dp', 'expert'), 'context')
- cont_out: bfloat16 [8, 2, 512, 768], P(('dp', 'expert'), None, 'context')
- prompt_dx: float32 [8, 1024, 768], P(('dp', 'expert'), 'context')
- cont_dx: float32 [8, 2, 512, 768], P(('dp', 'expert'), None, 'context')
- g_attn_gain: float32 [768], replicated
- g_w_query: float32 [768, 768], replicated
- g_w_key: float32 [768, 768], replicated
- g_w_value: float32 [768, 768], replicated
- g_w_attn_out: float32 [768, 768], replicated
- g_rel_bias: float32 [32, 12], replicated
- g_ffn_gain: float32 [768], replicated
- g_router: float32 [768, 4], replicated
- g_w_in: float32 [4, 768, 3072], P('expert', ('dp', 'context'))
- g_w_out: float32 [4, 3072, 768], P('expert', ('dp', 'context'))
The draws below stay inside these ranges and needn't reach their ends.
Inputs may be any that keep to these rules, and one draw needn't show every extreme that they name: `prompt_route`: each token's 2 experts differ. `cont_route`: each token's 2 experts differ. `order`: each block's row lists each of its 512 tokens once.
All inputs are finite; a program needn't handle non-finite values.
Results may differ from the reference program's by a relative error of at most 0.015.
Values may be sent and summed in bfloat16 or wider, within the bound.
A program may use at most 384 MiB of HBM per device.

```python
from functools import partial
import jax
import jax.numpy as jnp
from jax import lax

D = 768
H = 12
HD = 64
FF = 3072
NB = 32
TOP = 2
CONT = 2
PCH = 256
CCH = 128
EXPERTS = 4
PROMPT = 1024
CLEN = 512
TOK = 512
SPAN = 1536
GROUPS = 8
CAP = 288
N_CONTEXT = 4


def touch_ends(values, stream_key, low, high):
    longest = values.shape.index(max(values.shape))
    spots = []
    for shift in (0, 1):
        where = [jax.random.randint(jax.random.fold_in(stream_key, axis), (), 0, length) for axis, length in enumerate(values.shape)]
        where[longest] = (where[longest] + shift) % values.shape[longest]
        spots.append(tuple(where))
    return values.at[spots[0]].set(low).at[spots[1]].set(high)


def block_scale(stream_key, extent, split, smallest, high):
    level, own = 1.0, jax.random.fold_in(stream_key, 6)
    for axis_at, shards_of in split:
        heights = jnp.exp(jax.random.uniform(jax.random.fold_in(own, axis_at), (shards_of,), jnp.float32, smallest / len(split), high / len(split)))
        level = level * jnp.repeat(heights, extent[axis_at] // shards_of).reshape([-1 if axis == axis_at else 1 for axis in range(len(extent))])
    return level


def choose_distinct(key, rows, amount, top, lift):
    order = jax.random.permutation(jax.random.fold_in(key, 1), amount)
    favour = order
    for power in range(3):
        favour = favour * favour // amount
    favour = favour * lift // amount
    chance = jax.random.randint(jax.random.fold_in(key, 2), (rows, amount), 0, 4096) + favour
    holders = jax.random.permutation(jax.random.fold_in(key, 3), rows)[jnp.arange(amount) % rows]
    chance = jnp.where(jnp.arange(rows)[:, None] == holders[None, :], 1 << 14, chance)
    score = chance * amount + jnp.arange(amount)
    return lax.top_k(score.astype(jnp.int32), top)[1].astype(jnp.int32)


def scatter_about(stream_key, dims, deviation, bound, shards=(), held_as=jnp.bfloat16):
    level = block_scale(stream_key, dims, shards, -0.22, 0.18) if shards else 1.0
    array = jax.random.normal(stream_key, dims, jnp.float32) * deviation * level
    return jnp.minimum(jnp.maximum(array, -bound), bound).astype(held_as)


def setup_inputs(seed: int = 0) -> dict:
    seeds = jax.random.split(jax.random.key(seed), 19)
    prompt_in = scatter_about(seeds[0], (GROUPS, PROMPT, D), 1.0, 6.0, ((0, 8), (1, 4)))
    cont_in = scatter_about(seeds[1], (GROUPS, CONT, CLEN, D), 1.0, 6.0, ((0, 8), (2, 4)))
    prompt_route = choose_distinct(seeds[2], GROUPS * PROMPT, EXPERTS, TOP, 4096).reshape((GROUPS, PROMPT, TOP))
    cont_route = choose_distinct(seeds[3], GROUPS * CONT * CLEN, EXPERTS, TOP, 4096).reshape((GROUPS, CONT, CLEN, TOP))
    order = jax.vmap(lambda own: jax.random.permutation(own, TOK))(jax.random.split(seeds[4], GROUPS * N_CONTEXT)).reshape((GROUPS, N_CONTEXT, TOK)).astype(jnp.int32)
    buckets = touch_ends(jax.random.randint(seeds[5], (SPAN,), 0, NB), jax.random.fold_in(seeds[5], 1), 0, NB - 1).astype(jnp.int32)
    attn_gain = jnp.clip(1.0 + 0.18 * jax.random.normal(seeds[6], (D,), jnp.float32), 0.1, 1.9)
    w_query = scatter_about(seeds[7], (D, D), D ** -0.5, 0.21875)
    w_key = scatter_about(seeds[8], (D, D), D ** -0.5, 0.21875)
    w_value = scatter_about(seeds[9], (D, D), D ** -0.5, 0.21875)
    w_attn_out = scatter_about(seeds[10], (D, D), (D // 8) ** -0.5, 0.625)
    rel_bias = scatter_about(seeds[11], (NB, H), 1.0, 4.0, (), jnp.float32)
    ffn_gain = jnp.clip(1.0 + 0.18 * jax.random.normal(seeds[12], (D,), jnp.float32), 0.1, 1.9)
    router = scatter_about(seeds[13], (D, EXPERTS), (4 * D) ** -0.5, 0.109375)
    w_in = scatter_about(seeds[14], (EXPERTS, D, FF), D ** -0.5, 0.21875, ((0, 4),))
    w_out = scatter_about(seeds[15], (EXPERTS, FF, D), (FF // 4) ** -0.5, 0.21875, ((0, 4),))
    prompt_cot = scatter_about(seeds[16], (GROUPS, PROMPT, D), 1.0, 6.0, ((0, 8), (1, 4)))
    cont_cot = scatter_about(seeds[17], (GROUPS, CONT, CLEN, D), 1.0, 6.0, ((0, 8), (2, 4)))
    return dict(prompt_in=prompt_in, cont_in=cont_in, prompt_route=prompt_route, cont_route=cont_route, order=order, buckets=buckets, attn_gain=attn_gain, w_query=w_query, w_key=w_key, w_value=w_value, w_attn_out=w_attn_out, rel_bias=rel_bias, ffn_gain=ffn_gain, router=router, w_in=w_in, w_out=w_out, prompt_cot=prompt_cot, cont_cot=cont_cot)


@jax.custom_vjp
def low(v):
    return lax.optimization_barrier(v.astype(jnp.bfloat16)).astype(jnp.float32)

@jax.custom_vjp
def low_back(v):
    return v

def low_keep(v):
    return (low(v), None)

def low_pass(kept, grad):
    return (grad,)

def back_keep(v):
    return (v, None)

def back_low(kept, grad):
    return (low(grad),)
low.defvjp(low_keep, low_pass)
low_back.defvjp(back_keep, back_low)
EPSILON = 1e-06
PRECISE = lax.Precision.HIGHEST
MASKED = -1e+30

def rms_scale(values, gain):
    return values * lax.rsqrt(lax.optimization_barrier(jnp.mean(values * values, axis=-1, keepdims=True)) + EPSILON) * gain

def gelu_tanh(values):
    return jax.nn.gelu(values, approximate=True)

def slot_plan(route, ranking, experts, capacity):
    rows_count = route.shape[0]
    top_k = route.shape[1]
    ranked = route[ranking]
    flat_route = ranked.T.reshape(-1)
    hot_rows = (flat_route[:, None] == jnp.arange(experts, dtype=jnp.int32)[None, :]).astype(jnp.int32)
    position = lax.optimization_barrier(jnp.sum((jnp.cumsum(hot_rows, axis=0) - hot_rows) * hot_rows, axis=1))
    slot_index = jnp.where(position < capacity, flat_route * capacity + position, experts * capacity).astype(jnp.int32)
    pick_index = jnp.arange(top_k * rows_count, dtype=jnp.int32) // rows_count
    anchor = jnp.tile(ranking, top_k) * top_k + pick_index
    destination = jnp.zeros((rows_count * top_k,), jnp.int32).at[anchor].set(slot_index).reshape(rows_count, top_k)
    source = jnp.full((experts * capacity + 1,), rows_count * top_k, jnp.int32).at[slot_index].set(anchor)[:experts * capacity]
    return (destination, source)

def to_blocks(prompt_part, cont_part):
    groups = prompt_part.shape[0]
    tail = prompt_part.shape[-1]
    prompt_blocks = prompt_part.reshape(groups, N_CONTEXT, PCH, tail)
    cont_blocks = cont_part.reshape(groups, CONT, N_CONTEXT, CCH, tail).transpose(0, 2, 1, 3, 4)
    cont_blocks = cont_blocks.reshape(groups, N_CONTEXT, CONT * CCH, tail)
    return jnp.concatenate([prompt_blocks, cont_blocks], axis=2)

def from_blocks(blocked):
    groups = blocked.shape[0]
    tail = blocked.shape[-1]
    prompt_part = blocked[:, :, :PCH].reshape(groups, PROMPT, tail)
    cont_part = blocked[:, :, PCH:].reshape(groups, N_CONTEXT, CONT, CCH, tail).transpose(0, 2, 1, 3, 4)
    return (prompt_part, cont_part.reshape(groups, CONT, CLEN, tail))

def group_attention(group_items, table, positions, sequences):
    queries, keys, values = group_items
    total_rows = queries.shape[0]
    distance = jnp.maximum(positions[:, None] - positions[None, :], 0)
    allowed = ((sequences[None, :] < 0) | (sequences[None, :] == sequences[:, None])) & (positions[None, :] <= positions[:, None])

    def per_head(head_items):
        query_head, key_head, value_head, table_head = head_items
        scores = jnp.dot(query_head, key_head.T, precision=PRECISE) * HD ** (-0.5) + table_head[distance]
        scores = low_back(scores)
        scores = jnp.where(allowed, scores, MASKED)
        probability = jax.nn.softmax(scores, axis=-1)
        return jnp.dot(low(probability), value_head, precision=PRECISE)

    def by_head(matrix):
        return matrix.reshape(total_rows, H, HD).transpose(1, 0, 2)
    mixed = lax.map(jax.checkpoint(per_head), (by_head(queries), by_head(keys), by_head(values), table))
    return mixed.transpose(1, 0, 2).reshape(total_rows, D)

def expert_apply(expert_items):
    rows, weight_in, weight_out = expert_items
    before = low_back(jnp.dot(rows, weight_in, precision=PRECISE))
    activated = low(gelu_tanh(before))
    return low(low_back(jnp.dot(activated, weight_out, precision=PRECISE)))

def reference(prompt_in, cont_in, prompt_route, cont_route, order, buckets, attn_gain, w_query, w_key, w_value, w_attn_out, rel_bias, ffn_gain, router, w_in, w_out, prompt_cot, cont_cot):
    groups = prompt_in.shape[0]
    routes = to_blocks(prompt_route, cont_route)
    destination, source = jax.vmap(jax.vmap(partial(slot_plan, experts=EXPERTS, capacity=CAP)))(routes, order)
    route_hot = (routes[..., None] == jnp.arange(EXPERTS, dtype=jnp.int32)).astype(jnp.float32)
    positions = jnp.concatenate([jnp.arange(PROMPT, dtype=jnp.int32), PROMPT + jnp.tile(jnp.arange(CLEN, dtype=jnp.int32), CONT)])
    sequences = jnp.concatenate([jnp.full((PROMPT,), -1, jnp.int32), jnp.repeat(jnp.arange(CONT, dtype=jnp.int32), CLEN)])
    bucket_hot = (buckets[:, None] == jnp.arange(NB, dtype=jnp.int32)[None, :]).astype(jnp.float32)
    anchor_rows = (source // TOP)[..., None]
    dest_rows = destination.reshape(groups, N_CONTEXT, TOK * TOP)[..., None]

    def forward(prompt_x, cont_x, gain_one, query_w, key_w, value_w, out_w, bias_w, gain_two, router_w, inner_w, outer_w):
        hidden = jnp.concatenate([prompt_x, cont_x.reshape(groups, CONT * CLEN, D)], axis=1)
        normed = low(rms_scale(hidden, gain_one))

        def project(weight):
            return low(low_back(jnp.einsum('gtd,de->gte', normed, weight, precision=PRECISE)))
        queries = project(query_w)
        keys = project(key_w)
        values = project(value_w)
        table = jnp.dot(bucket_hot, bias_w, precision=PRECISE).T
        attend = jax.checkpoint(partial(group_attention, table=table, positions=positions, sequences=sequences))
        mixed = low(low_back(lax.map(attend, (queries, keys, values))))
        middle = hidden + low_back(jnp.einsum('gtd,de->gte', mixed, out_w, precision=PRECISE))
        second = low(rms_scale(middle, gain_two))
        logits = jnp.einsum('gtd,de->gte', second, router_w, precision=PRECISE)

        def blocked(whole):
            return to_blocks(whole[:, :PROMPT], whole[:, PROMPT:].reshape(groups, CONT, CLEN, whole.shape[-1]))
        second_blocks = blocked(second)
        logit_blocks = blocked(logits)
        chosen = jnp.einsum('gctke,gcte->gctk', route_hot, logit_blocks, precision=PRECISE)
        gates = jax.nn.softmax(chosen, axis=-1)
        padded = jnp.concatenate([second_blocks, jnp.zeros((groups, N_CONTEXT, 1, D), jnp.float32)], axis=2)
        sent = low_back(jnp.take_along_axis(padded, anchor_rows, axis=2))
        rows = sent.reshape(groups * N_CONTEXT, EXPERTS, CAP, D).transpose(1, 0, 2, 3).reshape(EXPERTS, groups * N_CONTEXT * CAP, D)
        made = lax.map(jax.checkpoint(expert_apply), (rows, inner_w, outer_w))
        made = made.reshape(EXPERTS, groups, N_CONTEXT, CAP, D).transpose(1, 2, 0, 3, 4).reshape(groups, N_CONTEXT, EXPERTS * CAP, D)
        made = jnp.concatenate([made, jnp.zeros((groups, N_CONTEXT, 1, D), jnp.float32)], axis=2)
        picked = jnp.take_along_axis(made, dest_rows, axis=2).reshape(groups, N_CONTEXT, TOK, TOP, D)
        moe = lax.optimization_barrier(jnp.sum(gates[..., None] * picked, axis=3))
        moe_prompt, moe_cont = from_blocks(moe)
        return (middle[:, :PROMPT] + moe_prompt, middle[:, PROMPT:].reshape(groups, CONT, CLEN, D) + moe_cont)
    primals = tuple((item.astype(jnp.float32) for item in (prompt_in, cont_in, attn_gain, w_query, w_key, w_value, w_attn_out, rel_bias, ffn_gain, router, w_in, w_out)))
    outputs, pull = jax.vjp(forward, *primals)
    grads = pull((prompt_cot.astype(jnp.float32), cont_cot.astype(jnp.float32)))
    return (outputs[0].astype(jnp.bfloat16), outputs[1].astype(jnp.bfloat16), grads[0], grads[1], grads[2], grads[3], grads[4], grads[5], grads[6], grads[7], grads[8], grads[9], grads[10], grads[11])
```

```python
import functools

import jax
import jax.numpy as jnp
from jax import lax
from jax.experimental import pallas as pl
from jax.experimental.pallas import tpu as pltpu
from jax.sharding import PartitionSpec as P

HD = 64
BK = 256
EPSILON = 1e-06
MASKED = -1e30
F32 = jnp.float32
BF16 = jnp.bfloat16
PRECISE = lax.Precision.HIGHEST
VMEM = pltpu.VMEM
MIB = 1 << 20


def dot(a, b):
    return lax.dot_general(a, b, (((1,), (0,)), ((), ())), preferred_element_type=F32)


def dot_nt(a, b):
    return lax.dot_general(a, b, (((1,), (1,)), ((), ())), preferred_element_type=F32)


def dot_tn(a, b):
    return lax.dot_general(a, b, (((0,), (0,)), ((), ())), preferred_element_type=F32)


def split_dot(a, b, op):
    high = a.astype(BF16)
    low = (a - high.astype(F32)).astype(BF16)
    return op(high, b) + op(low, b)


def full(shape):
    return pl.BlockSpec(shape, lambda *_: (0,) * len(shape))


class Layout:
    def __init__(self, spread, prompt_rows, cont_count, cont_rows):
        assert prompt_rows == BK and BK % cont_rows == 0
        self.spread = spread
        self.prompt_rows = prompt_rows
        self.cont_count = cont_count
        self.cont_rows = cont_rows
        self.tokens = prompt_rows + cont_count * cont_rows
        self.per_cont = spread * cont_rows // BK
        self.blocks = spread + cont_count * self.per_cont
        self.total = self.blocks * BK
        self.keys, self.place, self.pieces = [], [], []
        for p in range(spread):
            self.keys.append(list(range(p + 1)))
            self.place.append(p)
            self.pieces.append([(p, 0, 0, BK)])
        each = BK // cont_rows
        for j in range(cont_count):
            for m in range(self.per_cont):
                first = spread + j * self.per_cont
                self.keys.append(list(range(spread)) + list(range(first, first + m + 1)))
                self.place.append(spread + m)
                self.pieces.append(
                    [
                        (m * each + n, prompt_rows + j * cont_rows, n * cont_rows, cont_rows)
                        for n in range(each)
                    ]
                )
        self.tile = {}
        for q in range(self.blocks):
            for k in self.keys[q]:
                self.tile[(q, k)] = len(self.tile)
        self.tiles = len(self.tile)
        self.distances = spread + self.per_cont

    def distance(self, q, k):
        return self.place[q] - self.place[k]


def plan_kernel(
    experts, capacity, route_ref, route_t_ref, order_row_ref, order_col_ref, dz_ref, rows_ref, cols_ref, dzp_ref
):
    tokens = dz_ref.shape[0]
    slots = experts * capacity
    side = (tokens, tokens)
    lane = lax.broadcasted_iota(jnp.int32, side, 1)
    sub = lax.broadcasted_iota(jnp.int32, side, 0)
    rank_col = jnp.sum(
        jnp.where(order_row_ref[...] == sub, lane, 0).astype(F32), axis=1, keepdims=True
    )
    rank_row = jnp.sum(
        jnp.where(order_col_ref[...] == lane, sub, 0).astype(F32), axis=0, keepdims=True
    )
    before = jnp.where(rank_row < rank_col, 1.0, 0.0).astype(BF16)
    before_t = jnp.where(rank_col < rank_row, 1.0, 0.0).astype(BF16)
    expert_lane = lax.broadcasted_iota(jnp.int32, (tokens, 128), 1)
    hots = [jnp.where(route_ref[:, i : i + 1] == expert_lane, 1.0, 0.0) for i in range(2)]
    counts = [dot(before, hot.astype(BF16)) for hot in hots]
    counts[1] = counts[1] + jnp.sum(hots[0], axis=0, keepdims=True)
    expert_sub = lax.broadcasted_iota(jnp.int32, (16, tokens), 0)
    hots_t = [jnp.where(route_t_ref[i : i + 1, :] == expert_sub, 1.0, 0.0) for i in range(2)]
    counts_t = [dot(hot.astype(BF16), before_t) for hot in hots_t]
    counts_t[1] = counts_t[1] + jnp.sum(hots_t[0], axis=1, keepdims=True)
    slot_rows = []
    cols = jnp.full((tokens, 128), -1, jnp.int32)
    for i in range(2):
        pos = jnp.sum(hots[i] * counts[i], axis=1, keepdims=True).astype(jnp.int32)
        slot = jnp.where(pos < capacity, route_ref[:, i : i + 1] * capacity + pos, -1)
        cols = jnp.where(expert_lane == i, slot, cols)
        pos = jnp.sum(hots_t[i] * counts_t[i], axis=0, keepdims=True).astype(jnp.int32)
        slot_rows.append(jnp.where(pos < capacity, route_t_ref[i : i + 1, :] * capacity + pos, -1))
    cols_ref[...] = cols
    sub8 = lax.broadcasted_iota(jnp.int32, (8, tokens), 0)
    rows_ref[...] = jnp.where(sub8 == 0, slot_rows[0], jnp.where(sub8 == 1, slot_rows[1], -1))
    dz = dz_ref[...]
    for start in range(0, slots, 128):
        number = lax.broadcasted_iota(jnp.int32, (128, tokens), 0) + start
        first = jnp.where(slot_rows[0] == number, 1.0, 0.0)
        second = jnp.where(slot_rows[1] == number, 1.0, 0.0)
        dzp_ref[start : start + 128, : dz.shape[1]] = dot((first + second).astype(BF16), dz).astype(BF16)
        other = dot(first.astype(BF16), hots[1].astype(BF16)) + dot(
            second.astype(BF16), hots[0].astype(BF16)
        )
        dzp_ref[start : start + 128, dz.shape[1] :] = other.astype(BF16)


def plan(routes, ranking, upstream, experts, capacity):
    tokens, width = upstream.shape
    return pl.pallas_call(
        functools.partial(plan_kernel, experts, capacity),
        out_shape=(
            jax.ShapeDtypeStruct((8, tokens), jnp.int32),
            jax.ShapeDtypeStruct((tokens, 128), jnp.int32),
            jax.ShapeDtypeStruct((experts * capacity, width + 128), BF16),
        ),
        compiler_params=pltpu.CompilerParams(vmem_limit_bytes=32 * MIB),
        name="slot_plan",
    )(routes, routes.T, ranking.reshape(1, tokens), ranking.reshape(tokens, 1), upstream)


def toeplitz_tile(table_row, d):
    line = jnp.concatenate(
        [table_row[:, (d + 1) * BK : (d + 2) * BK], table_row[:, d * BK : (d + 1) * BK]], axis=1
    )
    tile = jnp.broadcast_to(line, (8, 2 * BK))
    row = lax.broadcasted_iota(jnp.int32, (8, 2 * BK), 0)
    for bit in (1, 2, 4):
        tile = jnp.where((row & bit) > 0, pltpu.roll(tile, bit, 1), tile)
    height = 8
    while height < BK:
        tile = jnp.concatenate([tile, pltpu.roll(tile, height, 1)], axis=0)
        height *= 2
    tile = tile[:, :BK]
    if d == 0:
        key = lax.broadcasted_iota(jnp.int32, (BK, BK), 0)
        query = lax.broadcasted_iota(jnp.int32, (BK, BK), 1)
        tile = jnp.where(query >= key, tile, MASKED)
    return tile


def diagonal_sums(tile):
    tile = jnp.concatenate([tile, jnp.zeros((BK, BK), F32)], axis=1)
    height = BK
    while height > 8:
        height //= 2
        tile = tile[:height] + pltpu.roll(tile[height:], 2 * BK - height, 1)
    row = lax.broadcasted_iota(jnp.int32, (8, 2 * BK), 0)
    for bit in (1, 2, 4):
        tile = jnp.where((row & bit) > 0, pltpu.roll(tile, 2 * BK - bit, 1), tile)
    return jnp.sum(tile, axis=0, keepdims=True)


def attention_kernel(
    lay, heads, x_ref, gain_ref, w_ref, tab_ref, h1_ref, qkvn_ref, qkvt_ref, e_ref, ot_ref, rl_ref, at_ref, s_scr, bias_scr
):
    h = pl.program_id(0)

    @pl.when(h == 0)
    def _():
        for block in range(lay.blocks):
            base = block * BK
            for c, start, at, size in lay.pieces[block]:
                x = x_ref[c, start : start + size].astype(F32)
                r = lax.rsqrt(jnp.mean(x * x, axis=1, keepdims=True) + EPSILON)
                h1_ref[base + at : base + at + size] = (x * r * gain_ref[...]).astype(BF16)
            y = dot(h1_ref[base : base + BK], w_ref[...]).astype(BF16)
            scale = jnp.where(lax.broadcasted_iota(jnp.int32, y.shape, 1) < heads * HD, HD**-0.5, 1.0)
            y = (y.astype(F32) * scale).astype(BF16)
            yt = y.T
            qkvt_ref[:, base : base + BK] = yt
            for i in range(3 * heads):
                qkvn_ref[i, base : base + BK] = y[:, i * HD : (i + 1) * HD]

    table_row = tab_ref[0]
    for d in range(lay.distances):
        bias_scr[d] = toeplitz_tile(table_row, d)
    hrow = pl.multiple_of(h * HD, HD)
    for q in range(lay.blocks):
        qt = qkvt_ref[pl.ds(hrow, HD), q * BK : (q + 1) * BK]
        top = None
        for n, k in enumerate(lay.keys[q]):
            s = dot(qkvn_ref[heads + h, k * BK : (k + 1) * BK], qt) + bias_scr[lay.distance(q, k)]
            s_scr[n] = s
            m = jnp.max(s, axis=0, keepdims=True)
            top = m if top is None else jnp.maximum(top, m)
        total, out = 0.0, 0.0
        vrow = pl.multiple_of(2 * heads * HD + h * HD, HD)
        for n, k in enumerate(lay.keys[q]):
            e = jnp.exp(s_scr[n] - top)
            total = total + jnp.sum(e, axis=0, keepdims=True)
            e = e.astype(BF16)
            e_ref[0, lay.tile[(q, k)]] = e
            out = out + dot(qkvt_ref[pl.ds(vrow, HD), k * BK : (k + 1) * BK], e)
        inverse = 1.0 / total
        rl_ref[0, :, q * BK : (q + 1) * BK] = inverse
        out = out * inverse
        ot_ref[pl.ds(hrow, HD), q * BK : (q + 1) * BK] = out
        for c, start, at, size in lay.pieces[q]:
            at_ref[c, pl.ds(hrow, HD), start : start + size] = out[:, at : at + size].astype(BF16)


def attention_forward(lay, heads, x_all, gain, weights, table):
    width = x_all.shape[2]
    feats = heads * HD
    return pl.pallas_call(
        functools.partial(attention_kernel, lay, heads),
        grid=(heads,),
        in_specs=[
            full(x_all.shape),
            full((1, width)),
            full(weights.shape),
            pl.BlockSpec((1, 1, table.shape[2]), lambda h: (h, 0, 0)),
        ],
        out_specs=(
            full((lay.total, width)),
            full((3 * heads, lay.total, HD)),
            full((3 * feats, lay.total)),
            pl.BlockSpec((1, lay.tiles, BK, BK), lambda h: (h, 0, 0, 0)),
            full((feats, lay.total)),
            pl.BlockSpec((1, 1, lay.total), lambda h: (h, 0, 0)),
            full((lay.spread, feats, lay.tokens)),
        ),
        out_shape=(
            jax.ShapeDtypeStruct((lay.total, width), BF16),
            jax.ShapeDtypeStruct((3 * heads, lay.total, HD), BF16),
            jax.ShapeDtypeStruct((3 * feats, lay.total), BF16),
            jax.ShapeDtypeStruct((heads, lay.tiles, BK, BK), BF16),
            jax.ShapeDtypeStruct((feats, lay.total), F32),
            jax.ShapeDtypeStruct((heads, 1, lay.total), F32),
            jax.ShapeDtypeStruct((lay.spread, feats, lay.tokens), BF16),
        ),
        scratch_shapes=[
            VMEM((max(len(k) for k in lay.keys), BK, BK), F32),
            VMEM((lay.distances, BK, BK), F32),
        ],
        compiler_params=pltpu.CompilerParams(vmem_limit_bytes=58 * MIB),
        name="attention_forward",
    )(x_all, gain, weights, table)


def middle_kernel(
    experts, capacity, at_ref, x_ref, wo_ref, gain_ref, router_ref, route_ref, rows_ref, mid_ref, h2_ref, gates_ref, sent_ref
):
    mid = x_ref[...].astype(F32) + dot_tn(at_ref[...], wo_ref[...])
    mid_ref[...] = mid
    r = lax.rsqrt(jnp.mean(mid * mid, axis=1, keepdims=True) + EPSILON)
    h2 = (mid * r * gain_ref[...]).astype(BF16)
    h2_ref[...] = h2
    tokens = h2.shape[0]
    for start in range(0, experts * capacity, 128):
        number = lax.broadcasted_iota(jnp.int32, (128, tokens), 0) + start
        pick = (rows_ref[0:1, :] == number) | (rows_ref[1:2, :] == number)
        pick = jnp.where(pick, 1.0, 0.0).astype(BF16)
        sent_ref[start : start + 128] = dot(pick, h2).astype(BF16)
    logits = dot(h2, router_ref[...])
    lane = lax.broadcasted_iota(jnp.int32, logits.shape, 1)
    chosen = [
        jnp.sum(jnp.where(route_ref[:, i : i + 1] == lane, logits, 0.0), axis=1, keepdims=True)
        for i in range(2)
    ]
    most = jnp.maximum(chosen[0], chosen[1])
    parts = [jnp.exp(c - most) for c in chosen]
    inverse = 1.0 / (parts[0] + parts[1])
    wide = lax.broadcasted_iota(jnp.int32, (tokens, 128), 1)
    gates_ref[...] = jnp.where(
        wide == 0, parts[0] * inverse, jnp.where(wide == 1, parts[1] * inverse, 0.0)
    )


def middle(attended_t, x_local, w_attn_out, gain, router, routes, rows, experts, capacity):
    tokens, width = x_local.shape
    return pl.pallas_call(
        functools.partial(middle_kernel, experts, capacity),
        out_shape=(
            jax.ShapeDtypeStruct((tokens, width), F32),
            jax.ShapeDtypeStruct((tokens, width), BF16),
            jax.ShapeDtypeStruct((tokens, 128), F32),
            jax.ShapeDtypeStruct((experts * capacity, width), BF16),
        ),
        compiler_params=pltpu.CompilerParams(vmem_limit_bytes=40 * MIB),
        name="middle",
    )(attended_t, x_local, w_attn_out, gain, router, routes, rows)


def gelu_parts(u):
    slope = 0.7978845608028654
    cube = 0.044715
    square = u * u
    t = jnp.tanh(slope * u * (1.0 + cube * square))
    half = 0.5 * (1.0 + t)
    value = u * half
    grad = half + 0.5 * u * (1.0 - t * t) * (slope * (1.0 + 3.0 * cube * square))
    return value, grad


def expert_grad_kernel(
    steps, sent_ref, dzp_ref, router_ref, w_in_ref, w_out_ref, act_ref, dpre_ref, dsent_ref, dmade_ref, share_ref, acc, shares
):
    f = pl.program_id(0)
    width = sent_ref.shape[1]

    @pl.when(f == 0)
    def _():
        logits = dot(sent_ref[...], router_ref[...])
        lane = lax.broadcasted_iota(jnp.int32, logits.shape, 1)
        own = jnp.sum(
            jnp.where(lane == lax.axis_index("expert"), logits, 0.0), axis=1, keepdims=True
        )
        other_hot = dzp_ref[:, width : width + logits.shape[1]].astype(F32)
        other = jnp.sum(other_hot * logits, axis=1, keepdims=True)
        gate = 1.0 / (1.0 + jnp.exp(other - own))
        dmade_ref[...] = (gate * dzp_ref[:, :width].astype(F32)).astype(BF16)
        acc[...] = jnp.zeros_like(acc)
        shares[...] = jnp.zeros_like(shares)

    pre = dot(sent_ref[...], w_in_ref[0])
    dact = dot_nt(dmade_ref[...], w_out_ref[0])
    value, grad = gelu_parts(pre)
    act = value.astype(BF16)
    act_ref[...] = act
    dpre = (dact * grad).astype(BF16)
    dpre_ref[...] = dpre
    product = act.astype(F32) * dact
    part = product[:, :128]
    for i in range(1, product.shape[1] // 128):
        part = part + product[:, i * 128 : (i + 1) * 128]
    shares[...] += part
    acc[...] += dot_nt(dpre, w_in_ref[0])

    @pl.when(f == steps - 1)
    def _():
        dsent_ref[...] = acc[...].astype(BF16)
        total = jnp.sum(shares[...], axis=1, keepdims=True)
        share_ref[...] = jnp.broadcast_to(total, share_ref.shape)


def expert_grad(sent, dzp, router, w_in, w_out):
    rows, width = sent.shape
    hidden = w_in.shape[2]
    chunk = 512
    steps = hidden // chunk
    return pl.pallas_call(
        functools.partial(expert_grad_kernel, steps),
        grid=(steps,),
        in_specs=[
            full((rows, width)),
            full(dzp.shape),
            full(router.shape),
            pl.BlockSpec((1, width, chunk), lambda f: (0, 0, f)),
            pl.BlockSpec((1, chunk, width), lambda f: (0, f, 0)),
        ],
        out_specs=(
            pl.BlockSpec((rows, chunk), lambda f: (0, f)),
            pl.BlockSpec((rows, chunk), lambda f: (0, f)),
            full((rows, width)),
            full((rows, width)),
            full((rows, 128)),
        ),
        out_shape=(
            jax.ShapeDtypeStruct((rows, hidden), BF16),
            jax.ShapeDtypeStruct((rows, hidden), BF16),
            jax.ShapeDtypeStruct((rows, width), BF16),
            jax.ShapeDtypeStruct((rows, width), BF16),
            jax.ShapeDtypeStruct((rows, 128), F32),
        ),
        scratch_shapes=[VMEM((rows, width), F32), VMEM((rows, 128), F32)],
        compiler_params=pltpu.CompilerParams(vmem_limit_bytes=56 * MIB),
        name="expert_grad",
    )(sent, dzp, router, w_in, w_out)


def expert_weight_kernel(
    steps, sent_ref, dmade_ref, act_ref, dpre_ref, w_out_ref, made_ref, gin_ref, gout_ref, acc
):
    f = pl.program_id(0)

    @pl.when(f == 0)
    def _():
        acc[...] = jnp.zeros_like(acc)

    acc[...] += dot(act_ref[...], w_out_ref[0])
    gout_ref[0] = dot_tn(act_ref[...], dmade_ref[...]).astype(BF16)
    gin_ref[0] = dot_tn(sent_ref[...], dpre_ref[...]).astype(BF16)

    @pl.when(f == steps - 1)
    def _():
        made_ref[...] = acc[...].astype(BF16)


def expert_weights(sent, dmade, act, dpre, w_out):
    rows, width = sent.shape
    hidden = act.shape[1]
    chunk = 512
    steps = hidden // chunk
    return pl.pallas_call(
        functools.partial(expert_weight_kernel, steps),
        grid=(steps,),
        in_specs=[
            full((rows, width)),
            full((rows, width)),
            pl.BlockSpec((rows, chunk), lambda f: (0, f)),
            pl.BlockSpec((rows, chunk), lambda f: (0, f)),
            pl.BlockSpec((1, chunk, width), lambda f: (0, f, 0)),
        ],
        out_specs=(
            full((rows, width)),
            pl.BlockSpec((1, width, chunk), lambda f: (0, 0, f)),
            pl.BlockSpec((1, chunk, width), lambda f: (0, f, 0)),
        ),
        out_shape=(
            jax.ShapeDtypeStruct((rows, width), BF16),
            jax.ShapeDtypeStruct((1, width, hidden), BF16),
            jax.ShapeDtypeStruct((1, hidden, width), BF16),
        ),
        scratch_shapes=[VMEM((rows, width), F32)],
        compiler_params=pltpu.CompilerParams(vmem_limit_bytes=56 * MIB),
        name="expert_weights",
    )(sent, dmade, act, dpre, w_out)


def turn_kernel(
    slots, dsent_ref, share_ref, cols_ref, gates_ref, route_ref, mid_ref, dz_ref, h2_ref, gain_ref, router_ref, wo_ref, at_ref, dmid_ref, dot_ref, gwo_ref, ggain_ref, grouter_ref
):
    tokens = mid_ref.shape[0]
    lane = lax.broadcasted_iota(jnp.int32, (tokens, slots), 1)
    picks = [cols_ref[:, i : i + 1] == lane for i in range(2)]
    both = jnp.where(picks[0] | picks[1], 1.0, 0.0).astype(BF16)
    dh2 = dot(both, dsent_ref[...])
    share = [
        jnp.sum(jnp.where(picks[i], share_ref[0:1, :], 0.0), axis=1, keepdims=True)
        for i in range(2)
    ]
    total = share[0] + share[1]
    dchosen = [share[i] - gates_ref[:, i : i + 1] * total for i in range(2)]
    experts = router_ref.shape[1]
    elane = lax.broadcasted_iota(jnp.int32, (tokens, experts), 1)
    dlogits = sum(
        jnp.where(route_ref[:, i : i + 1] == elane, dchosen[i], 0.0) for i in range(2)
    )
    dh2 = dh2 + split_dot(dlogits, router_ref[...], dot_nt)
    grouter_ref[...] = split_dot(dlogits, h2_ref[...], dot_tn)
    mid = mid_ref[...]
    r = lax.rsqrt(jnp.mean(mid * mid, axis=1, keepdims=True) + EPSILON)
    u = dh2 * gain_ref[...]
    mean = jnp.mean(u * mid, axis=1, keepdims=True)
    dmid = dz_ref[...].astype(F32) + r * u - (r * r * r) * mid * mean
    dmid_ref[...] = dmid
    ggain_ref[...] = jnp.sum(dh2 * mid * r, axis=0, keepdims=True)
    branch = dmid.astype(BF16)
    gwo_ref[...] = dot(at_ref[...], branch)
    dot_ref[...] = dot_nt(wo_ref[...], branch).astype(BF16)


def turn(dsent, share, cols, gates, routes, mid, dz, h2, gain, router, wo, attended_t):
    tokens, width = mid.shape
    return pl.pallas_call(
        functools.partial(turn_kernel, dsent.shape[0]),
        out_shape=(
            jax.ShapeDtypeStruct((tokens, width), F32),
            jax.ShapeDtypeStruct((width, tokens), BF16),
            jax.ShapeDtypeStruct((width, width), F32),
            jax.ShapeDtypeStruct((1, width), F32),
            jax.ShapeDtypeStruct((router.shape[1], width), F32),
        ),
        compiler_params=pltpu.CompilerParams(vmem_limit_bytes=48 * MIB),
        name="turn",
    )(dsent, share, cols, gates, routes, mid, dz, h2, gain, router, wo, attended_t)


def attention_back_kernel(
    lay, heads, dot_ref, e_ref, qkvn_ref, qkvt_ref, ot_ref, rl_ref, h1_ref, wt_ref, dh1_ref, gw_ref, gtab_ref, dst_scr, doT_scr, do_scr, dT_scr
):
    h = pl.program_id(0)
    feats = heads * HD
    hrow = pl.multiple_of(h * HD, HD)
    deltas = []
    for q in range(lay.blocks):
        cols = slice(q * BK, (q + 1) * BK)
        for c, start, at, size in lay.pieces[q]:
            piece = dot_ref[c, pl.ds(hrow, HD), start : start + size]
            where = q * BK + at
            doT_scr[:, where : where + size] = piece
        raw = doT_scr[:, cols].astype(F32)
        inverse = rl_ref[0, :, cols]
        deltas.append(
            inverse * jnp.sum(raw * ot_ref[pl.ds(hrow, HD), cols], axis=0, keepdims=True)
        )
        scaled = raw * inverse
        doT_scr[:, cols] = scaled.astype(BF16)
        do_scr[cols] = scaled.T.astype(BF16)
    krow = pl.multiple_of(feats + h * HD, HD)
    vrow = pl.multiple_of(2 * feats + h * HD, HD)
    for q in range(lay.blocks):
        cols = slice(q * BK, (q + 1) * BK)
        dq = 0.0
        for k in lay.keys[q]:
            t = lay.tile[(q, k)]
            rows = slice(k * BK, (k + 1) * BK)
            dp = dot(qkvn_ref[2 * heads + h, rows], doT_scr[:, cols])
            ds = (e_ref[0, t].astype(F32) * (dp - deltas[q])).astype(BF16)
            dst_scr[t] = ds
            dq = dq + dot(qkvt_ref[pl.ds(krow, HD), rows], ds)
        dT_scr[pl.ds(hrow, HD), cols] = (dq * HD**-0.5).astype(BF16)
    for k in range(lay.blocks):
        rows = slice(k * BK, (k + 1) * BK)
        dk, dv = 0.0, 0.0
        for q in range(lay.blocks):
            if k in lay.keys[q]:
                t = lay.tile[(q, k)]
                cols = slice(q * BK, (q + 1) * BK)
                dk = dk + dot(dst_scr[t], qkvn_ref[h, cols])
                dv = dv + dot(e_ref[0, t], do_scr[cols])
        dT_scr[pl.ds(krow, HD), rows] = dk.T.astype(BF16)
        dT_scr[pl.ds(vrow, HD), rows] = dv.T.astype(BF16)
    gtab_ref[...] = jnp.zeros_like(gtab_ref)
    for d in range(lay.distances):
        tile = 0.0
        for (q, k), t in lay.tile.items():
            if lay.distance(q, k) == d:
                tile = tile + dst_scr[t].astype(F32)
        sums = diagonal_sums(tile)
        gtab_ref[0, :, (d + 1) * BK : (d + 2) * BK] += sums[:, :BK]
        gtab_ref[0, :, d * BK : (d + 1) * BK] += sums[:, BK:]

    @pl.when(h == heads - 1)
    def _():
        for q in range(lay.blocks):
            cols = slice(q * BK, (q + 1) * BK)
            part = dot_tn(dT_scr[:, cols], wt_ref[...]).astype(BF16)
            for c, start, at, size in lay.pieces[q]:
                dh1_ref[c, start : start + size] = part[at : at + size]
        gw_ref[...] = dot(dT_scr[...], h1_ref[...])


def attention_backward(lay, heads, dattn_t, e, qkvn, qkvt, ot, rl, h1, weights_t):
    width = h1.shape[1]
    feats = heads * HD
    span = (lay.distances + 1) * BK
    return pl.pallas_call(
        functools.partial(attention_back_kernel, lay, heads),
        grid=(heads,),
        in_specs=[
            full(dattn_t.shape),
            pl.BlockSpec((1, lay.tiles, BK, BK), lambda h: (h, 0, 0, 0)),
            full(qkvn.shape),
            full(qkvt.shape),
            full(ot.shape),
            pl.BlockSpec((1, 1, lay.total), lambda h: (h, 0, 0)),
            full(h1.shape),
            full(weights_t.shape),
        ],
        out_specs=(
            full((lay.spread, lay.tokens, width)),
            full((3 * feats, width)),
            pl.BlockSpec((1, 1, span), lambda h: (h, 0, 0)),
        ),
        out_shape=(
            jax.ShapeDtypeStruct((lay.spread, lay.tokens, width), BF16),
            jax.ShapeDtypeStruct((3 * feats, width), F32),
            jax.ShapeDtypeStruct((heads, 1, span), F32),
        ),
        scratch_shapes=[
            VMEM((lay.tiles, BK, BK), BF16),
            VMEM((HD, lay.total), BF16),
            VMEM((lay.total, HD), BF16),
            VMEM((3 * feats, lay.total), BF16),
        ],
        compiler_params=pltpu.CompilerParams(vmem_limit_bytes=58 * MIB),
        name="attention_backward",
    )(dattn_t, e, qkvn, qkvt, ot, rl, h1, weights_t)


def finish_kernel(dh1_ref, x_ref, gain_ref, dmid_ref, dx_ref, ggain_ref):
    x = x_ref[...].astype(F32)
    dh1 = dh1_ref[...].astype(F32)
    r = lax.rsqrt(jnp.mean(x * x, axis=1, keepdims=True) + EPSILON)
    w = dh1 * gain_ref[...]
    mean = jnp.mean(w * x, axis=1, keepdims=True)
    dx_ref[...] = dmid_ref[...] + r * w - (r * r * r) * x * mean
    ggain_ref[...] = jnp.sum(dh1 * x * r, axis=0, keepdims=True)


def finish(dh1, x_local, gain, dmid):
    return pl.pallas_call(
        finish_kernel,
        out_shape=(
            jax.ShapeDtypeStruct(dmid.shape, F32),
            jax.ShapeDtypeStruct((1, dmid.shape[1]), F32),
        ),
        compiler_params=pltpu.CompilerParams(vmem_limit_bytes=32 * MIB),
        name="finish",
    )(dh1, x_local, gain, dmid)


def result_kernel(mid_ref, cols_ref, gates_ref, made_ref, out_ref):
    tokens = mid_ref.shape[0]
    slots = made_ref.shape[0]
    lane = lax.broadcasted_iota(jnp.int32, (tokens, slots), 1)
    out = mid_ref[...]
    for i in range(2):
        pick = jnp.where(cols_ref[:, i : i + 1] == lane, 1.0, 0.0).astype(BF16)
        out = out + gates_ref[:, i : i + 1] * dot(pick, made_ref[...])
    out_ref[...] = out.astype(BF16)


def result(mid, cols, gates, made):
    return pl.pallas_call(
        result_kernel,
        out_shape=jax.ShapeDtypeStruct(mid.shape, BF16),
        compiler_params=pltpu.CompilerParams(vmem_limit_bytes=32 * MIB),
        name="result",
    )(mid, cols, gates, made)


def body(
    prompt_in,
    cont_in,
    prompt_route,
    cont_route,
    order,
    buckets,
    attn_gain,
    w_query,
    w_key,
    w_value,
    w_attn_out,
    rel_bias,
    ffn_gain,
    router,
    w_in,
    w_out,
    prompt_cot,
    cont_cot,
):
    prompt_rows = prompt_in.shape[1]
    cont_count = cont_in.shape[1]
    cont_rows = cont_in.shape[2]
    width = prompt_in.shape[2]
    spread = lax.axis_size("context")
    expert_devices = lax.axis_size("expert")
    lay = Layout(spread, prompt_rows, cont_count, cont_rows)
    tokens = lay.tokens
    head_count = rel_bias.shape[1]
    heads = head_count // spread
    feats = heads * HD
    experts = w_in.shape[0] * expert_devices
    capacity = 9 * tokens * 2 // (8 * experts)
    slots = experts * capacity
    buckets_count = rel_bias.shape[0]
    context = lax.axis_index("context")

    def local_rows(prompt_part, cont_part):
        return jnp.concatenate(
            [prompt_part.reshape(prompt_rows, -1), cont_part.reshape(cont_count * cont_rows, -1)],
            axis=0,
        )

    def own_columns(matrix):
        return lax.dynamic_slice_in_dim(matrix, context * feats, feats, 1)

    def exchange(array, axis):
        return lax.all_to_all(array, axis, split_axis=0, concat_axis=0, tiled=True)

    x_local = local_rows(prompt_in, cont_in)
    x_all = lax.all_gather(x_local, "context", axis=0, tiled=False)
    routes = local_rows(prompt_route, cont_route)
    upstream = local_rows(prompt_cot, cont_cot)
    gain_one = attn_gain.reshape(1, width)
    gain_two = ffn_gain.reshape(1, width)
    slot_rows, slot_cols, dz_slots = plan(routes, order.reshape(tokens), upstream, experts, capacity)
    dz_slots = exchange(dz_slots.reshape(expert_devices, slots // expert_devices, -1), "expert")
    dz_slots = dz_slots.reshape(slots, -1)

    bucket_hot = (buckets[:, None] == jnp.arange(buckets_count, dtype=jnp.int32)[None, :]).astype(F32)
    own_bias = lax.dynamic_slice_in_dim(rel_bias, context * heads, heads, 1)
    table = jnp.dot(bucket_hot, own_bias, precision=PRECISE).T
    table = jnp.pad(table, ((0, 0), (BK, 0))).reshape(heads, 1, -1)
    weights = jnp.concatenate([own_columns(w) for w in (w_query, w_key, w_value)], axis=1)
    weights_t = weights.T
    h1, qkvn, qkvt, e, ot, rl, at = attention_forward(lay, heads, x_all, gain_one, weights, table)
    attended_t = exchange(at, "context").reshape(width, tokens)
    mid, h2, gates, sent = middle(
        attended_t, x_local, w_attn_out, gain_two, router, routes, slot_rows, experts, capacity
    )
    arrived = exchange(sent.reshape(expert_devices, slots // expert_devices, width), "expert")
    arrived = arrived.reshape(slots, width)
    act, dpre, dsent, dmade, share = expert_grad(arrived, dz_slots, router, w_in, w_out)
    dsent = exchange(dsent.reshape(expert_devices, slots // expert_devices, width), "expert")
    share = exchange(share[:, 0].reshape(expert_devices, slots // expert_devices), "expert")
    made, g_in, g_out = expert_weights(arrived, dmade, act, dpre, w_out)
    dmid, dattn_t, g_wo, g_gain_two, g_router = turn(
        dsent.reshape(slots, width),
        share.reshape(1, slots),
        slot_cols,
        gates,
        routes,
        mid,
        upstream,
        h2,
        gain_two,
        router,
        w_attn_out,
        attended_t,
    )
    dattn_t = exchange(dattn_t.reshape(spread, feats, tokens), "context")
    made = exchange(made.reshape(expert_devices, slots // expert_devices, width), "expert")
    g_in_sum, g_out_sum = (
        lax.psum_scatter(g, ("dp", "context"), scatter_dimension=1, tiled=True).astype(F32)
        for g in (g_in, g_out)
    )
    dh1, g_qkv, g_table = attention_backward(
        lay, heads, dattn_t, e, qkvn, qkvt, ot, rl, h1, weights_t
    )
    dh1 = lax.psum_scatter(dh1, "context", scatter_dimension=0, tiled=False)
    dx, g_gain_one = finish(dh1, x_local, gain_one, dmid)
    out = result(mid, slot_cols, gates, made.reshape(slots, width))

    g_bias = jnp.dot(g_table[:, 0, BK:], bucket_hot, precision=PRECISE)
    g_bias = lax.dynamic_update_slice_in_dim(
        jnp.zeros((head_count, width), F32), jnp.pad(g_bias, ((0, 0), (0, width - buckets_count))), context * heads, 0
    )
    small = jnp.concatenate([g_gain_one, g_gain_two, g_router, g_bias], axis=0)
    g_wo, small = lax.psum((g_wo, small), ("dp", "context", "expert"))
    g_qkv = lax.psum(g_qkv, ("dp", "expert"))
    g_qkv = lax.all_gather(g_qkv, "context", axis=0, tiled=False)
    g_qkv = g_qkv.reshape(spread, 3, feats, width)
    g_query, g_key, g_value = (g_qkv[:, i].reshape(width, width).T for i in range(3))
    g_bias = small[2 + experts :, :buckets_count].T
    g_router = small[2 : 2 + experts].T
    return (
        out[:prompt_rows].reshape(1, prompt_rows, width),
        out[prompt_rows:].reshape(1, cont_count, cont_rows, width),
        dx[:prompt_rows].reshape(1, prompt_rows, width),
        dx[prompt_rows:].reshape(1, cont_count, cont_rows, width),
        small[0],
        g_query,
        g_key,
        g_value,
        g_wo,
        g_bias,
        small[1],
        g_router,
        g_in_sum,
        g_out_sum,
    )


def solution(mesh):
    split = P(("dp", "expert"), "context", None)
    split_cont = P(("dp", "expert"), None, "context", None)
    whole = P()
    expert = P("expert", None, None)
    grad = P("expert", ("dp", "context"), None)
    return jax.shard_map(
        body,
        mesh=mesh,
        in_specs=(split, split_cont, split, split_cont, split)
        + (whole,) * 9
        + (expert, expert, split, split_cont),
        out_specs=(split, split_cont, split, split_cont) + (whole,) * 8 + (grad, grad),
        check_vma=False,
    )
```

```python
import functools

import jax
import jax.numpy as jnp
from jax import lax
from jax.experimental import pallas as pl
from jax.experimental.pallas import tpu as pltpu
from jax.sharding import PartitionSpec as P

HD = 64
BK = 256
EPSILON = 1e-06
MASKED = -1e30
F32 = jnp.float32
BF16 = jnp.bfloat16
PRECISE = lax.Precision.HIGHEST
VMEM = pltpu.VMEM
MESH = pl.DeviceIdType.MESH
MIB = 1 << 20


def dot(a, b):
    return lax.dot_general(a, b, (((1,), (0,)), ((), ())), preferred_element_type=F32)


def dot_nt(a, b):
    return lax.dot_general(a, b, (((1,), (1,)), ((), ())), preferred_element_type=F32)


def dot_tn(a, b):
    return lax.dot_general(a, b, (((0,), (0,)), ((), ())), preferred_element_type=F32)


def split_dot(a, b, op):
    high = a.astype(BF16)
    low = (a - high.astype(F32)).astype(BF16)
    return op(high, b) + op(low, b)


def full(shape):
    return pl.BlockSpec(shape, lambda *_: (0,) * len(shape))


class Layout:
    def __init__(self, spread, prompt_rows, cont_count, cont_rows):
        assert prompt_rows == BK and BK % cont_rows == 0
        self.spread = spread
        self.prompt_rows = prompt_rows
        self.cont_count = cont_count
        self.cont_rows = cont_rows
        self.tokens = prompt_rows + cont_count * cont_rows
        self.per_cont = spread * cont_rows // BK
        self.blocks = spread + cont_count * self.per_cont
        self.total = self.blocks * BK
        self.keys, self.place, self.pieces = [], [], []
        for p in range(spread):
            self.keys.append(list(range(p + 1)))
            self.place.append(p)
            self.pieces.append([(p, 0, 0, BK)])
        each = BK // cont_rows
        for j in range(cont_count):
            for m in range(self.per_cont):
                first = spread + j * self.per_cont
                self.keys.append(list(range(spread)) + list(range(first, first + m + 1)))
                self.place.append(spread + m)
                self.pieces.append(
                    [
                        (m * each + n, prompt_rows + j * cont_rows, n * cont_rows, cont_rows)
                        for n in range(each)
                    ]
                )
        self.tile = {}
        for q in range(self.blocks):
            for k in self.keys[q]:
                self.tile[(q, k)] = len(self.tile)
        self.tiles = len(self.tile)
        self.distances = spread + self.per_cont

    def distance(self, q, k):
        return self.place[q] - self.place[k]


def flip(index, mask):
    bit = 1
    while bit <= mask:
        if mask & bit:
            index = index + bit * (1 - 2 * ((index // bit) % 2))
        bit *= 2
    return index


def remote(src, dst, send, recv, **where):
    return pltpu.make_async_remote_copy(
        src_ref=src,
        dst_ref=dst,
        send_sem=send,
        recv_sem=recv,
        device_id=where,
        device_id_type=MESH,
    )


def greet(partners):
    barrier = pltpu.get_barrier_semaphore()
    for where in partners:
        pl.semaphore_signal(barrier, inc=1, device_id=where, device_id_type=MESH)
    pl.semaphore_wait(barrier, len(partners))


def make_plan(capacity, routes, order_row):
    tokens = routes.shape[0]
    side = (tokens, tokens)
    lane = lax.broadcasted_iota(jnp.int32, side, 1).astype(F32)
    sub = lax.broadcasted_iota(jnp.int32, side, 0)
    rank_col = jnp.sum(jnp.where(order_row == sub, lane, 0.0), axis=1, keepdims=True)
    rank_row = jnp.broadcast_to(rank_col, (tokens, 128)).T[0:1]
    before = jnp.where(rank_row < rank_col, 1.0, 0.0).astype(BF16)
    expert_lane = lax.broadcasted_iota(jnp.int32, (tokens, 128), 1).astype(F32)
    hots = [jnp.where(routes[:, i : i + 1] == expert_lane, 1.0, 0.0) for i in range(2)]
    counts = [dot(before, hot.astype(BF16)) for hot in hots]
    counts[1] = counts[1] + jnp.sum(hots[0], axis=0, keepdims=True)
    cols = jnp.zeros((tokens, 128), F32)
    for i in range(2):
        pos = jnp.sum(hots[i] * counts[i], axis=1, keepdims=True)
        route = routes[:, i : i + 1]
        slot = jnp.where(pos < capacity, route * capacity + pos, -1.0)
        cols = jnp.where(expert_lane == i, slot, cols)
        cols = jnp.where(expert_lane == 2 + i, route, cols)
    return cols, cols.T[0:8], hots


def toeplitz_tile(table_row, d):
    line = jnp.concatenate(
        [table_row[:, (d + 1) * BK : (d + 2) * BK], table_row[:, d * BK : (d + 1) * BK]], axis=1
    )
    tile = jnp.broadcast_to(line, (8, 2 * BK))
    row = lax.broadcasted_iota(jnp.int32, (8, 2 * BK), 0)
    for bit in (1, 2, 4):
        tile = jnp.where((row & bit) > 0, pltpu.roll(tile, bit, 1), tile)
    height = 8
    while height < BK:
        tile = jnp.concatenate([tile, pltpu.roll(tile, height, 1)], axis=0)
        height *= 2
    tile = tile[:, :BK]
    if d == 0:
        key = lax.broadcasted_iota(jnp.int32, (BK, BK), 0)
        query = lax.broadcasted_iota(jnp.int32, (BK, BK), 1)
        tile = jnp.where(query >= key, tile, MASKED)
    return tile


def diagonal_sums(tile):
    tile = jnp.concatenate([tile, jnp.zeros((BK, BK), F32)], axis=1)
    height = BK
    while height > 8:
        height //= 2
        tile = tile[:height] + pltpu.roll(tile[height:], 2 * BK - height, 1)
    row = lax.broadcasted_iota(jnp.int32, (8, 2 * BK), 0)
    for bit in (1, 2, 4):
        tile = jnp.where((row & bit) > 0, pltpu.roll(tile, 2 * BK - bit, 1), tile)
    return jnp.sum(tile, axis=0, keepdims=True)


def front_kernel(
    lay,
    heads,
    peers,
    capacity,
    xp_ref,
    xc_ref,
    rp_ref,
    rc_ref,
    order_ref,
    buckets_ref,
    gain_ref,
    wq_ref,
    wk_ref,
    wv_ref,
    bias_ref,
    zp_ref,
    zc_ref,
    h1_ref,
    qkvn_ref,
    qkvt_ref,
    e_ref,
    ot_ref,
    rl_ref,
    w_ref,
    cols_ref,
    rows_ref,
    at_ref,
    dz_ref,
    x_all,
    at_scr,
    dz_scr,
    s_scr,
    bias_scr,
    x_send,
    x_recv,
    a_send,
    a_recv,
    z_send,
    z_recv,
    own_sem,
):
    h = pl.program_id(0)
    me = lax.axis_index("context")
    expert = lax.axis_index("expert")
    feats = heads * HD
    half = lay.prompt_rows
    near, across, far = flip(me, 1), flip(me, 2), flip(me, 3)
    width = gain_ref.shape[1]

    def x_copy(slot, part, index, target):
        view = x_all.at[slot, pl.ds(part * half, half)]
        return remote(view, view, x_send.at[index], x_recv.at[index], context=target)

    def z_copy(k):
        return remote(
            dz_scr.at[k], dz_ref.at[k], z_send.at[k], z_recv.at[k], expert=flip(expert, k)
        )

    def a_copy(k, head):
        target = flip(me, k)
        src = at_scr.at[target, pl.ds(head * HD, HD)]
        dst = at_ref.at[me, pl.ds(head * HD, HD)]
        return remote(src, dst, a_send.at[head, k], a_recv.at[head, k], context=target)

    def a_own(head):
        return pltpu.make_async_copy(
            at_scr.at[me, pl.ds(head * HD, HD)],
            at_ref.at[me, pl.ds(head * HD, HD)],
            a_send.at[head, 0],
        )

    z_own = pltpu.make_async_copy(dz_scr.at[0], dz_ref.at[0], own_sem)

    def project(slot):
        x = x_all[slot].astype(F32)
        r = lax.rsqrt(jnp.mean(x * x, axis=1, keepdims=True) + EPSILON)
        normed = (x * r * gain_ref[...]).astype(BF16)
        y = dot(normed, w_ref[...])
        scale = jnp.where(lax.broadcasted_iota(jnp.int32, y.shape, 1) < feats, HD**-0.5, 1.0)
        y = (y.astype(BF16).astype(F32) * scale).astype(BF16)
        yt = y.T
        spots = [(0, pl.multiple_of(slot * half, 128), half)]
        for j in range(lay.cont_count):
            first = lay.spread * half + j * lay.spread * lay.cont_rows
            spots.append(
                (
                    half + j * lay.cont_rows,
                    pl.multiple_of(first + slot * lay.cont_rows, 128),
                    lay.cont_rows,
                )
            )
        for start, to, size in spots:
            h1_ref[pl.ds(to, size)] = normed[start : start + size]
            qkvt_ref[:, pl.ds(to, size)] = yt[:, start : start + size]
            for i in range(3 * heads):
                qkvn_ref[i, pl.ds(to, size)] = y[start : start + size, i * HD : (i + 1) * HD]

    @pl.when(h == 0)
    def _():
        greet(
            [{"context": t} for t in (near, across, far)]
            + [{"expert": flip(expert, k)} for k in range(1, peers)]
        )
        x_all[me, :half] = xp_ref[...]
        x_all[me, half:] = xc_ref[...]
        for part in range(2):
            x_copy(me, part, part, across).start()
        for part in range(2):
            x_copy(me, part, 2 + part, near).start()
        tokens = lay.tokens
        lane = lax.broadcasted_iota(jnp.int32, (tokens, 128), 1)
        routes = jnp.concatenate([rp_ref[...], rc_ref[...]], axis=0).astype(F32)
        routes = jnp.where(lane == 0, routes[:, 0:1], routes[:, 1:2])
        cols, rows, hots = make_plan(capacity, routes, order_ref[...])
        cols_ref[...] = cols
        rows_ref[...] = rows
        dz = jnp.concatenate([zp_ref[...], zc_ref[...]], axis=0)
        for k in list(range(1, peers)) + [0]:
            base = flip(expert, k) * capacity
            number = (lax.broadcasted_iota(jnp.int32, (capacity, tokens), 0) + base).astype(F32)
            first = jnp.where(rows[0:1] == number, 1.0, 0.0)
            second = jnp.where(rows[1:2] == number, 1.0, 0.0)
            dz_scr[k, :, :width] = dot((first + second).astype(BF16), dz).astype(BF16)
            other = dot(first.astype(BF16), hots[1].astype(BF16))
            other = other + dot(second.astype(BF16), hots[0].astype(BF16))
            dz_scr[k, :, width:] = other.astype(BF16)
            if k:
                z_copy(k).start()
            else:
                z_own.start()
        for c in range(lay.spread):

            @pl.when(me == c)
            def _():
                for i, ref in enumerate((wq_ref, wk_ref, wv_ref)):
                    w_ref[:, i * feats : (i + 1) * feats] = ref[:, c * feats : (c + 1) * feats]

        project(me)
        for part in range(2):
            x_copy(near, part, 2 + part, near).wait_recv()
        project(near)
        for part in range(2):
            x_copy(across, part, part, across).wait_recv()
            x_copy(across, part, 4 + part, near).start()
        project(across)
        for part in range(2):
            x_copy(far, part, 4 + part, near).wait_recv()
        project(far)
        for part in range(2):
            x_copy(me, part, part, across).wait_send()
            x_copy(me, part, 2 + part, near).wait_send()
            x_copy(across, part, 4 + part, near).wait_send()

    column = lax.broadcasted_iota(jnp.int32, bias_ref.shape, 1) == me * heads + h
    column = jnp.sum(jnp.where(column, bias_ref[...], 0.0), axis=1, keepdims=True)
    span = buckets_ref.shape[1]
    number = lax.broadcasted_iota(jnp.int32, (bias_ref.shape[0], span), 0)
    table_row = jnp.sum(
        jnp.where(buckets_ref[...] == number, column, 0.0), axis=0, keepdims=True
    )
    table_row = jnp.concatenate([jnp.zeros((1, BK), F32), table_row], axis=1)
    for d in range(lay.distances):
        bias_scr[d] = toeplitz_tile(table_row, d)
    hrow = pl.multiple_of(h * HD, HD)
    vrow = pl.multiple_of(2 * feats + h * HD, HD)
    for q in range(lay.blocks):
        qt = qkvt_ref[pl.ds(hrow, HD), q * BK : (q + 1) * BK]
        top = None
        for n, k in enumerate(lay.keys[q]):
            s = dot(qkvn_ref[heads + h, k * BK : (k + 1) * BK], qt) + bias_scr[lay.distance(q, k)]
            s_scr[n] = s
            m = jnp.max(s, axis=0, keepdims=True)
            top = m if top is None else jnp.maximum(top, m)
        total, out = 0.0, 0.0
        for n, k in enumerate(lay.keys[q]):
            e = jnp.exp(s_scr[n] - top)
            total = total + jnp.sum(e, axis=0, keepdims=True)
            e = e.astype(BF16)
            e_ref[0, lay.tile[(q, k)]] = e
            out = out + dot(qkvt_ref[pl.ds(vrow, HD), k * BK : (k + 1) * BK], e)
        inverse = 1.0 / total
        rl_ref[0, :, q * BK : (q + 1) * BK] = inverse
        out = out * inverse
        ot_ref[pl.ds(hrow, HD), q * BK : (q + 1) * BK] = out
        for c, start, at, size in lay.pieces[q]:
            at_scr[c, pl.ds(hrow, HD), start : start + size] = out[:, at : at + size].astype(BF16)

    for k in (3, 2, 1):
        a_copy(k, h).start()
    a_own(h).start()

    @pl.when(h == heads - 1)
    def _():
        for head in range(heads):
            a_own(head).wait()
            for k in (1, 2, 3):
                a_copy(k, head).wait()
        z_own.wait()
        for k in range(1, peers):
            z_copy(k).wait()


def front(lay, heads, peers, capacity, *args):
    width = args[0].shape[1]
    feats = heads * HD
    dma = pltpu.SemaphoreType.DMA
    anywhere = pl.BlockSpec(memory_space=pl.ANY)
    return pl.pallas_call(
        functools.partial(front_kernel, lay, heads, peers, capacity),
        grid=(heads,),
        in_specs=[full(a.shape) for a in args],
        out_specs=(
            full((lay.total, width)),
            full((3 * heads, lay.total, HD)),
            full((3 * feats, lay.total)),
            pl.BlockSpec((1, lay.tiles, BK, BK), lambda h: (h, 0, 0, 0)),
            full((feats, lay.total)),
            pl.BlockSpec((1, 1, lay.total), lambda h: (h, 0, 0)),
            full((width, 3 * feats)),
            full((lay.tokens, 128)),
            full((8, lay.tokens)),
            anywhere,
            anywhere,
        ),
        out_shape=(
            jax.ShapeDtypeStruct((lay.total, width), BF16),
            jax.ShapeDtypeStruct((3 * heads, lay.total, HD), BF16),
            jax.ShapeDtypeStruct((3 * feats, lay.total), BF16),
            jax.ShapeDtypeStruct((heads, lay.tiles, BK, BK), BF16),
            jax.ShapeDtypeStruct((feats, lay.total), F32),
            jax.ShapeDtypeStruct((heads, 1, lay.total), F32),
            jax.ShapeDtypeStruct((width, 3 * feats), BF16),
            jax.ShapeDtypeStruct((lay.tokens, 128), F32),
            jax.ShapeDtypeStruct((8, lay.tokens), F32),
            jax.ShapeDtypeStruct((lay.spread, feats, lay.tokens), BF16),
            jax.ShapeDtypeStruct((peers, capacity, width + 128), BF16),
        ),
        scratch_shapes=[
            VMEM((lay.spread, lay.tokens, width), BF16),
            VMEM((lay.spread, feats, lay.tokens), BF16),
            VMEM((peers, capacity, width + 128), BF16),
            VMEM((max(len(k) for k in lay.keys), BK, BK), F32),
            VMEM((lay.distances, BK, BK), F32),
            dma((6,)),
            dma((6,)),
            dma((heads, 4)),
            dma((heads, 4)),
            dma((peers,)),
            dma((peers,)),
            dma,
        ],
        compiler_params=pltpu.CompilerParams(
            vmem_limit_bytes=60 * MIB, collective_id=0, has_side_effects=True
        ),
        name="front",
    )(*args)


def middle_kernel(
    experts, capacity, at_ref, x_ref, wo_ref, gain_ref, router_ref, route_ref, rows_ref, mid_ref, h2_ref, gates_ref, sent_ref
):
    mid = x_ref[...].astype(F32) + dot_tn(at_ref[...], wo_ref[...])
    mid_ref[...] = mid
    r = lax.rsqrt(jnp.mean(mid * mid, axis=1, keepdims=True) + EPSILON)
    h2 = (mid * r * gain_ref[...]).astype(BF16)
    h2_ref[...] = h2
    tokens = h2.shape[0]
    for start in range(0, experts * capacity, 128):
        number = lax.broadcasted_iota(jnp.int32, (128, tokens), 0) + start
        pick = (rows_ref[0:1, :] == number) | (rows_ref[1:2, :] == number)
        pick = jnp.where(pick, 1.0, 0.0).astype(BF16)
        sent_ref[start : start + 128] = dot(pick, h2).astype(BF16)
    logits = dot(h2, router_ref[...])
    lane = lax.broadcasted_iota(jnp.int32, logits.shape, 1)
    chosen = [
        jnp.sum(jnp.where(route_ref[:, i : i + 1] == lane, logits, 0.0), axis=1, keepdims=True)
        for i in range(2)
    ]
    most = jnp.maximum(chosen[0], chosen[1])
    parts = [jnp.exp(c - most) for c in chosen]
    inverse = 1.0 / (parts[0] + parts[1])
    wide = lax.broadcasted_iota(jnp.int32, (tokens, 128), 1)
    gates_ref[...] = jnp.where(
        wide == 0, parts[0] * inverse, jnp.where(wide == 1, parts[1] * inverse, 0.0)
    )


def middle(attended_t, x_local, w_attn_out, gain, router, routes, rows, experts, capacity):
    tokens, width = x_local.shape
    return pl.pallas_call(
        functools.partial(middle_kernel, experts, capacity),
        out_shape=(
            jax.ShapeDtypeStruct((tokens, width), F32),
            jax.ShapeDtypeStruct((tokens, width), BF16),
            jax.ShapeDtypeStruct((tokens, 128), F32),
            jax.ShapeDtypeStruct((experts * capacity, width), BF16),
        ),
        compiler_params=pltpu.CompilerParams(vmem_limit_bytes=40 * MIB),
        name="middle",
    )(attended_t, x_local, w_attn_out, gain, router, routes, rows)


def gelu_parts(u):
    slope = 0.7978845608028654
    cube = 0.044715
    square = u * u
    t = jnp.tanh(slope * u * (1.0 + cube * square))
    half = 0.5 * (1.0 + t)
    value = u * half
    grad = half + 0.5 * u * (1.0 - t * t) * (slope * (1.0 + 3.0 * cube * square))
    return value, grad


def expert_grad_kernel(
    steps, sent_ref, dzp_ref, router_ref, w_in_ref, w_out_ref, act_ref, dpre_ref, dsent_ref, dmade_ref, share_ref, acc, shares
):
    f = pl.program_id(0)
    width = sent_ref.shape[1]

    @pl.when(f == 0)
    def _():
        logits = dot(sent_ref[...], router_ref[...])
        lane = lax.broadcasted_iota(jnp.int32, logits.shape, 1)
        own = jnp.sum(
            jnp.where(lane == lax.axis_index("expert"), logits, 0.0), axis=1, keepdims=True
        )
        other_hot = dzp_ref[:, width : width + logits.shape[1]].astype(F32)
        other = jnp.sum(other_hot * logits, axis=1, keepdims=True)
        gate = 1.0 / (1.0 + jnp.exp(other - own))
        dmade_ref[...] = (gate * dzp_ref[:, :width].astype(F32)).astype(BF16)
        acc[...] = jnp.zeros_like(acc)
        shares[...] = jnp.zeros_like(shares)

    pre = dot(sent_ref[...], w_in_ref[0])
    dact = dot_nt(dmade_ref[...], w_out_ref[0])
    value, grad = gelu_parts(pre)
    act = value.astype(BF16)
    act_ref[...] = act
    dpre = (dact * grad).astype(BF16)
    dpre_ref[...] = dpre
    product = act.astype(F32) * dact
    part = product[:, :128]
    for i in range(1, product.shape[1] // 128):
        part = part + product[:, i * 128 : (i + 1) * 128]
    shares[...] += part
    acc[...] += dot_nt(dpre, w_in_ref[0])

    @pl.when(f == steps - 1)
    def _():
        dsent_ref[...] = acc[...].astype(BF16)
        total = jnp.sum(shares[...], axis=1, keepdims=True)
        share_ref[...] = jnp.broadcast_to(total, share_ref.shape)


def expert_grad(sent, dzp, router, w_in, w_out):
    rows, width = sent.shape
    hidden = w_in.shape[2]
    chunk = 512
    steps = hidden // chunk
    return pl.pallas_call(
        functools.partial(expert_grad_kernel, steps),
        grid=(steps,),
        in_specs=[
            full((rows, width)),
            full(dzp.shape),
            full(router.shape),
            pl.BlockSpec((1, width, chunk), lambda f: (0, 0, f)),
            pl.BlockSpec((1, chunk, width), lambda f: (0, f, 0)),
        ],
        out_specs=(
            pl.BlockSpec((rows, chunk), lambda f: (0, f)),
            pl.BlockSpec((rows, chunk), lambda f: (0, f)),
            full((rows, width)),
            full((rows, width)),
            full((rows, 128)),
        ),
        out_shape=(
            jax.ShapeDtypeStruct((rows, hidden), BF16),
            jax.ShapeDtypeStruct((rows, hidden), BF16),
            jax.ShapeDtypeStruct((rows, width), BF16),
            jax.ShapeDtypeStruct((rows, width), BF16),
            jax.ShapeDtypeStruct((rows, 128), F32),
        ),
        scratch_shapes=[VMEM((rows, width), F32), VMEM((rows, 128), F32)],
        compiler_params=pltpu.CompilerParams(vmem_limit_bytes=56 * MIB),
        name="expert_grad",
    )(sent, dzp, router, w_in, w_out)


def expert_weight_kernel(
    steps, sent_ref, dmade_ref, act_ref, dpre_ref, w_out_ref, made_ref, gin_ref, gout_ref, acc
):
    f = pl.program_id(0)

    @pl.when(f == 0)
    def _():
        acc[...] = jnp.zeros_like(acc)

    acc[...] += dot(act_ref[...], w_out_ref[0])
    gout_ref[0] = dot_tn(act_ref[...], dmade_ref[...]).astype(BF16)
    gin_ref[0] = dot_tn(sent_ref[...], dpre_ref[...]).astype(BF16)

    @pl.when(f == steps - 1)
    def _():
        made_ref[...] = acc[...].astype(BF16)


def expert_weights(sent, dmade, act, dpre, w_out):
    rows, width = sent.shape
    hidden = act.shape[1]
    chunk = 512
    steps = hidden // chunk
    return pl.pallas_call(
        functools.partial(expert_weight_kernel, steps),
        grid=(steps,),
        in_specs=[
            full((rows, width)),
            full((rows, width)),
            pl.BlockSpec((rows, chunk), lambda f: (0, f)),
            pl.BlockSpec((rows, chunk), lambda f: (0, f)),
            pl.BlockSpec((1, chunk, width), lambda f: (0, f, 0)),
        ],
        out_specs=(
            full((rows, width)),
            pl.BlockSpec((1, width, chunk), lambda f: (0, 0, f)),
            pl.BlockSpec((1, chunk, width), lambda f: (0, f, 0)),
        ),
        out_shape=(
            jax.ShapeDtypeStruct((rows, width), BF16),
            jax.ShapeDtypeStruct((1, width, hidden), BF16),
            jax.ShapeDtypeStruct((1, hidden, width), BF16),
        ),
        scratch_shapes=[VMEM((rows, width), F32)],
        compiler_params=pltpu.CompilerParams(vmem_limit_bytes=56 * MIB),
        name="expert_weights",
    )(sent, dmade, act, dpre, w_out)


def turn_kernel(
    slots, dsent_ref, share_ref, cols_ref, gates_ref, route_ref, mid_ref, dz_ref, h2_ref, gain_ref, router_ref, wo_ref, at_ref, dmid_ref, dot_ref, gwo_ref, ggain_ref, grouter_ref
):
    tokens = mid_ref.shape[0]
    lane = lax.broadcasted_iota(jnp.int32, (tokens, slots), 1)
    picks = [cols_ref[:, i : i + 1] == lane for i in range(2)]
    both = jnp.where(picks[0] | picks[1], 1.0, 0.0).astype(BF16)
    dh2 = dot(both, dsent_ref[...])
    share = [
        jnp.sum(jnp.where(picks[i], share_ref[0:1, :], 0.0), axis=1, keepdims=True)
        for i in range(2)
    ]
    total = share[0] + share[1]
    dchosen = [share[i] - gates_ref[:, i : i + 1] * total for i in range(2)]
    experts = router_ref.shape[1]
    elane = lax.broadcasted_iota(jnp.int32, (tokens, experts), 1)
    dlogits = sum(
        jnp.where(route_ref[:, i : i + 1] == elane, dchosen[i], 0.0) for i in range(2)
    )
    dh2 = dh2 + split_dot(dlogits, router_ref[...], dot_nt)
    grouter_ref[...] = split_dot(dlogits, h2_ref[...], dot_tn)
    mid = mid_ref[...]
    r = lax.rsqrt(jnp.mean(mid * mid, axis=1, keepdims=True) + EPSILON)
    u = dh2 * gain_ref[...]
    mean = jnp.mean(u * mid, axis=1, keepdims=True)
    dmid = dz_ref[...].astype(F32) + r * u - (r * r * r) * mid * mean
    dmid_ref[...] = dmid
    ggain_ref[...] = jnp.sum(dh2 * mid * r, axis=0, keepdims=True)
    branch = dmid.astype(BF16)
    gwo_ref[...] = dot(at_ref[...], branch)
    dot_ref[...] = dot_nt(wo_ref[...], branch).astype(BF16)


def turn(dsent, share, cols, gates, routes, mid, dz, h2, gain, router, wo, attended_t):
    tokens, width = mid.shape
    return pl.pallas_call(
        functools.partial(turn_kernel, dsent.shape[0]),
        out_shape=(
            jax.ShapeDtypeStruct((tokens, width), F32),
            jax.ShapeDtypeStruct((width, tokens), BF16),
            jax.ShapeDtypeStruct((width, width), F32),
            jax.ShapeDtypeStruct((1, width), F32),
            jax.ShapeDtypeStruct((router.shape[1], width), F32),
        ),
        compiler_params=pltpu.CompilerParams(vmem_limit_bytes=48 * MIB),
        name="turn",
    )(dsent, share, cols, gates, routes, mid, dz, h2, gain, router, wo, attended_t)


def attention_back_kernel(
    lay, heads, dot_ref, e_ref, qkvn_ref, qkvt_ref, ot_ref, rl_ref, h1_ref, wt_ref, dh1_ref, gw_ref, gtab_ref, dst_scr, doT_scr, do_scr, dT_scr
):
    h = pl.program_id(0)
    feats = heads * HD
    hrow = pl.multiple_of(h * HD, HD)
    deltas = []
    for q in range(lay.blocks):
        cols = slice(q * BK, (q + 1) * BK)
        for c, start, at, size in lay.pieces[q]:
            piece = dot_ref[c, pl.ds(hrow, HD), start : start + size]
            where = q * BK + at
            doT_scr[:, where : where + size] = piece
        raw = doT_scr[:, cols].astype(F32)
        inverse = rl_ref[0, :, cols]
        deltas.append(
            inverse * jnp.sum(raw * ot_ref[pl.ds(hrow, HD), cols], axis=0, keepdims=True)
        )
        scaled = raw * inverse
        doT_scr[:, cols] = scaled.astype(BF16)
        do_scr[cols] = scaled.T.astype(BF16)
    krow = pl.multiple_of(feats + h * HD, HD)
    vrow = pl.multiple_of(2 * feats + h * HD, HD)
    for q in range(lay.blocks):
        cols = slice(q * BK, (q + 1) * BK)
        dq = 0.0
        for k in lay.keys[q]:
            t = lay.tile[(q, k)]
            rows = slice(k * BK, (k + 1) * BK)
            dp = dot(qkvn_ref[2 * heads + h, rows], doT_scr[:, cols])
            ds = (e_ref[0, t].astype(F32) * (dp - deltas[q])).astype(BF16)
            dst_scr[t] = ds
            dq = dq + dot(qkvt_ref[pl.ds(krow, HD), rows], ds)
        dT_scr[pl.ds(hrow, HD), cols] = (dq * HD**-0.5).astype(BF16)
    for k in range(lay.blocks):
        rows = slice(k * BK, (k + 1) * BK)
        dk, dv = 0.0, 0.0
        for q in range(lay.blocks):
            if k in lay.keys[q]:
                t = lay.tile[(q, k)]
                cols = slice(q * BK, (q + 1) * BK)
                dk = dk + dot(dst_scr[t], qkvn_ref[h, cols])
                dv = dv + dot(e_ref[0, t], do_scr[cols])
        dT_scr[pl.ds(krow, HD), rows] = dk.T.astype(BF16)
        dT_scr[pl.ds(vrow, HD), rows] = dv.T.astype(BF16)
    gtab_ref[...] = jnp.zeros_like(gtab_ref)
    for d in range(lay.distances):
        tile = 0.0
        for (q, k), t in lay.tile.items():
            if lay.distance(q, k) == d:
                tile = tile + dst_scr[t].astype(F32)
        sums = diagonal_sums(tile)
        gtab_ref[0, :, (d + 1) * BK : (d + 2) * BK] += sums[:, :BK]
        gtab_ref[0, :, d * BK : (d + 1) * BK] += sums[:, BK:]

    @pl.when(h == heads - 1)
    def _():
        for q in range(lay.blocks):
            cols = slice(q * BK, (q + 1) * BK)
            part = dot_tn(dT_scr[:, cols], wt_ref[...]).astype(BF16)
            for c, start, at, size in lay.pieces[q]:
                dh1_ref[c, start : start + size] = part[at : at + size]
        gw_ref[...] = dot(dT_scr[...], h1_ref[...])


def attention_backward(lay, heads, dattn_t, e, qkvn, qkvt, ot, rl, h1, weights_t):
    width = h1.shape[1]
    feats = heads * HD
    span = (lay.distances + 1) * BK
    return pl.pallas_call(
        functools.partial(attention_back_kernel, lay, heads),
        grid=(heads,),
        in_specs=[
            full(dattn_t.shape),
            pl.BlockSpec((1, lay.tiles, BK, BK), lambda h: (h, 0, 0, 0)),
            full(qkvn.shape),
            full(qkvt.shape),
            full(ot.shape),
            pl.BlockSpec((1, 1, lay.total), lambda h: (h, 0, 0)),
            full(h1.shape),
            full(weights_t.shape),
        ],
        out_specs=(
            full((lay.spread, lay.tokens, width)),
            full((3 * feats, width)),
            pl.BlockSpec((1, 1, span), lambda h: (h, 0, 0)),
        ),
        out_shape=(
            jax.ShapeDtypeStruct((lay.spread, lay.tokens, width), BF16),
            jax.ShapeDtypeStruct((3 * feats, width), F32),
            jax.ShapeDtypeStruct((heads, 1, span), F32),
        ),
        scratch_shapes=[
            VMEM((lay.tiles, BK, BK), BF16),
            VMEM((HD, lay.total), BF16),
            VMEM((lay.total, HD), BF16),
            VMEM((3 * feats, lay.total), BF16),
        ],
        compiler_params=pltpu.CompilerParams(vmem_limit_bytes=58 * MIB),
        name="attention_backward",
    )(dattn_t, e, qkvn, qkvt, ot, rl, h1, weights_t)


def finish_kernel(dh1_ref, x_ref, gain_ref, dmid_ref, dx_ref, ggain_ref):
    x = x_ref[...].astype(F32)
    dh1 = dh1_ref[...].astype(F32)
    r = lax.rsqrt(jnp.mean(x * x, axis=1, keepdims=True) + EPSILON)
    w = dh1 * gain_ref[...]
    mean = jnp.mean(w * x, axis=1, keepdims=True)
    dx_ref[...] = dmid_ref[...] + r * w - (r * r * r) * x * mean
    ggain_ref[...] = jnp.sum(dh1 * x * r, axis=0, keepdims=True)


def finish(dh1, x_local, gain, dmid):
    return pl.pallas_call(
        finish_kernel,
        out_shape=(
            jax.ShapeDtypeStruct(dmid.shape, F32),
            jax.ShapeDtypeStruct((1, dmid.shape[1]), F32),
        ),
        compiler_params=pltpu.CompilerParams(vmem_limit_bytes=32 * MIB),
        name="finish",
    )(dh1, x_local, gain, dmid)


def result_kernel(mid_ref, cols_ref, gates_ref, made_ref, out_ref):
    tokens = mid_ref.shape[0]
    slots = made_ref.shape[0]
    lane = lax.broadcasted_iota(jnp.int32, (tokens, slots), 1)
    out = mid_ref[...]
    for i in range(2):
        pick = jnp.where(cols_ref[:, i : i + 1] == lane, 1.0, 0.0).astype(BF16)
        out = out + gates_ref[:, i : i + 1] * dot(pick, made_ref[...])
    out_ref[...] = out.astype(BF16)


def result(mid, cols, gates, made):
    return pl.pallas_call(
        result_kernel,
        out_shape=jax.ShapeDtypeStruct(mid.shape, BF16),
        compiler_params=pltpu.CompilerParams(vmem_limit_bytes=32 * MIB),
        name="result",
    )(mid, cols, gates, made)


def body(
    prompt_in,
    cont_in,
    prompt_route,
    cont_route,
    order,
    buckets,
    attn_gain,
    w_query,
    w_key,
    w_value,
    w_attn_out,
    rel_bias,
    ffn_gain,
    router,
    w_in,
    w_out,
    prompt_cot,
    cont_cot,
):
    prompt_rows = prompt_in.shape[1]
    cont_count = cont_in.shape[1]
    cont_rows = cont_in.shape[2]
    width = prompt_in.shape[2]
    spread = lax.axis_size("context")
    expert_devices = lax.axis_size("expert")
    lay = Layout(spread, prompt_rows, cont_count, cont_rows)
    tokens = lay.tokens
    head_count = rel_bias.shape[1]
    heads = head_count // spread
    feats = heads * HD
    experts = w_in.shape[0] * expert_devices
    capacity = 9 * tokens * 2 // (8 * experts)
    slots = experts * capacity
    buckets_count = rel_bias.shape[0]
    context = lax.axis_index("context")

    def local_rows(prompt_part, cont_part):
        return jnp.concatenate(
            [prompt_part.reshape(prompt_rows, -1), cont_part.reshape(cont_count * cont_rows, -1)],
            axis=0,
        )

    def exchange(array, axis):
        return lax.all_to_all(array, axis, split_axis=0, concat_axis=0, tiled=True)

    x_local = local_rows(prompt_in, cont_in)
    routes = local_rows(prompt_route, cont_route)
    upstream = local_rows(prompt_cot, cont_cot)
    gain_one = attn_gain.reshape(1, width)
    gain_two = ffn_gain.reshape(1, width)
    h1, qkvn, qkvt, e, ot, rl, weights, cols, rows, at, dz_slots = front(
        lay,
        heads,
        expert_devices,
        capacity,
        prompt_in.reshape(prompt_rows, width),
        cont_in.reshape(cont_count * cont_rows, width),
        prompt_route.reshape(prompt_rows, 2),
        cont_route.reshape(cont_count * cont_rows, 2),
        order.reshape(1, tokens),
        buckets.reshape(1, -1),
        gain_one,
        w_query,
        w_key,
        w_value,
        rel_bias,
        prompt_cot.reshape(prompt_rows, width),
        cont_cot.reshape(cont_count * cont_rows, width),
    )
    slot_cols, slot_rows = cols.astype(jnp.int32), rows.astype(jnp.int32)
    turned = jnp.arange(expert_devices, dtype=jnp.int32) ^ lax.axis_index("expert")
    dz_slots = dz_slots[turned].reshape(slots, -1)
    attended_t = at.reshape(width, tokens)
    bucket_hot = (buckets[:, None] == jnp.arange(buckets_count, dtype=jnp.int32)[None, :]).astype(F32)
    weights_t = weights.T
    mid, h2, gates, sent = middle(
        attended_t, x_local, w_attn_out, gain_two, router, routes, slot_rows, experts, capacity
    )
    arrived = exchange(sent.reshape(expert_devices, slots // expert_devices, width), "expert")
    arrived = arrived.reshape(slots, width)
    act, dpre, dsent, dmade, share = expert_grad(arrived, dz_slots, router, w_in, w_out)
    dsent = exchange(dsent.reshape(expert_devices, slots // expert_devices, width), "expert")
    share = exchange(share[:, 0].reshape(expert_devices, slots // expert_devices), "expert")
    made, g_in, g_out = expert_weights(arrived, dmade, act, dpre, w_out)
    dmid, dattn_t, g_wo, g_gain_two, g_router = turn(
        dsent.reshape(slots, width),
        share.reshape(1, slots),
        slot_cols,
        gates,
        routes,
        mid,
        upstream,
        h2,
        gain_two,
        router,
        w_attn_out,
        attended_t,
    )
    dattn_t = exchange(dattn_t.reshape(spread, feats, tokens), "context")
    made = exchange(made.reshape(expert_devices, slots // expert_devices, width), "expert")
    g_in_sum, g_out_sum = (
        lax.psum_scatter(g, ("dp", "context"), scatter_dimension=1, tiled=True).astype(F32)
        for g in (g_in, g_out)
    )
    dh1, g_qkv, g_table = attention_backward(
        lay, heads, dattn_t, e, qkvn, qkvt, ot, rl, h1, weights_t
    )
    dh1 = lax.psum_scatter(dh1, "context", scatter_dimension=0, tiled=False)
    dx, g_gain_one = finish(dh1, x_local, gain_one, dmid)
    out = result(mid, slot_cols, gates, made.reshape(slots, width))

    g_bias = jnp.dot(g_table[:, 0, BK:], bucket_hot, precision=PRECISE)
    g_bias = lax.dynamic_update_slice_in_dim(
        jnp.zeros((head_count, width), F32), jnp.pad(g_bias, ((0, 0), (0, width - buckets_count))), context * heads, 0
    )
    small = jnp.concatenate([g_gain_one, g_gain_two, g_router, g_bias], axis=0)
    g_wo, small = lax.psum((g_wo, small), ("dp", "context", "expert"))
    g_qkv = lax.psum(g_qkv, ("dp", "expert"))
    g_qkv = lax.all_gather(g_qkv, "context", axis=0, tiled=False)
    g_qkv = g_qkv.reshape(spread, 3, feats, width)
    g_query, g_key, g_value = (g_qkv[:, i].reshape(width, width).T for i in range(3))
    g_bias = small[2 + experts :, :buckets_count].T
    g_router = small[2 : 2 + experts].T
    return (
        out[:prompt_rows].reshape(1, prompt_rows, width),
        out[prompt_rows:].reshape(1, cont_count, cont_rows, width),
        dx[:prompt_rows].reshape(1, prompt_rows, width),
        dx[prompt_rows:].reshape(1, cont_count, cont_rows, width),
        small[0],
        g_query,
        g_key,
        g_value,
        g_wo,
        g_bias,
        small[1],
        g_router,
        g_in_sum,
        g_out_sum,
    )


def solution(mesh):
    split = P(("dp", "expert"), "context", None)
    split_cont = P(("dp", "expert"), None, "context", None)
    whole = P()
    expert = P("expert", None, None)
    grad = P("expert", ("dp", "context"), None)
    return jax.shard_map(
        body,
        mesh=mesh,
        in_specs=(split, split_cont, split, split_cont, split)
        + (whole,) * 9
        + (expert, expert, split, split_cont),
        out_specs=(split, split_cont, split, split_cont) + (whole,) * 8 + (grad, grad),
        check_vma=False,
    )
```

```python
import functools

import jax
import jax.numpy as jnp
from jax import lax
from jax.experimental import pallas as pl
from jax.experimental.pallas import tpu as pltpu
from jax.sharding import PartitionSpec as P

HD = 64
BK = 256
BUCKETS = 32
EPSILON = 1e-06
MASKED = -1e30
F32 = jnp.float32
BF16 = jnp.bfloat16
VMEM = pltpu.VMEM
MESH = pl.DeviceIdType.MESH
MIB = 1 << 20


def dot(a, b):
    return lax.dot_general(a, b, (((1,), (0,)), ((), ())), preferred_element_type=F32)


def dot_nt(a, b):
    return lax.dot_general(a, b, (((1,), (1,)), ((), ())), preferred_element_type=F32)


def dot_tn(a, b):
    return lax.dot_general(a, b, (((0,), (0,)), ((), ())), preferred_element_type=F32)


def split_dot(a, b, op):
    high = a.astype(BF16)
    low = (a - high.astype(F32)).astype(BF16)
    return op(high, b) + op(low, b)


def full(shape):
    return pl.BlockSpec(shape, lambda *_: (0,) * len(shape))


class Layout:
    def __init__(self, spread, prompt_rows, cont_count, cont_rows):
        assert prompt_rows == BK and BK % cont_rows == 0
        self.spread = spread
        self.prompt_rows = prompt_rows
        self.cont_count = cont_count
        self.cont_rows = cont_rows
        self.tokens = prompt_rows + cont_count * cont_rows
        self.per_cont = spread * cont_rows // BK
        self.blocks = spread + cont_count * self.per_cont
        self.total = self.blocks * BK
        self.keys, self.place, self.pieces = [], [], []
        for p in range(spread):
            self.keys.append(list(range(p + 1)))
            self.place.append(p)
            self.pieces.append([(p, 0, 0, BK)])
        each = BK // cont_rows
        for j in range(cont_count):
            for m in range(self.per_cont):
                first = spread + j * self.per_cont
                self.keys.append(list(range(spread)) + list(range(first, first + m + 1)))
                self.place.append(spread + m)
                self.pieces.append(
                    [
                        (m * each + n, prompt_rows + j * cont_rows, n * cont_rows, cont_rows)
                        for n in range(each)
                    ]
                )
        self.tile = {}
        for q in range(self.blocks):
            for k in self.keys[q]:
                self.tile[(q, k)] = len(self.tile)
        self.tiles = len(self.tile)
        self.distances = spread + self.per_cont

    def distance(self, q, k):
        return self.place[q] - self.place[k]


def flip(index, mask):
    bit = 1
    while bit <= mask:
        if mask & bit:
            index = index + bit * (1 - 2 * ((index // bit) % 2))
        bit *= 2
    return index


def remote(src, dst, send, recv, **where):
    return pltpu.make_async_remote_copy(
        src_ref=src,
        dst_ref=dst,
        send_sem=send,
        recv_sem=recv,
        device_id=where,
        device_id_type=MESH,
    )


def greet(partners):
    barrier = pltpu.get_barrier_semaphore()
    for where in partners:
        pl.semaphore_signal(barrier, inc=1, device_id=where, device_id_type=MESH)
    pl.semaphore_wait(barrier, len(partners))


def make_plan(capacity, routes, order_row):
    tokens = routes.shape[0]
    side = (tokens, tokens)
    lane = lax.broadcasted_iota(jnp.int32, side, 1).astype(F32)
    sub = lax.broadcasted_iota(jnp.int32, side, 0)
    rank_col = jnp.sum(jnp.where(order_row == sub, lane, 0.0), axis=1, keepdims=True)
    rank_row = jnp.broadcast_to(rank_col, (tokens, 128)).T[0:1]
    before = jnp.where(rank_row < rank_col, 1.0, 0.0).astype(BF16)
    expert_lane = lax.broadcasted_iota(jnp.int32, (tokens, 128), 1).astype(F32)
    hots = [jnp.where(routes[:, i : i + 1] == expert_lane, 1.0, 0.0) for i in range(2)]
    counts = [dot(before, hot.astype(BF16)) for hot in hots]
    counts[1] = counts[1] + jnp.sum(hots[0], axis=0, keepdims=True)
    cols = jnp.zeros((tokens, 128), F32)
    for i in range(2):
        pos = jnp.sum(hots[i] * counts[i], axis=1, keepdims=True)
        route = routes[:, i : i + 1]
        slot = jnp.where(pos < capacity, route * capacity + pos, -1.0)
        cols = jnp.where(expert_lane == i, slot, cols)
        cols = jnp.where(expert_lane == 2 + i, route, cols)
    return cols, cols.T[0:8], hots


def toeplitz_tile(table_row, d):
    line = jnp.concatenate(
        [table_row[:, (d + 1) * BK : (d + 2) * BK], table_row[:, d * BK : (d + 1) * BK]], axis=1
    )
    tile = jnp.broadcast_to(line, (8, 2 * BK))
    row = lax.broadcasted_iota(jnp.int32, (8, 2 * BK), 0)
    for bit in (1, 2, 4):
        tile = jnp.where((row & bit) > 0, pltpu.roll(tile, bit, 1), tile)
    height = 8
    while height < BK:
        tile = jnp.concatenate([tile, pltpu.roll(tile, height, 1)], axis=0)
        height *= 2
    tile = tile[:, :BK]
    if d == 0:
        key = lax.broadcasted_iota(jnp.int32, (BK, BK), 0)
        query = lax.broadcasted_iota(jnp.int32, (BK, BK), 1)
        tile = jnp.where(query >= key, tile, MASKED)
    return tile


def diagonal_sums(tile):
    tile = jnp.concatenate([tile, jnp.zeros((BK, BK), F32)], axis=1)
    height = BK
    while height > 8:
        height //= 2
        tile = tile[:height] + pltpu.roll(tile[height:], 2 * BK - height, 1)
    row = lax.broadcasted_iota(jnp.int32, (8, 2 * BK), 0)
    for bit in (1, 2, 4):
        tile = jnp.where((row & bit) > 0, pltpu.roll(tile, 2 * BK - bit, 1), tile)
    return jnp.sum(tile, axis=0, keepdims=True)


def front_kernel(
    lay,
    heads,
    peers,
    capacity,
    xp_ref,
    xc_ref,
    rp_ref,
    rc_ref,
    order_ref,
    buckets_ref,
    gain_ref,
    wq_ref,
    wk_ref,
    wv_ref,
    bias_ref,
    zp_ref,
    zc_ref,
    h1_ref,
    qkvn_ref,
    qkvt_ref,
    e_ref,
    ot_ref,
    rl_ref,
    w_ref,
    cols_ref,
    rows_ref,
    at_ref,
    dz_ref,
    x_all,
    at_scr,
    dz_scr,
    s_scr,
    bias_scr,
    x_send,
    x_recv,
    a_send,
    a_recv,
    z_send,
    z_recv,
    own_sem,
):
    h = pl.program_id(0)
    me = lax.axis_index("context")
    expert = lax.axis_index("expert")
    feats = heads * HD
    half = lay.prompt_rows
    near, across, far = flip(me, 1), flip(me, 2), flip(me, 3)
    width = gain_ref.shape[1]

    def x_copy(slot, part, index, target):
        view = x_all.at[slot, pl.ds(part * half, half)]
        return remote(view, view, x_send.at[index], x_recv.at[index], context=target)

    def z_copy(k):
        return remote(
            dz_scr.at[k], dz_ref.at[k], z_send.at[k], z_recv.at[k], expert=flip(expert, k)
        )

    def a_copy(k, head):
        target = flip(me, k)
        src = at_scr.at[target, pl.ds(head * HD, HD)]
        dst = at_ref.at[me, pl.ds(head * HD, HD)]
        return remote(src, dst, a_send.at[head, k], a_recv.at[head, k], context=target)

    def a_own(head):
        return pltpu.make_async_copy(
            at_scr.at[me, pl.ds(head * HD, HD)],
            at_ref.at[me, pl.ds(head * HD, HD)],
            a_send.at[head, 0],
        )

    z_own = pltpu.make_async_copy(dz_scr.at[0], dz_ref.at[0], own_sem)

    def project(slot):
        x = x_all[slot].astype(F32)
        r = lax.rsqrt(jnp.mean(x * x, axis=1, keepdims=True) + EPSILON)
        normed = (x * r * gain_ref[...]).astype(BF16)
        y = dot(normed, w_ref[...])
        scale = jnp.where(lax.broadcasted_iota(jnp.int32, y.shape, 1) < feats, HD**-0.5, 1.0)
        y = (y.astype(BF16).astype(F32) * scale).astype(BF16)
        yt = y.T
        spots = [(0, pl.multiple_of(slot * half, 128), half)]
        for j in range(lay.cont_count):
            first = lay.spread * half + j * lay.spread * lay.cont_rows
            spots.append(
                (
                    half + j * lay.cont_rows,
                    pl.multiple_of(first + slot * lay.cont_rows, 128),
                    lay.cont_rows,
                )
            )
        for start, to, size in spots:
            h1_ref[pl.ds(to, size)] = normed[start : start + size]
            qkvt_ref[:, pl.ds(to, size)] = yt[:, start : start + size]
            for i in range(3 * heads):
                qkvn_ref[i, pl.ds(to, size)] = y[start : start + size, i * HD : (i + 1) * HD]

    @pl.when(h == 0)
    def _():
        greet(
            [{"context": t} for t in (near, across, far)]
            + [{"expert": flip(expert, k)} for k in range(1, peers)]
        )
        x_all[me, :half] = xp_ref[...]
        x_all[me, half:] = xc_ref[...]
        for part in range(2):
            x_copy(me, part, part, across).start()
        for part in range(2):
            x_copy(me, part, 2 + part, near).start()
        tokens = lay.tokens
        lane = lax.broadcasted_iota(jnp.int32, (tokens, 128), 1)
        routes = jnp.concatenate([rp_ref[...], rc_ref[...]], axis=0).astype(F32)
        routes = jnp.where(lane == 0, routes[:, 0:1], routes[:, 1:2])
        cols, rows, hots = make_plan(capacity, routes, order_ref[...])
        cols_ref[...] = cols
        rows_ref[...] = rows
        dz = jnp.concatenate([zp_ref[...], zc_ref[...]], axis=0)
        for k in list(range(1, peers)) + [0]:
            base = flip(expert, k) * capacity
            number = (lax.broadcasted_iota(jnp.int32, (capacity, tokens), 0) + base).astype(F32)
            first = jnp.where(rows[0:1] == number, 1.0, 0.0)
            second = jnp.where(rows[1:2] == number, 1.0, 0.0)
            dz_scr[k, :, :width] = dot((first + second).astype(BF16), dz).astype(BF16)
            other = dot(first.astype(BF16), hots[1].astype(BF16))
            other = other + dot(second.astype(BF16), hots[0].astype(BF16))
            dz_scr[k, :, width:] = other.astype(BF16)
            if k:
                z_copy(k).start()
            else:
                z_own.start()
        for c in range(lay.spread):

            @pl.when(me == c)
            def _():
                for i, ref in enumerate((wq_ref, wk_ref, wv_ref)):
                    w_ref[:, i * feats : (i + 1) * feats] = ref[:, c * feats : (c + 1) * feats]

        project(me)
        for part in range(2):
            x_copy(near, part, 2 + part, near).wait_recv()
        project(near)
        for part in range(2):
            x_copy(across, part, part, across).wait_recv()
            x_copy(across, part, 4 + part, near).start()
        project(across)
        for part in range(2):
            x_copy(far, part, 4 + part, near).wait_recv()
        project(far)
        for part in range(2):
            x_copy(me, part, part, across).wait_send()
            x_copy(me, part, 2 + part, near).wait_send()
            x_copy(across, part, 4 + part, near).wait_send()

    column = lax.broadcasted_iota(jnp.int32, bias_ref.shape, 1) == me * heads + h
    column = jnp.sum(jnp.where(column, bias_ref[...], 0.0), axis=1, keepdims=True)
    span = buckets_ref.shape[1]
    number = lax.broadcasted_iota(jnp.int32, (bias_ref.shape[0], span), 0)
    table_row = jnp.sum(
        jnp.where(buckets_ref[...] == number, column, 0.0), axis=0, keepdims=True
    )
    table_row = jnp.concatenate([jnp.zeros((1, BK), F32), table_row], axis=1)
    for d in range(lay.distances):
        bias_scr[d] = toeplitz_tile(table_row, d)
    hrow = pl.multiple_of(h * HD, HD)
    vrow = pl.multiple_of(2 * feats + h * HD, HD)
    for q in range(lay.blocks):
        qt = qkvt_ref[pl.ds(hrow, HD), q * BK : (q + 1) * BK]
        top = None
        for n, k in enumerate(lay.keys[q]):
            s = dot(qkvn_ref[heads + h, k * BK : (k + 1) * BK], qt) + bias_scr[lay.distance(q, k)]
            s_scr[n] = s
            m = jnp.max(s, axis=0, keepdims=True)
            top = m if top is None else jnp.maximum(top, m)
        total, out = 0.0, 0.0
        for n, k in enumerate(lay.keys[q]):
            e = jnp.exp(s_scr[n] - top)
            total = total + jnp.sum(e, axis=0, keepdims=True)
            e = e.astype(BF16)
            e_ref[0, lay.tile[(q, k)]] = e
            out = out + dot(qkvt_ref[pl.ds(vrow, HD), k * BK : (k + 1) * BK], e)
        inverse = 1.0 / total
        rl_ref[0, :, q * BK : (q + 1) * BK] = inverse
        out = out * inverse
        ot_ref[pl.ds(hrow, HD), q * BK : (q + 1) * BK] = out
        for c, start, at, size in lay.pieces[q]:
            at_scr[c, pl.ds(hrow, HD), start : start + size] = out[:, at : at + size].astype(BF16)

    for k in (3, 2, 1):
        a_copy(k, h).start()
    a_own(h).start()

    @pl.when(h == heads - 1)
    def _():
        for head in range(heads):
            a_own(head).wait()
            for k in (1, 2, 3):
                a_copy(k, head).wait()
        z_own.wait()
        for k in range(1, peers):
            z_copy(k).wait()


def front(lay, heads, peers, capacity, *args):
    width = args[0].shape[1]
    feats = heads * HD
    dma = pltpu.SemaphoreType.DMA
    anywhere = pl.BlockSpec(memory_space=pl.ANY)
    return pl.pallas_call(
        functools.partial(front_kernel, lay, heads, peers, capacity),
        grid=(heads,),
        in_specs=[full(a.shape) for a in args],
        out_specs=(
            full((lay.total, width)),
            full((3 * heads, lay.total, HD)),
            full((3 * feats, lay.total)),
            pl.BlockSpec((1, lay.tiles, BK, BK), lambda h: (h, 0, 0, 0)),
            full((feats, lay.total)),
            pl.BlockSpec((1, 1, lay.total), lambda h: (h, 0, 0)),
            full((width, 3 * feats)),
            full((lay.tokens, 128)),
            full((8, lay.tokens)),
            anywhere,
            anywhere,
        ),
        out_shape=(
            jax.ShapeDtypeStruct((lay.total, width), BF16),
            jax.ShapeDtypeStruct((3 * heads, lay.total, HD), BF16),
            jax.ShapeDtypeStruct((3 * feats, lay.total), BF16),
            jax.ShapeDtypeStruct((heads, lay.tiles, BK, BK), BF16),
            jax.ShapeDtypeStruct((feats, lay.total), F32),
            jax.ShapeDtypeStruct((heads, 1, lay.total), F32),
            jax.ShapeDtypeStruct((width, 3 * feats), BF16),
            jax.ShapeDtypeStruct((lay.tokens, 128), F32),
            jax.ShapeDtypeStruct((8, lay.tokens), F32),
            jax.ShapeDtypeStruct((lay.spread, feats, lay.tokens), BF16),
            jax.ShapeDtypeStruct((peers, capacity, width + 128), BF16),
        ),
        scratch_shapes=[
            VMEM((lay.spread, lay.tokens, width), BF16),
            VMEM((lay.spread, feats, lay.tokens), BF16),
            VMEM((peers, capacity, width + 128), BF16),
            VMEM((max(len(k) for k in lay.keys), BK, BK), F32),
            VMEM((lay.distances, BK, BK), F32),
            dma((6,)),
            dma((6,)),
            dma((heads, 4)),
            dma((heads, 4)),
            dma((peers,)),
            dma((peers,)),
            dma,
        ],
        compiler_params=pltpu.CompilerParams(
            vmem_limit_bytes=60 * MIB, collective_id=0, has_side_effects=True
        ),
        name="front",
    )(*args)


def gelu_parts(u):
    slope = 0.7978845608028654
    cube = 0.044715
    square = u * u
    t = jnp.tanh(slope * u * (1.0 + cube * square))
    half = 0.5 * (1.0 + t)
    value = u * half
    grad = half + 0.5 * u * (1.0 - t * t) * (slope * (1.0 + 3.0 * cube * square))
    return value, grad


def turn_index(index, mask, size):
    bit = 1
    while bit < size:
        index = index + ((mask // bit) % 2) * bit * (1 - 2 * ((index // bit) % 2))
        bit *= 2
    return index


def experts_kernel(
    peers,
    pairs,
    capacity,
    at_ref,
    xp_ref,
    xc_ref,
    wo_ref,
    gain_ref,
    router_ref,
    cols_ref,
    rows_ref,
    zp_ref,
    zc_ref,
    w_in_ref,
    w_out_ref,
    dz_ref,
    mid_ref,
    gates_ref,
    dmid_ref,
    gwo_ref,
    gsmall_ref,
    made_ref,
    gin_ref,
    gout_ref,
    da_ref,
    w_in,
    w_out,
    dz,
    sent,
    arrived,
    act_scr,
    dpre_scr,
    dsent,
    back,
    share,
    share_back,
    h2_scr,
    gin,
    gout,
    gin_near,
    gout_near,
    da_scr,
    load_sem,
    s_send,
    s_recv,
    r_send,
    r_recv,
    h_send,
    h_recv,
    p_send,
    p_recv,
    d_send,
    d_recv,
    out_sem,
):
    me = lax.axis_index("context")
    expert = lax.axis_index("expert")
    core = me % 2
    near = flip(me, 1)
    tokens = cols_ref.shape[0]
    width = gain_ref.shape[1]
    hidden = w_in_ref.shape[2]
    lanes = share.shape[2]
    chunk = 512
    loads = [
        pltpu.make_async_copy(dz_ref, dz, load_sem.at[0]),
        pltpu.make_async_copy(w_in_ref.at[0], w_in, load_sem.at[1]),
        pltpu.make_async_copy(w_out_ref.at[0], w_out, load_sem.at[2]),
    ]
    for copy in loads:
        copy.start()
    greet(
        [{"context": flip(me, k)} for k in (1, 2, 3)]
        + [{"expert": flip(expert, k)} for k in range(1, peers)]
    )

    def to_peer(k, src, dst, send, recv):
        target = turn_index(expert, k, peers)
        return remote(src.at[k], dst.at[k], send.at[k], recv.at[k], expert=target)

    def dispatch(k):
        return to_peer(k, sent, arrived, s_send, s_recv)

    def returns(k):
        return (
            to_peer(k, dsent, back, r_send, r_recv),
            to_peer(k, share, share_back, h_send, h_recv),
        )

    mid = jnp.concatenate([xp_ref[...], xc_ref[...]], axis=0).astype(F32)
    mid = mid + dot_tn(at_ref[...], wo_ref[...])
    mid_ref[...] = mid
    r = lax.rsqrt(jnp.mean(mid * mid, axis=1, keepdims=True) + EPSILON)
    h2_scr[...] = (mid * r * gain_ref[...]).astype(BF16)
    for k in list(range(1, peers)) + [0]:
        base = flip(expert, k) * capacity
        number = (lax.broadcasted_iota(jnp.int32, (capacity, tokens), 0) + base).astype(F32)
        pick = (rows_ref[0:1] == number) | (rows_ref[1:2] == number)
        block = dot(jnp.where(pick, 1.0, 0.0).astype(BF16), h2_scr[...]).astype(BF16)
        if k:
            sent[k] = block
            dispatch(k).start()
        else:
            arrived[0] = block
    logits = dot(h2_scr[...], router_ref[...])
    lane = lax.broadcasted_iota(jnp.int32, logits.shape, 1).astype(F32)
    hots = [cols_ref[:, 2 + i : 3 + i] == lane for i in range(2)]
    chosen = [jnp.sum(jnp.where(hot, logits, 0.0), axis=1, keepdims=True) for hot in hots]
    most = jnp.maximum(chosen[0], chosen[1])
    parts = [jnp.exp(c - most) for c in chosen]
    inverse = 1.0 / (parts[0] + parts[1])
    gates = [p * inverse for p in parts]
    wide = lax.broadcasted_iota(jnp.int32, (tokens, 128), 1)
    gates_ref[...] = jnp.where(wide == 0, gates[0], jnp.where(wide == 1, gates[1], 0.0))
    for copy in loads:
        copy.wait()

    def process(k):
        rows = arrived[k]
        scores = dot(rows, router_ref[...])
        elane = lax.broadcasted_iota(jnp.int32, scores.shape, 1)
        own = jnp.sum(jnp.where(elane == expert, scores, 0.0), axis=1, keepdims=True)
        other_hot = dz[k, :, width : width + scores.shape[1]].astype(F32)
        other = jnp.sum(other_hot * scores, axis=1, keepdims=True)
        gate = 1.0 / (1.0 + jnp.exp(other - own))
        dmade = (gate * dz[k, :, :width].astype(F32)).astype(BF16)
        dz[k, :, :width] = dmade
        where = pl.ds(pl.multiple_of(k * capacity, 16), capacity)
        total, part = 0.0, 0.0
        for f in range(0, hidden, chunk):
            pre = dot(rows, w_in[:, f : f + chunk])
            dact = dot_nt(dmade, w_out[f : f + chunk])
            value, grad = gelu_parts(pre)
            act = value.astype(BF16)
            act_scr[where, f : f + chunk] = act
            dpre = (dact * grad).astype(BF16)
            dpre_scr[where, f : f + chunk] = dpre
            product = act.astype(F32) * dact
            for i in range(0, chunk, 128):
                part = part + product[:, i : i + 128]
            total = total + dot_nt(dpre, w_in[:, f : f + chunk])
        dsent[k] = total.astype(BF16)
        column = jnp.broadcast_to(jnp.sum(part, axis=1, keepdims=True), (capacity, 128))
        column = jnp.concatenate([column, jnp.zeros((lanes - capacity, 128), F32)], axis=0)
        share[k] = column.T[:8]

    process(0)

    @pl.loop(1, peers)
    def _(k):
        dispatch(k).wait_recv()
        process(k)
        for copy in returns(k):
            copy.start()

    @pl.loop(1, peers)
    def _(k):
        dispatch(k).wait_send()

    def near_copies(pair):
        return (
            remote(
                gout.at[pair, 1 - core],
                gout_near.at[pair],
                p_send.at[0, pair],
                p_recv.at[0, pair],
                context=near,
            ),
            remote(
                gin.at[pair, 1 - core],
                gin_near.at[pair],
                p_send.at[1, pair],
                p_recv.at[1, pair],
                context=near,
            ),
        )

    def store_copies(pair):
        return (
            pltpu.make_async_copy(gout.at[pair, core], gout_ref.at[pair], out_sem.at[0, pair]),
            pltpu.make_async_copy(gin.at[pair, core], gin_ref.at[pair], out_sem.at[1, pair]),
        )

    slots = peers * capacity
    out_rows, in_rows = gout.shape[2], gin.shape[2]
    dmade_all = dz[:, :, :width].reshape(slots, width)
    for pair in range(pairs):
        left = act_scr[:, 2 * pair * out_rows : 2 * (pair + 1) * out_rows]
        grad = dot_tn(left, dmade_all).astype(BF16)
        gout[pair, 0] = grad[:out_rows]
        gout[pair, 1] = grad[out_rows:]
        near_copies(pair)[0].start()
    for pair in range(pairs):
        left = arrived[:, :, 2 * pair * in_rows : 2 * (pair + 1) * in_rows]
        left = left.reshape(slots, 2 * in_rows)
        for f in range(0, hidden, 2 * chunk):
            grad = dot_tn(left, dpre_scr[:, f : f + 2 * chunk]).astype(BF16)
            gin[pair, 0, :, f : f + 2 * chunk] = grad[:in_rows]
            gin[pair, 1, :, f : f + 2 * chunk] = grad[in_rows:]
        near_copies(pair)[1].start()

    @pl.loop(0, peers)
    def _(k):
        where = pl.ds(pl.multiple_of(k * capacity, 16), capacity)
        sent[k] = dot(act_scr[where], w_out[...]).astype(BF16)

    made_copy = pltpu.make_async_copy(sent, made_ref, load_sem.at[0])
    made_copy.start()
    for pair in range(pairs):
        for copy in near_copies(pair):
            copy.wait_recv()
        gout[pair, core] = (gout[pair, core].astype(F32) + gout_near[pair].astype(F32)).astype(BF16)
        gin[pair, core] = (gin[pair, core].astype(F32) + gin_near[pair].astype(F32)).astype(BF16)
        for copy in store_copies(pair):
            copy.start()

    dmid_ref[...] = jnp.zeros_like(dmid_ref)

    def collect(k, shares, block, share_row):
        base = (turn_index(expert, k, peers) * capacity).astype(F32)
        number = lax.broadcasted_iota(jnp.int32, (tokens, lanes), 1).astype(F32) + base
        picks = [cols_ref[:, i : i + 1] == number for i in range(2)]
        both = jnp.where(picks[0] | picks[1], 1.0, 0.0)[:, :capacity].astype(BF16)
        dmid_ref[...] += dot(both, block)
        return tuple(
            shares[i] + jnp.sum(jnp.where(picks[i], share_row, 0.0), axis=1, keepdims=True)
            for i in range(2)
        )

    zero = jnp.zeros((tokens, 1), F32)
    shares = collect(0, (zero, zero), dsent[0], share[0, 0:1])

    def gather_step(k, shares):
        for copy in returns(k):
            copy.wait()
        return collect(k, shares, back[k], share_back[k, 0:1])

    shares = lax.fori_loop(1, peers, gather_step, shares)
    total = shares[0] + shares[1]
    dchosen = [shares[i] - gates_ref[:, i : i + 1] * total for i in range(2)]
    elane = lax.broadcasted_iota(jnp.int32, (tokens, router_ref.shape[1]), 1).astype(F32)
    dlogits = sum(
        jnp.where(cols_ref[:, 2 + i : 3 + i] == elane, dchosen[i], 0.0) for i in range(2)
    )
    dh2 = dmid_ref[...] + split_dot(dlogits, router_ref[...], dot_nt)
    mid = mid_ref[...]
    r = lax.rsqrt(jnp.mean(mid * mid, axis=1, keepdims=True) + EPSILON)
    u = dh2 * gain_ref[...]
    mean = jnp.mean(u * mid, axis=1, keepdims=True)
    cot = jnp.concatenate([zp_ref[...], zc_ref[...]], axis=0).astype(F32)
    dmid = cot + r * u - (r * r * r) * mid * mean
    dmid_ref[...] = dmid
    branch = dmid.astype(BF16)
    feats = da_scr.shape[1]

    def da_copy(k):
        target = flip(me, k)
        return remote(
            da_scr.at[k], da_ref.at[me], d_send.at[k], d_recv.at[k], context=target
        )

    da_own = pltpu.make_async_copy(da_scr.at[0], da_ref.at[me], d_send.at[0])
    for k in (3, 2, 1, 0):
        first = pl.multiple_of(flip(me, k) * feats, 64)
        da_scr[k] = dot_nt(wo_ref[pl.ds(first, feats)], branch).astype(BF16)
        if k:
            da_copy(k).start()
        else:
            da_own.start()
    gsmall_ref[0:1] = jnp.sum(dh2 * mid * r, axis=0, keepdims=True)
    gsmall_ref[1:] = split_dot(dlogits, h2_scr[...], dot_tn)
    gwo_ref[...] = dot(at_ref[...], branch).astype(BF16)
    da_own.wait()
    for k in (1, 2, 3):
        da_copy(k).wait()
    made_copy.wait()
    for pair in range(pairs):
        for copy in store_copies(pair):
            copy.wait()
        for copy in near_copies(pair):
            copy.wait_send()


def experts_layer(peers, pairs, spread, capacity, *args):
    at, xp, xc, wo, gain, router, cols, rows, zp, zc, w_in, w_out, dz = args
    tokens, width = cols.shape[0], gain.shape[1]
    hidden = w_in.shape[2]
    slots = peers * capacity
    in_rows, out_rows = width // (2 * pairs), hidden // (2 * pairs)
    lanes = -(-capacity // 128) * 128
    dma = pltpu.SemaphoreType.DMA
    anywhere = pl.BlockSpec(memory_space=pl.ANY)
    inside = pl.BlockSpec(memory_space=VMEM)
    return pl.pallas_call(
        functools.partial(experts_kernel, peers, pairs, capacity),
        in_specs=[inside] * 10 + [anywhere] * 3,
        out_specs=(inside,) * 5 + (anywhere,) * 4,
        out_shape=(
            jax.ShapeDtypeStruct((tokens, width), F32),
            jax.ShapeDtypeStruct((tokens, 128), F32),
            jax.ShapeDtypeStruct((tokens, width), F32),
            jax.ShapeDtypeStruct((width, width), BF16),
            jax.ShapeDtypeStruct((1 + router.shape[1], width), F32),
            jax.ShapeDtypeStruct((peers, capacity, width), BF16),
            jax.ShapeDtypeStruct((pairs, in_rows, hidden), BF16),
            jax.ShapeDtypeStruct((pairs, out_rows, width), BF16),
            jax.ShapeDtypeStruct((spread, width // spread, tokens), BF16),
        ),
        scratch_shapes=[
            VMEM((width, hidden), BF16),
            VMEM((hidden, width), BF16),
            VMEM((peers, capacity, width + 128), BF16),
            VMEM((peers, capacity, width), BF16),
            VMEM((peers, capacity, width), BF16),
            VMEM((slots, hidden), BF16),
            VMEM((slots, hidden), BF16),
            VMEM((peers, capacity, width), BF16),
            VMEM((peers, capacity, width), BF16),
            VMEM((peers, 8, lanes), F32),
            VMEM((peers, 8, lanes), F32),
            VMEM((tokens, width), BF16),
            VMEM((pairs, 2, in_rows, hidden), BF16),
            VMEM((pairs, 2, out_rows, width), BF16),
            VMEM((pairs, in_rows, hidden), BF16),
            VMEM((pairs, out_rows, width), BF16),
            VMEM((spread, width // spread, tokens), BF16),
            dma((3,)),
            dma((peers,)),
            dma((peers,)),
            dma((peers,)),
            dma((peers,)),
            dma((peers,)),
            dma((peers,)),
            dma((2, pairs)),
            dma((2, pairs)),
            dma((spread,)),
            dma((spread,)),
            dma((2, pairs)),
        ],
        compiler_params=pltpu.CompilerParams(
            vmem_limit_bytes=63 * MIB, collective_id=1, has_side_effects=True
        ),
        name="experts",
    )(*args)


def rear_kernel(
    lay,
    heads,
    groups,
    peers,
    da_ref,
    e_ref,
    qkvn_ref,
    qkvt_ref,
    ot_ref,
    rl_ref,
    h1_ref,
    w_ref,
    buckets_ref,
    gsmall_ref,
    gwo_ref,
    made_ref,
    gin_ref,
    gout_ref,
    dh_ref,
    gin_own_ref,
    gout_own_ref,
    small_ref,
    bias_ref,
    back_ref,
    gin_far_ref,
    gout_far_ref,
    dh_far_ref,
    sums_ref,
    ds_scr,
    dot_scr,
    do_scr,
    dt_scr,
    dh_scr,
    dh_near,
    gin_scr,
    gin_land,
    gout_scr,
    gout_land,
    wo_near,
    wo_far,
    wo_send,
    shares,
    share_land,
    total_scr,
    small_scr,
    small_land,
    bias_scr,
    bias_land,
    made_sem,
    exp_sem,
    exp2_sem,
    load_sem,
    wo_sem,
    dh_sem,
    rs_send,
    rs_recv,
    z_send,
    z_recv,
    y_sem,
    x_send,
    x_recv,
    c_send,
    c_recv,
    small_send,
    small_recv,
    bias_send,
    bias_recv,
):
    h = pl.program_id(0)
    me = lax.axis_index("context")
    expert = lax.axis_index("expert")
    group = lax.axis_index("dp")
    near, across, far = flip(me, 1), flip(me, 2), flip(me, 3)
    high = me // 2
    feats = heads * HD
    hrow = pl.multiple_of(h * HD, HD)
    others = range(1, groups)

    def made_copy(k):
        return remote(
            made_ref.at[k],
            back_ref.at[k],
            made_sem.at[0, k],
            made_sem.at[1, k],
            expert=flip(expert, k),
        )

    made_own = pltpu.make_async_copy(made_ref.at[0], back_ref.at[0], made_sem.at[0, 0])
    load_in = pltpu.make_async_copy(gin_ref.at[:, high], gin_scr, load_sem.at[0])
    load_out = pltpu.make_async_copy(gout_ref.at[group], gout_scr, load_sem.at[1])

    def out_first(k):
        target = flip(group, k)
        return remote(
            gout_ref.at[target],
            gout_land.at[k],
            exp_sem.at[0, k],
            exp_sem.at[1, k],
            dp=target,
        )

    in_first = remote(
        gin_ref.at[:, 1 - high], gin_land, exp_sem.at[0, 0], exp_sem.at[1, 0], context=across
    )

    def in_second(k):
        target = flip(group, k)
        return remote(
            gin_scr.at[target],
            gin_far_ref.at[k - 1],
            exp2_sem.at[0, k],
            exp2_sem.at[1, k],
            dp=target,
        )

    out_second = remote(
        gout_scr.at[1 - high], gout_far_ref, exp2_sem.at[0, 0], exp2_sem.at[1, 0], context=across
    )
    wo_first = [
        remote(
            gwo_ref.at[slab],
            wo_near.at[i],
            wo_sem.at[0, i],
            wo_sem.at[1, i],
            context=near,
        )
        for i, slab in enumerate((near, far))
    ]
    wo_second = remote(wo_send, wo_far, wo_sem.at[0, 2], wo_sem.at[1, 2], context=across)
    dh_first = [
        remote(dh_scr.at[k], dh_near.at[i], dh_sem.at[0, i], dh_sem.at[1, i], context=near)
        for i, k in enumerate((1, 3))
    ]
    dh_second = remote(
        dh_scr.at[2], dh_far_ref, dh_sem.at[0, 2], dh_sem.at[1, 2], context=across
    )

    def scatter_copy(part, kd, ke):
        td, te = flip(group, kd), flip(expert, ke)
        index = kd * peers + ke
        return remote(
            shares.at[part, td, te],
            share_land.at[part, index],
            rs_send.at[part, index],
            rs_recv.at[part, index],
            dp=td,
            expert=te,
        )

    pairs = [(kd, ke) for ke in range(peers) for kd in range(groups) if kd or ke]

    def scatter(part, value):
        rows, width = value.shape[0] // peers, value.shape[1] // groups
        value = value.astype(BF16)
        for i in range(groups):
            for j in range(peers):
                shares[part, i, j] = value[
                    j * rows : (j + 1) * rows, i * width : (i + 1) * width
                ]
        for kd, ke in reversed(pairs):
            scatter_copy(part, kd, ke).start()

    def spread_copy(part, k):
        return remote(
            total_scr.at[part],
            sums_ref.at[part, group, me, expert],
            z_send.at[part, k],
            z_recv.at[part, k],
            expert=flip(expert, k),
        )

    def spread_own(part):
        return pltpu.make_async_copy(
            total_scr.at[part], sums_ref.at[part, group, me, expert], z_send.at[part, 0]
        )

    def collect(part):
        total = shares[part, group, expert].astype(F32)
        for kd, ke in pairs:
            scatter_copy(part, kd, ke).wait_recv()
            total = total + share_land[part, kd * peers + ke].astype(F32)
        total_scr[part] = total.astype(BF16)
        for k in reversed(range(1, peers)):
            spread_copy(part, k).start()
        spread_own(part).start()

    def y_copy(part):
        view = sums_ref.at[part, group, me]
        return remote(view, view, y_sem.at[0, part], y_sem.at[1, part], context=across)

    def x_copy(part, k, i):
        view = sums_ref.at[part, group, (me, across)[i]]
        return remote(
            view, view, x_send.at[part, k, i], x_recv.at[part, k, i], dp=flip(group, k)
        )

    def core_copy(part, k, i):
        view = sums_ref.at[part, flip(group, k), (me, across)[i]]
        return remote(view, view, c_send.at[part, k, i], c_recv.at[part, k, i], context=near)

    stages = [("dp", group, groups), ("expert", expert, peers), ("context", me, lay.spread)]
    offsets = [0, groups, groups + peers]

    def small_copies(stage, k):
        axis, index, _ = stages[stage]
        spot = offsets[stage] + k
        where = {axis: flip(index, k)}
        return (
            remote(
                small_scr.at[stage],
                small_land.at[spot],
                small_send.at[spot],
                small_recv.at[spot],
                **where,
            ),
            remote(
                bias_scr.at[stage],
                bias_land.at[spot],
                bias_send.at[spot],
                bias_recv.at[spot],
                **where,
            ),
        )

    def small_start(stage):
        for k in range(1, stages[stage][2]):
            for copy in small_copies(stage, k):
                copy.start()

    def small_sum(stage):
        small, bias = small_scr[stage], bias_scr[stage]
        for k in range(1, stages[stage][2]):
            for copy in small_copies(stage, k):
                copy.wait_recv()
            small = small + small_land[offsets[stage] + k]
            bias = bias + bias_land[offsets[stage] + k]
        return small, bias

    @pl.when(h == 0)
    def _():
        greet(
            [{"context": t} for t in (near, across, far)]
            + [{"dp": flip(group, kd), "expert": flip(expert, ke)} for kd, ke in pairs]
        )
        for copy in wo_first:
            copy.start()
        for k in others:
            out_first(k).start()
        in_first.start()
        load_in.start()
        load_out.start()
        for k in reversed(range(1, peers)):
            made_copy(k).start()
        made_own.start()
        bias_scr[0] = jnp.zeros_like(bias_scr[0])
        small_scr[0] = jnp.zeros_like(small_scr[0])
        small_scr[0, : gsmall_ref.shape[0]] = gsmall_ref[...]

    deltas = []
    for q in range(lay.blocks):
        cols = slice(q * BK, (q + 1) * BK)
        for c, start, at, size in lay.pieces[q]:
            where = q * BK + at
            dot_scr[:, where : where + size] = da_ref[c, pl.ds(hrow, HD), start : start + size]
        raw = dot_scr[:, cols].astype(F32)
        inverse = rl_ref[0, :, cols]
        deltas.append(
            inverse * jnp.sum(raw * ot_ref[pl.ds(hrow, HD), cols], axis=0, keepdims=True)
        )
        scaled = raw * inverse
        dot_scr[:, cols] = scaled.astype(BF16)
        do_scr[cols] = scaled.T.astype(BF16)
    krow = pl.multiple_of(feats + h * HD, HD)
    vrow = pl.multiple_of(2 * feats + h * HD, HD)
    for q in range(lay.blocks):
        cols = slice(q * BK, (q + 1) * BK)
        dq = 0.0
        for k in lay.keys[q]:
            t = lay.tile[(q, k)]
            rows = slice(k * BK, (k + 1) * BK)
            dp = dot(qkvn_ref[2 * heads + h, rows], dot_scr[:, cols])
            ds = (e_ref[0, t].astype(F32) * (dp - deltas[q])).astype(BF16)
            ds_scr[t] = ds
            dq = dq + dot(qkvt_ref[pl.ds(krow, HD), rows], ds)
        dt_scr[pl.ds(hrow, HD), cols] = (dq * HD**-0.5).astype(BF16)

    @pl.when(h == 1)
    def _():
        for copy in wo_first:
            copy.wait_recv()
        wo_send[...] = (gwo_ref[across].astype(F32) + wo_near[1].astype(F32)).astype(BF16)
        wo_second.start()

    for k in range(lay.blocks):
        rows = slice(k * BK, (k + 1) * BK)
        dk, dv = 0.0, 0.0
        for q in range(lay.blocks):
            if k in lay.keys[q]:
                t = lay.tile[(q, k)]
                cols = slice(q * BK, (q + 1) * BK)
                dk = dk + dot(ds_scr[t], qkvn_ref[h, cols])
                dv = dv + dot(e_ref[0, t], do_scr[cols])
        dt_scr[pl.ds(krow, HD), rows] = dk.T.astype(BF16)
        dt_scr[pl.ds(vrow, HD), rows] = dv.T.astype(BF16)

    @pl.when(h == heads - 1)
    def _():
        load_in.wait()
        load_out.wait()
        total = gout_scr[...].astype(F32)
        for k in others:
            out_first(k).wait_recv()
            total = total + gout_land[k].astype(F32)
        gout_scr[...] = total.astype(BF16)
        out_second.start()
        in_first.wait_recv()
        for k in others:
            target = flip(group, k)
            gin_scr[target] = (gin_scr[target].astype(F32) + gin_land[target].astype(F32)).astype(
                BF16
            )
            in_second(k).start()
        gin_own_ref[...] = gin_scr[group].astype(F32) + gin_land[group].astype(F32)
        gout_own_ref[...] = gout_scr[high].astype(F32)

    d_all = jnp.concatenate(
        [dt_scr[pl.ds(row, HD)] for row in (hrow, krow, vrow)], axis=0
    )
    grad = dot(d_all, h1_ref[...])
    for head in range(heads):

        @pl.when(h == head)
        def _():
            scatter(head, grad)

    column = lax.broadcasted_iota(jnp.int32, bias_scr.shape[1:], 1) == me * heads + h
    span = buckets_ref.shape[1]
    number = lax.broadcasted_iota(jnp.int32, (bias_scr.shape[1], span), 0)
    pieces = [jnp.zeros((1, BK), F32) for _ in range(lay.distances + 1)]
    for d in range(lay.distances):
        tile = 0.0
        for (q, k), t in lay.tile.items():
            if lay.distance(q, k) == d:
                tile = tile + ds_scr[t].astype(F32)
        sums = diagonal_sums(tile)
        pieces[d + 1] = pieces[d + 1] + sums[:, :BK]
        pieces[d] = pieces[d] + sums[:, BK:]
    by_distance = jnp.concatenate(pieces[1:], axis=1)
    summed = jnp.sum(
        jnp.where(buckets_ref[...] == number, by_distance, 0.0), axis=1, keepdims=True
    )
    bias_scr[0] += jnp.where(column, summed, 0.0)

    @pl.when(h == heads - 1)
    def _():
        small_start(0)
        half = lay.prompt_rows
        for k in (1, 3, 2, 0):
            c = flip(me, k)
            parts = [dt_scr[:, pl.ds(pl.multiple_of(c * half, 128), half)]]
            for j in range(lay.cont_count):
                first = lay.spread * (half + j * lay.cont_rows) + c * lay.cont_rows
                parts.append(dt_scr[:, pl.ds(pl.multiple_of(first, 128), lay.cont_rows)])
            block = jnp.concatenate(parts, axis=1).T
            dh_scr[k] = dot_nt(block, w_ref[...]).astype(BF16)
            if k == 1:
                dh_first[0].start()
            if k == 3:
                dh_first[1].start()
        wo_second.wait_recv()
        scatter(
            heads,
            gwo_ref[me].astype(F32) + wo_near[0].astype(F32) + wo_far[...].astype(F32),
        )
        for copy in dh_first:
            copy.wait_recv()
        dh_scr[2] = (dh_scr[2].astype(F32) + dh_near[1].astype(F32)).astype(BF16)
        dh_second.start()
        dh_ref[...] = dh_scr[0].astype(F32) + dh_near[0].astype(F32)
        small, bias = small_sum(0)
        small_scr[1], bias_scr[1] = small, bias
        small_start(1)
        for part in range(heads + 1):
            collect(part)
        small, bias = small_sum(1)
        small_scr[2], bias_scr[2] = small, bias
        small_start(2)
        for part in range(heads + 1):
            for k in range(1, peers):
                spread_copy(part, k).wait_recv()
            spread_own(part).wait()
            y_copy(part).start()
        for part in range(heads + 1):
            y_copy(part).wait_recv()
            for k in others:
                for i in range(2):
                    x_copy(part, k, i).start()
            for i in range(2):
                core_copy(part, 0, i).start()
        for part in range(heads + 1):
            for k in others:
                for i in range(2):
                    x_copy(part, k, i).wait_recv()
                    core_copy(part, k, i).start()
        small, bias = small_sum(2)
        small_ref[...] = small
        bias_ref[...] = bias
        for part in range(heads + 1):
            for k in range(groups):
                for i in range(2):
                    core_copy(part, k, i).wait()
            for k in others:
                for i in range(2):
                    x_copy(part, k, i).wait_send()
            y_copy(part).wait_send()
            for k in range(1, peers):
                spread_copy(part, k).wait_send()
            for kd, ke in pairs:
                scatter_copy(part, kd, ke).wait_send()
        for stage in range(3):
            for k in range(1, stages[stage][2]):
                for copy in small_copies(stage, k):
                    copy.wait_send()
        for copy in wo_first:
            copy.wait_send()
        wo_second.wait_send()
        for copy in dh_first:
            copy.wait_send()
        dh_second.wait()
        for k in others:
            out_first(k).wait_send()
            in_second(k).wait()
        in_first.wait_send()
        out_second.wait()
        made_own.wait()
        for k in range(1, peers):
            made_copy(k).wait()


def rear(lay, heads, groups, peers, *args):
    da, e, qkvn, qkvt, ot, rl, h1, w, buckets, gsmall, gwo, made, gin, gout = args
    width = h1.shape[1]
    feats = heads * HD
    in_rows, hidden = gin.shape[2:]
    out_rows = gout.shape[2]
    parts = heads + 1
    small_rows = -(-gsmall.shape[0] // 8) * 8
    rows, lanes = feats // peers, width // groups
    dma = pltpu.SemaphoreType.DMA
    anywhere = pl.BlockSpec(memory_space=pl.ANY)
    links = groups + peers + lay.spread

    def once(array):
        return pl.BlockSpec(
            array.shape, lambda h: (0,) * len(array.shape), pipeline_mode=pl.Buffered(1)
        )

    def result(shape, dtype):
        return jax.ShapeDtypeStruct(shape, dtype)

    kept = (
        result((lay.tokens, width), F32),
        result((in_rows, hidden), F32),
        result((out_rows, width), F32),
        result((small_rows, width), F32),
        result((BUCKETS, 128), F32),
    )
    return pl.pallas_call(
        functools.partial(rear_kernel, lay, heads, groups, peers),
        grid=(heads,),
        in_specs=[
            once(da),
            pl.BlockSpec((1, lay.tiles, BK, BK), lambda h: (h, 0, 0, 0)),
            once(qkvn),
            once(qkvt),
            once(ot),
            pl.BlockSpec((1, 1, lay.total), lambda h: (h, 0, 0)),
            once(h1),
            once(w),
            once(buckets),
            once(gsmall),
            once(gwo),
            anywhere,
            anywhere,
            anywhere,
        ],
        out_specs=tuple(once(k) for k in kept) + (anywhere,) * 5,
        out_shape=kept
        + (
            result(made.shape, BF16),
            result((max(groups - 1, 1), in_rows, hidden), BF16),
            result((out_rows, width), BF16),
            result((lay.tokens, width), BF16),
            result((parts, groups, lay.spread, peers, rows, lanes), BF16),
        ),
        scratch_shapes=[
            VMEM((lay.tiles, BK, BK), BF16),
            VMEM((HD, lay.total), BF16),
            VMEM((lay.total, HD), BF16),
            VMEM((3 * feats, lay.total), BF16),
            VMEM((4, lay.tokens, width), BF16),
            VMEM((2, lay.tokens, width), BF16),
            VMEM((groups, in_rows, hidden), BF16),
            VMEM((groups, in_rows, hidden), BF16),
            VMEM((2, out_rows, width), BF16),
            VMEM((groups, 2, out_rows, width), BF16),
            VMEM((2, feats, width), BF16),
            VMEM((feats, width), BF16),
            VMEM((feats, width), BF16),
            VMEM((parts, groups, peers, rows, lanes), BF16),
            VMEM((parts, groups * peers, rows, lanes), BF16),
            VMEM((parts, rows, lanes), BF16),
            VMEM((3, small_rows, width), F32),
            VMEM((links, small_rows, width), F32),
            VMEM((3, BUCKETS, 128), F32),
            VMEM((links, BUCKETS, 128), F32),
            dma((2, peers)),
            dma((2, groups)),
            dma((2, groups)),
            dma((2,)),
            dma((2, 3)),
            dma((2, 3)),
            dma((parts, groups * peers)),
            dma((parts, groups * peers)),
            dma((parts, peers)),
            dma((parts, peers)),
            dma((2, parts)),
            dma((parts, groups, 2)),
            dma((parts, groups, 2)),
            dma((parts, groups, 2)),
            dma((parts, groups, 2)),
            dma((links,)),
            dma((links,)),
            dma((links,)),
            dma((links,)),
        ],
        compiler_params=pltpu.CompilerParams(
            vmem_limit_bytes=63 * MIB, collective_id=2, has_side_effects=True
        ),
        name="rear",
    )(*args)


def finish_kernel(
    lay,
    heads,
    groups,
    peers,
    capacity,
    dh_ref,
    dh_far_ref,
    xp_ref,
    xc_ref,
    gain_ref,
    dmid_ref,
    mid_ref,
    cols_ref,
    gates_ref,
    made_ref,
    gin_ref,
    gin_far_ref,
    gout_ref,
    gout_far_ref,
    small_ref,
    bias_ref,
    sums_ref,
    wq_ref,
    wk_ref,
    wv_ref,
    outp_ref,
    outc_ref,
    dxp_ref,
    dxc_ref,
    ggain_ref,
    gq_ref,
    gk_ref,
    gv_ref,
    gwo_ref,
    gbias_ref,
    ggain2_ref,
    grouter_ref,
    gins_ref,
    gouts_ref,
    turn_scr,
):
    expert = lax.axis_index("expert")
    half = lay.prompt_rows
    tokens = lay.tokens
    feats = heads * HD
    out = mid_ref[...]
    for k in range(peers):
        base = (flip(expert, k) * capacity).astype(F32)
        number = lax.broadcasted_iota(jnp.int32, (tokens, capacity), 1).astype(F32) + base
        for i in range(2):
            pick = jnp.where(cols_ref[:, i : i + 1] == number, 1.0, 0.0).astype(BF16)
            out = out + gates_ref[:, i : i + 1] * dot(pick, made_ref[k])
    outp_ref[...] = out[:half].astype(BF16)
    outc_ref[...] = out[half:].astype(BF16)

    x = jnp.concatenate([xp_ref[...], xc_ref[...]], axis=0).astype(F32)
    dh1 = dh_ref[...] + dh_far_ref[...].astype(F32)
    r = lax.rsqrt(jnp.mean(x * x, axis=1, keepdims=True) + EPSILON)
    w = dh1 * gain_ref[...]
    mean = jnp.mean(w * x, axis=1, keepdims=True)
    dx = dmid_ref[...] + r * w - (r * r * r) * x * mean
    dxp_ref[...] = dx[:half]
    dxc_ref[...] = dx[half:]

    total = gin_ref[...]
    for k in range(groups - 1):
        total = total + gin_far_ref[k].astype(F32)
    gins_ref[...] = total
    gouts_ref[...] = gout_ref[...] + gout_far_ref[...].astype(F32)
    experts = grouter_ref.shape[1]
    ggain2_ref[...] = small_ref[0:1]
    pad = jnp.concatenate(
        [small_ref[...], jnp.zeros((128 - small_ref.shape[0], small_ref.shape[1]), F32)], axis=0
    )
    grouter_ref[...] = pad.T[:, 1 : 1 + experts]
    gbias_ref[...] = bias_ref[:, : gbias_ref.shape[1]]

    lanes = sums_ref.shape[5]
    gained = 0.0
    for n, (w_ref, g_ref) in enumerate(((wq_ref, gq_ref), (wk_ref, gk_ref), (wv_ref, gv_ref))):
        for c in range(lay.spread):
            for head in range(heads):
                to = c * feats + head * HD
                for i in range(groups):
                    block = sums_ref[head, i, c].reshape(feats, lanes)
                    turn_scr[to : to + HD, i * lanes : (i + 1) * lanes] = block[
                        n * HD : (n + 1) * HD
                    ]
        grad = turn_scr[...].T.astype(F32)
        g_ref[...] = grad
        gained = gained + jnp.sum(grad * w_ref[...].astype(F32), axis=1, keepdims=True)
    for c in range(lay.spread):
        for i in range(groups):
            gwo_ref[c * feats : (c + 1) * feats, i * lanes : (i + 1) * lanes] = (
                sums_ref[heads, i, c].reshape(feats, lanes).astype(F32)
            )
    gained = jnp.broadcast_to(gained, (gained.shape[0], 128)).T[0:1]
    ggain_ref[...] = gained / gain_ref[...]


def finish(lay, heads, groups, peers, capacity, experts, head_count, *args):
    width = args[2].shape[1]
    in_rows, hidden = args[10].shape
    out_rows = args[12].shape[0]

    def result(shape, dtype=F32):
        return jax.ShapeDtypeStruct(shape, dtype)

    rest = lay.tokens - lay.prompt_rows
    return pl.pallas_call(
        functools.partial(finish_kernel, lay, heads, groups, peers, capacity),
        out_shape=(
            result((lay.prompt_rows, width), BF16),
            result((rest, width), BF16),
            result((lay.prompt_rows, width)),
            result((rest, width)),
            result((1, width)),
            result((width, width)),
            result((width, width)),
            result((width, width)),
            result((width, width)),
            result((BUCKETS, head_count)),
            result((1, width)),
            result((width, experts)),
            result((in_rows, hidden)),
            result((out_rows, width)),
        ),
        scratch_shapes=[VMEM((width, width), BF16)],
        compiler_params=pltpu.CompilerParams(vmem_limit_bytes=60 * MIB),
        name="finish",
    )(*args)


def body(
    prompt_in,
    cont_in,
    prompt_route,
    cont_route,
    order,
    buckets,
    attn_gain,
    w_query,
    w_key,
    w_value,
    w_attn_out,
    rel_bias,
    ffn_gain,
    router,
    w_in,
    w_out,
    prompt_cot,
    cont_cot,
):
    prompt_rows = prompt_in.shape[1]
    cont_count = cont_in.shape[1]
    cont_rows = cont_in.shape[2]
    width = prompt_in.shape[2]
    spread = lax.axis_size("context")
    peers = lax.axis_size("expert")
    groups = lax.axis_size("dp")
    lay = Layout(spread, prompt_rows, cont_count, cont_rows)
    tokens = lay.tokens
    head_count = rel_bias.shape[1]
    heads = head_count // spread
    experts = peers * w_in.shape[0]
    capacity = 9 * tokens * 2 // (8 * experts)
    rest = cont_count * cont_rows
    gain_one = attn_gain.reshape(1, width)
    gain_two = ffn_gain.reshape(1, width)
    xp, xc = prompt_in.reshape(prompt_rows, width), cont_in.reshape(rest, width)
    zp, zc = prompt_cot.reshape(prompt_rows, width), cont_cot.reshape(rest, width)
    bucket_row = buckets.reshape(1, -1)
    h1, qkvn, qkvt, e, ot, rl, weights, cols, rows, at, dz_slots = front(
        lay,
        heads,
        peers,
        capacity,
        xp,
        xc,
        prompt_route.reshape(prompt_rows, 2),
        cont_route.reshape(rest, 2),
        order.reshape(1, tokens),
        bucket_row,
        gain_one,
        w_query,
        w_key,
        w_value,
        rel_bias,
        zp,
        zc,
    )
    pairs = groups * spread // 2
    mid, gates, dmid, g_wo, g_small, made, g_in, g_out, dattn_t = experts_layer(
        peers,
        pairs,
        spread,
        capacity,
        at.reshape(width, tokens),
        xp,
        xc,
        w_attn_out,
        gain_two,
        router,
        cols,
        rows,
        zp,
        zc,
        w_in,
        w_out,
        dz_slots,
    )
    dh, gin_own, gout_own, small, bias, made, gin_far, gout_far, dh_far, sums = rear(
        lay,
        heads,
        groups,
        peers,
        dattn_t,
        e,
        qkvn,
        qkvt,
        ot,
        rl,
        h1,
        weights,
        bucket_row,
        g_small,
        g_wo.reshape(spread, width // spread, width),
        made,
        g_in.reshape(groups, 2, *g_in.shape[1:]),
        g_out.reshape(groups, 2, *g_out.shape[1:]),
    )
    outs = finish(
        lay,
        heads,
        groups,
        peers,
        capacity,
        experts,
        head_count,
        dh,
        dh_far,
        xp,
        xc,
        gain_one,
        dmid,
        mid,
        cols,
        gates,
        made,
        gin_own,
        gin_far,
        gout_own,
        gout_far,
        small,
        bias,
        sums,
        w_query,
        w_key,
        w_value,
    )
    outp, outc, dxp, dxc, g_gain, g_q, g_k, g_v, g_wo, g_bias, g_gain2, g_router, g_in, g_out = outs
    return (
        outp[None],
        outc.reshape(1, cont_count, cont_rows, width),
        dxp[None],
        dxc.reshape(1, cont_count, cont_rows, width),
        g_gain.reshape(width),
        g_q,
        g_k,
        g_v,
        g_wo,
        g_bias,
        g_gain2.reshape(width),
        g_router,
        g_in[None],
        g_out[None],
    )


def solution(mesh):
    split = P(("dp", "expert"), "context", None)
    split_cont = P(("dp", "expert"), None, "context", None)
    whole = P()
    expert = P("expert", None, None)
    grad = P("expert", ("dp", "context"), None)
    return jax.shard_map(
        body,
        mesh=mesh,
        in_specs=(split, split_cont, split, split_cont, split)
        + (whole,) * 9
        + (expert, expert, split, split_cont),
        out_specs=(split, split_cont, split, split_cont) + (whole,) * 8 + (grad, grad),
        check_vma=False,
    )
```

```python
import functools

import jax
import jax.numpy as jnp
from jax import lax
from jax.experimental import pallas as pl
from jax.experimental.pallas import tpu as pltpu
from jax.sharding import PartitionSpec as P

HD = 64
BK = 256
BUCKETS = 32
EPSILON = 1e-06
MASKED = -1e30
F32 = jnp.float32
BF16 = jnp.bfloat16
VMEM = pltpu.VMEM
MESH = pl.DeviceIdType.MESH
MIB = 1 << 20


def dot(a, b):
    return lax.dot_general(a, b, (((1,), (0,)), ((), ())), preferred_element_type=F32)


def dot_nt(a, b):
    return lax.dot_general(a, b, (((1,), (1,)), ((), ())), preferred_element_type=F32)


def dot_tn(a, b):
    return lax.dot_general(a, b, (((0,), (0,)), ((), ())), preferred_element_type=F32)


def split_dot(a, b, op):
    high = a.astype(BF16)
    low = (a - high.astype(F32)).astype(BF16)
    return op(high, b) + op(low, b)


def full(shape):
    return pl.BlockSpec(shape, lambda *_: (0,) * len(shape))


class Layout:
    def __init__(self, spread, prompt_rows, cont_count, cont_rows):
        assert prompt_rows == BK and BK % cont_rows == 0
        self.spread = spread
        self.prompt_rows = prompt_rows
        self.cont_count = cont_count
        self.cont_rows = cont_rows
        self.tokens = prompt_rows + cont_count * cont_rows
        self.per_cont = spread * cont_rows // BK
        self.blocks = spread + cont_count * self.per_cont
        self.total = self.blocks * BK
        self.keys, self.place, self.pieces = [], [], []
        for p in range(spread):
            self.keys.append(list(range(p + 1)))
            self.place.append(p)
            self.pieces.append([(p, 0, 0, BK)])
        each = BK // cont_rows
        for j in range(cont_count):
            for m in range(self.per_cont):
                first = spread + j * self.per_cont
                self.keys.append(list(range(spread)) + list(range(first, first + m + 1)))
                self.place.append(spread + m)
                self.pieces.append(
                    [
                        (m * each + n, prompt_rows + j * cont_rows, n * cont_rows, cont_rows)
                        for n in range(each)
                    ]
                )
        self.tile = {}
        for q in range(self.blocks):
            for k in self.keys[q]:
                self.tile[(q, k)] = len(self.tile)
        self.tiles = len(self.tile)
        self.distances = spread + self.per_cont

    def distance(self, q, k):
        return self.place[q] - self.place[k]


def flip(index, mask):
    bit = 1
    while bit <= mask:
        if mask & bit:
            index = index + bit * (1 - 2 * ((index // bit) % 2))
        bit *= 2
    return index


def remote(src, dst, send, recv, **where):
    return pltpu.make_async_remote_copy(
        src_ref=src,
        dst_ref=dst,
        send_sem=send,
        recv_sem=recv,
        device_id=where,
        device_id_type=MESH,
    )


def greet(partners):
    barrier = pltpu.get_barrier_semaphore()
    for where in partners:
        pl.semaphore_signal(barrier, inc=1, device_id=where, device_id_type=MESH)
    pl.semaphore_wait(barrier, len(partners))


def make_plan(capacity, routes, order_row):
    tokens = routes.shape[0]
    side = (tokens, tokens)
    lane = lax.broadcasted_iota(jnp.int32, side, 1).astype(F32)
    sub = lax.broadcasted_iota(jnp.int32, side, 0)
    rank_col = jnp.sum(jnp.where(order_row == sub, lane, 0.0), axis=1, keepdims=True)
    rank_row = jnp.broadcast_to(rank_col, (tokens, 128)).T[0:1]
    before = jnp.where(rank_row < rank_col, 1.0, 0.0).astype(BF16)
    expert_lane = lax.broadcasted_iota(jnp.int32, (tokens, 128), 1).astype(F32)
    hots = [jnp.where(routes[:, i : i + 1] == expert_lane, 1.0, 0.0) for i in range(2)]
    counts = [dot(before, hot.astype(BF16)) for hot in hots]
    counts[1] = counts[1] + jnp.sum(hots[0], axis=0, keepdims=True)
    cols = jnp.zeros((tokens, 128), F32)
    for i in range(2):
        pos = jnp.sum(hots[i] * counts[i], axis=1, keepdims=True)
        route = routes[:, i : i + 1]
        slot = jnp.where(pos < capacity, route * capacity + pos, -1.0)
        cols = jnp.where(expert_lane == i, slot, cols)
        cols = jnp.where(expert_lane == 2 + i, route, cols)
    return cols, cols.T[0:8], hots


def toeplitz_tile(table_row, d):
    line = jnp.concatenate(
        [table_row[:, (d + 1) * BK : (d + 2) * BK], table_row[:, d * BK : (d + 1) * BK]], axis=1
    )
    tile = jnp.broadcast_to(line, (8, 2 * BK))
    row = lax.broadcasted_iota(jnp.int32, (8, 2 * BK), 0)
    for bit in (1, 2, 4):
        tile = jnp.where((row & bit) > 0, pltpu.roll(tile, bit, 1), tile)
    height = 8
    while height < BK:
        tile = jnp.concatenate([tile, pltpu.roll(tile, height, 1)], axis=0)
        height *= 2
    tile = tile[:, :BK]
    if d == 0:
        key = lax.broadcasted_iota(jnp.int32, (BK, BK), 0)
        query = lax.broadcasted_iota(jnp.int32, (BK, BK), 1)
        tile = jnp.where(query >= key, tile, MASKED)
    return tile


def diagonal_sums(tile):
    tile = jnp.concatenate([tile, jnp.zeros((BK, BK), F32)], axis=1)
    height = BK
    while height > 8:
        height //= 2
        tile = tile[:height] + pltpu.roll(tile[height:], 2 * BK - height, 1)
    row = lax.broadcasted_iota(jnp.int32, (8, 2 * BK), 0)
    for bit in (1, 2, 4):
        tile = jnp.where((row & bit) > 0, pltpu.roll(tile, 2 * BK - bit, 1), tile)
    return jnp.sum(tile, axis=0, keepdims=True)


def front_kernel(
    lay,
    heads,
    peers,
    capacity,
    xp_ref,
    xc_ref,
    rp_ref,
    rc_ref,
    order_ref,
    buckets_ref,
    gain_ref,
    wq_ref,
    wk_ref,
    wv_ref,
    bias_ref,
    zp_ref,
    zc_ref,
    h1_ref,
    qkvn_ref,
    qkvt_ref,
    e_ref,
    ot_ref,
    rl_ref,
    w_ref,
    cols_ref,
    rows_ref,
    at_ref,
    dz_ref,
    x_all,
    at_scr,
    dz_scr,
    s_scr,
    bias_scr,
    x_send,
    x_recv,
    a_send,
    a_recv,
    z_send,
    z_recv,
    own_sem,
):
    h = pl.program_id(0)
    me = lax.axis_index("context")
    expert = lax.axis_index("expert")
    feats = heads * HD
    half = lay.prompt_rows
    near, across, far = flip(me, 1), flip(me, 2), flip(me, 3)
    width = gain_ref.shape[0]
    gain = gain_ref[...].reshape(1, width)

    def x_copy(slot, part, index, target):
        view = x_all.at[slot, pl.ds(part * half, half)]
        return remote(view, view, x_send.at[index], x_recv.at[index], context=target)

    def z_copy(k):
        return remote(
            dz_scr.at[k], dz_ref.at[k], z_send.at[k], z_recv.at[k], expert=flip(expert, k)
        )

    def a_copy(k, head):
        target = flip(me, k)
        src = at_scr.at[target, pl.ds(head * HD, HD)]
        dst = at_ref.at[me, pl.ds(head * HD, HD)]
        return remote(src, dst, a_send.at[head, k], a_recv.at[head, k], context=target)

    def a_own(head):
        return pltpu.make_async_copy(
            at_scr.at[me, pl.ds(head * HD, HD)],
            at_ref.at[me, pl.ds(head * HD, HD)],
            a_send.at[head, 0],
        )

    z_own = pltpu.make_async_copy(dz_scr.at[0], dz_ref.at[0], own_sem)

    def project(slot):
        x = x_all[slot].astype(F32)
        r = lax.rsqrt(jnp.mean(x * x, axis=1, keepdims=True) + EPSILON)
        normed = (x * r * gain).astype(BF16)
        y = dot(normed, w_ref[...])
        scale = jnp.where(lax.broadcasted_iota(jnp.int32, y.shape, 1) < feats, HD**-0.5, 1.0)
        y = (y.astype(BF16).astype(F32) * scale).astype(BF16)
        yt = y.T
        spots = [(0, pl.multiple_of(slot * half, 128), half)]
        for j in range(lay.cont_count):
            first = lay.spread * half + j * lay.spread * lay.cont_rows
            spots.append(
                (
                    half + j * lay.cont_rows,
                    pl.multiple_of(first + slot * lay.cont_rows, 128),
                    lay.cont_rows,
                )
            )
        for start, to, size in spots:
            h1_ref[pl.ds(to, size)] = normed[start : start + size]
            qkvt_ref[:, pl.ds(to, size)] = yt[:, start : start + size]
            for i in range(3 * heads):
                qkvn_ref[i, pl.ds(to, size)] = y[start : start + size, i * HD : (i + 1) * HD]

    @pl.when(h == 0)
    def _():
        greet(
            [{"context": t} for t in (near, across, far)]
            + [{"expert": flip(expert, k)} for k in range(1, peers)]
        )
        x_all[me, :half] = xp_ref[...]
        x_all[me, half:] = xc_ref[...]
        for part in range(2):
            x_copy(me, part, part, across).start()
        for part in range(2):
            x_copy(me, part, 2 + part, near).start()
        tokens = lay.tokens
        routes = jnp.concatenate(
            [rp_ref[...]] + [rc_ref[j] for j in range(lay.cont_count)], axis=1
        ).astype(F32)
        routes = jnp.concatenate([routes, jnp.zeros((126, tokens), F32)], axis=0).T
        cols, rows, hots = make_plan(capacity, routes, order_ref[...])
        cols_ref[...] = cols
        rows_ref[...] = rows
        dz = jnp.concatenate([zp_ref[...], zc_ref[...]], axis=0)
        for k in list(range(1, peers)) + [0]:
            base = flip(expert, k) * capacity
            number = (lax.broadcasted_iota(jnp.int32, (capacity, tokens), 0) + base).astype(F32)
            first = jnp.where(rows[0:1] == number, 1.0, 0.0)
            second = jnp.where(rows[1:2] == number, 1.0, 0.0)
            dz_scr[k, :, :width] = dot((first + second).astype(BF16), dz).astype(BF16)
            other = dot(first.astype(BF16), hots[1].astype(BF16))
            other = other + dot(second.astype(BF16), hots[0].astype(BF16))
            dz_scr[k, :, width:] = other.astype(BF16)
            if k:
                z_copy(k).start()
            else:
                z_own.start()
        for c in range(lay.spread):

            @pl.when(me == c)
            def _():
                for i, ref in enumerate((wq_ref, wk_ref, wv_ref)):
                    w_ref[:, i * feats : (i + 1) * feats] = ref[:, c * feats : (c + 1) * feats]

        project(me)
        for part in range(2):
            x_copy(near, part, 2 + part, near).wait_recv()
        project(near)
        for part in range(2):
            x_copy(across, part, part, across).wait_recv()
            x_copy(across, part, 4 + part, near).start()
        project(across)
        for part in range(2):
            x_copy(far, part, 4 + part, near).wait_recv()
        project(far)
        for part in range(2):
            x_copy(me, part, part, across).wait_send()
            x_copy(me, part, 2 + part, near).wait_send()
            x_copy(across, part, 4 + part, near).wait_send()

    pick = lax.broadcasted_iota(jnp.int32, bias_ref.shape, 0) == me * heads + h
    bias_row = jnp.sum(jnp.where(pick, bias_ref[...], 0.0), axis=0, keepdims=True)
    bias_row = jnp.concatenate([bias_row, jnp.zeros((1, 128 - BUCKETS), F32)], axis=1)
    column = jnp.broadcast_to(bias_row, (128, 128)).T[:BUCKETS, 0:1]
    span = buckets_ref.shape[0]
    number = lax.broadcasted_iota(jnp.int32, (BUCKETS, span), 0)
    table_row = jnp.sum(
        jnp.where(buckets_ref[...].reshape(1, span) == number, column, 0.0), axis=0, keepdims=True
    )
    table_row = jnp.concatenate([jnp.zeros((1, BK), F32), table_row], axis=1)
    for d in range(lay.distances):
        bias_scr[d] = toeplitz_tile(table_row, d)
    hrow = pl.multiple_of(h * HD, HD)
    vrow = pl.multiple_of(2 * feats + h * HD, HD)
    for q in range(lay.blocks):
        qt = qkvt_ref[pl.ds(hrow, HD), q * BK : (q + 1) * BK]
        top = None
        for n, k in enumerate(lay.keys[q]):
            s = dot(qkvn_ref[heads + h, k * BK : (k + 1) * BK], qt) + bias_scr[lay.distance(q, k)]
            s_scr[n] = s
            m = jnp.max(s, axis=0, keepdims=True)
            top = m if top is None else jnp.maximum(top, m)
        total, out = 0.0, 0.0
        for n, k in enumerate(lay.keys[q]):
            e = jnp.exp(s_scr[n] - top)
            total = total + jnp.sum(e, axis=0, keepdims=True)
            e = e.astype(BF16)
            e_ref[0, lay.tile[(q, k)]] = e
            out = out + dot(qkvt_ref[pl.ds(vrow, HD), k * BK : (k + 1) * BK], e)
        inverse = 1.0 / total
        rl_ref[0, :, q * BK : (q + 1) * BK] = inverse
        out = out * inverse
        ot_ref[pl.ds(hrow, HD), q * BK : (q + 1) * BK] = out
        for c, start, at, size in lay.pieces[q]:
            at_scr[c, pl.ds(hrow, HD), start : start + size] = out[:, at : at + size].astype(BF16)

    for k in (3, 2, 1):
        a_copy(k, h).start()
    a_own(h).start()

    @pl.when(h == heads - 1)
    def _():
        for head in range(heads):
            a_own(head).wait()
            for k in (1, 2, 3):
                a_copy(k, head).wait()
        z_own.wait()
        for k in range(1, peers):
            z_copy(k).wait()


def front(lay, heads, peers, capacity, *args):
    width = args[0].shape[1]
    feats = heads * HD
    dma = pltpu.SemaphoreType.DMA
    anywhere = pl.BlockSpec(memory_space=pl.ANY)
    return pl.pallas_call(
        functools.partial(front_kernel, lay, heads, peers, capacity),
        grid=(heads,),
        in_specs=[full(a.shape) for a in args],
        out_specs=(
            full((lay.total, width)),
            full((3 * heads, lay.total, HD)),
            full((3 * feats, lay.total)),
            pl.BlockSpec((1, lay.tiles, BK, BK), lambda h: (h, 0, 0, 0)),
            full((feats, lay.total)),
            pl.BlockSpec((1, 1, lay.total), lambda h: (h, 0, 0)),
            full((width, 3 * feats)),
            full((lay.tokens, 128)),
            full((8, lay.tokens)),
            anywhere,
            anywhere,
        ),
        out_shape=(
            jax.ShapeDtypeStruct((lay.total, width), BF16),
            jax.ShapeDtypeStruct((3 * heads, lay.total, HD), BF16),
            jax.ShapeDtypeStruct((3 * feats, lay.total), BF16),
            jax.ShapeDtypeStruct((heads, lay.tiles, BK, BK), BF16),
            jax.ShapeDtypeStruct((feats, lay.total), F32),
            jax.ShapeDtypeStruct((heads, 1, lay.total), F32),
            jax.ShapeDtypeStruct((width, 3 * feats), BF16),
            jax.ShapeDtypeStruct((lay.tokens, 128), F32),
            jax.ShapeDtypeStruct((8, lay.tokens), F32),
            jax.ShapeDtypeStruct((lay.spread, feats, lay.tokens), BF16),
            jax.ShapeDtypeStruct((peers, capacity, width + 128), BF16),
        ),
        scratch_shapes=[
            VMEM((lay.spread, lay.tokens, width), BF16),
            VMEM((lay.spread, feats, lay.tokens), BF16),
            VMEM((peers, capacity, width + 128), BF16),
            VMEM((max(len(k) for k in lay.keys), BK, BK), F32),
            VMEM((lay.distances, BK, BK), F32),
            dma((6,)),
            dma((6,)),
            dma((heads, 4)),
            dma((heads, 4)),
            dma((peers,)),
            dma((peers,)),
            dma,
        ],
        compiler_params=pltpu.CompilerParams(
            vmem_limit_bytes=60 * MIB, collective_id=0, has_side_effects=True
        ),
        name="front",
    )(*args)


def gelu_parts(u):
    slope = 0.7978845608028654
    cube = 0.044715
    square = u * u
    t = jnp.tanh(slope * u * (1.0 + cube * square))
    half = 0.5 * (1.0 + t)
    value = u * half
    grad = half + 0.5 * u * (1.0 - t * t) * (slope * (1.0 + 3.0 * cube * square))
    return value, grad


def turn_index(index, mask, size):
    bit = 1
    while bit < size:
        index = index + ((mask // bit) % 2) * bit * (1 - 2 * ((index // bit) % 2))
        bit *= 2
    return index


def experts_kernel(
    peers,
    pairs,
    capacity,
    at_ref,
    xp_ref,
    xc_ref,
    wo_ref,
    gain_ref,
    router_ref,
    cols_ref,
    rows_ref,
    zp_ref,
    zc_ref,
    w_in_ref,
    w_out_ref,
    dz_ref,
    mid_ref,
    gates_ref,
    dmid_ref,
    gwo_ref,
    gsmall_ref,
    made_ref,
    gin_ref,
    ginr_ref,
    gout_ref,
    goutr_ref,
    da_ref,
    w_in,
    w_out,
    dz,
    sent,
    arrived,
    act_scr,
    dpre_scr,
    dsent,
    back,
    share,
    share_back,
    h2_scr,
    gin,
    gout,
    gin_near,
    gout_near,
    gin_y,
    gin_x,
    gout_y,
    gout_x,
    load_sem,
    s_send,
    s_recv,
    r_send,
    r_recv,
    h_send,
    h_recv,
    p_send,
    p_recv,
    q_send,
    q_recv,
    d_send,
    d_recv,
    out_sem,
):
    me = lax.axis_index("context")
    expert = lax.axis_index("expert")
    core = me % 2
    near = flip(me, 1)
    tokens = cols_ref.shape[0]
    width = gain_ref.shape[0]
    gain = gain_ref[...].reshape(1, width)
    hidden = w_in_ref.shape[2]
    lanes = share.shape[2]
    chunk = 512
    loads = [
        pltpu.make_async_copy(dz_ref, dz, load_sem.at[0]),
        pltpu.make_async_copy(w_in_ref.at[0], w_in, load_sem.at[1]),
        pltpu.make_async_copy(w_out_ref.at[0], w_out, load_sem.at[2]),
    ]
    for copy in loads:
        copy.start()
    greet(
        [{"context": flip(me, k)} for k in (1, 2, 3)]
        + [{"expert": flip(expert, k)} for k in range(1, peers)]
        + [{"dp": flip(lax.axis_index("dp"), k)} for k in range(1, pairs // 2)]
    )

    def to_peer(k, src, dst, send, recv):
        target = turn_index(expert, k, peers)
        return remote(src.at[k], dst.at[k], send.at[k], recv.at[k], expert=target)

    def dispatch(k):
        return to_peer(k, sent, arrived, s_send, s_recv)

    def returns(k):
        return (
            to_peer(k, dsent, back, r_send, r_recv),
            to_peer(k, share, share_back, h_send, h_recv),
        )

    mid = jnp.concatenate([xp_ref[...], xc_ref[...]], axis=0).astype(F32)
    mid = mid + dot_tn(at_ref[...], wo_ref[...])
    mid_ref[...] = mid
    r = lax.rsqrt(jnp.mean(mid * mid, axis=1, keepdims=True) + EPSILON)
    h2_scr[...] = (mid * r * gain).astype(BF16)
    for k in list(range(1, peers)) + [0]:
        base = flip(expert, k) * capacity
        number = (lax.broadcasted_iota(jnp.int32, (capacity, tokens), 0) + base).astype(F32)
        pick = (rows_ref[0:1] == number) | (rows_ref[1:2] == number)
        block = dot(jnp.where(pick, 1.0, 0.0).astype(BF16), h2_scr[...]).astype(BF16)
        if k:
            sent[k] = block
            dispatch(k).start()
        else:
            arrived[0] = block
    logits = dot_nt(h2_scr[...], router_ref[...])
    lane = lax.broadcasted_iota(jnp.int32, logits.shape, 1).astype(F32)
    hots = [cols_ref[:, 2 + i : 3 + i] == lane for i in range(2)]
    chosen = [jnp.sum(jnp.where(hot, logits, 0.0), axis=1, keepdims=True) for hot in hots]
    most = jnp.maximum(chosen[0], chosen[1])
    parts = [jnp.exp(c - most) for c in chosen]
    inverse = 1.0 / (parts[0] + parts[1])
    gates = [p * inverse for p in parts]
    wide = lax.broadcasted_iota(jnp.int32, (tokens, 128), 1)
    gates_ref[...] = jnp.where(wide == 0, gates[0], jnp.where(wide == 1, gates[1], 0.0))
    for copy in loads:
        copy.wait()

    def process(k):
        rows = arrived[k]
        scores = dot_nt(rows, router_ref[...])
        elane = lax.broadcasted_iota(jnp.int32, scores.shape, 1)
        own = jnp.sum(jnp.where(elane == expert, scores, 0.0), axis=1, keepdims=True)
        other_hot = dz[k, :, width : width + scores.shape[1]].astype(F32)
        other = jnp.sum(other_hot * scores, axis=1, keepdims=True)
        gate = 1.0 / (1.0 + jnp.exp(other - own))
        dmade = (gate * dz[k, :, :width].astype(F32)).astype(BF16)
        dz[k, :, :width] = dmade
        where = pl.ds(pl.multiple_of(k * capacity, 16), capacity)
        total, part = 0.0, 0.0
        for f in range(0, hidden, chunk):
            pre = dot(rows, w_in[:, f : f + chunk])
            dact = dot_nt(dmade, w_out[f : f + chunk])
            value, grad = gelu_parts(pre)
            act = value.astype(BF16)
            act_scr[where, f : f + chunk] = act
            dpre = (dact * grad).astype(BF16)
            dpre_scr[where, f : f + chunk] = dpre
            product = act.astype(F32) * dact
            for i in range(0, chunk, 128):
                part = part + product[:, i : i + 128]
            total = total + dot_nt(dpre, w_in[:, f : f + chunk])
        dsent[k] = total.astype(BF16)
        column = jnp.broadcast_to(jnp.sum(part, axis=1, keepdims=True), (capacity, 128))
        column = jnp.concatenate([column, jnp.zeros((lanes - capacity, 128), F32)], axis=0)
        share[k] = column.T[:8]

    process(0)

    @pl.loop(1, peers)
    def _(k):
        dispatch(k).wait_recv()
        process(k)
        for copy in returns(k):
            copy.start()

    @pl.loop(1, peers)
    def _(k):
        dispatch(k).wait_send()

    def near_copies(pair):
        return (
            remote(
                gout.at[pair, 1 - core],
                gout_near.at[pair],
                p_send.at[0, pair],
                p_recv.at[0, pair],
                context=near,
            ),
            remote(
                gin.at[pair, 1 - core],
                gin_near.at[pair],
                p_send.at[1, pair],
                p_recv.at[1, pair],
                context=near,
            ),
        )

    slots = peers * capacity
    out_rows, in_rows = gout.shape[2], gin.shape[2]
    group = lax.axis_index("dp")
    high = me // 2
    across = flip(me, 2)
    groups = pairs // 2

    totals = ((gin, gin_y, gin_x, hidden // 2), (gout, gout_y, gout_x, width // 2))

    def y_first(n, i):
        total, land, _, half = totals[n]
        return remote(
            total.at[2 * i + 1 - high, core, :, pl.ds(0, half)],
            land.at[i],
            q_send.at[n, 0, i],
            q_recv.at[n, 0, i],
            context=across,
        )

    def x_first(n, k, y):
        total, _, land, half = totals[n]
        target = flip(group, k)
        return remote(
            total.at[2 * target + y, core, :, pl.ds(half, half)],
            land.at[k - 1, y],
            q_send.at[n, 1 + y, k],
            q_recv.at[n, 1 + y, k],
            dp=target,
        )

    def first_copies(n):
        copies = [y_first(n, i) for i in range(groups)]
        return copies + [x_first(n, k, y) for k in range(1, groups) for y in range(2)]

    dmade_all = dz[:, :, :width].reshape(slots, width)
    for pair in range(pairs):
        left = arrived[:, :, 2 * pair * in_rows : 2 * (pair + 1) * in_rows]
        left = left.reshape(slots, 2 * in_rows)
        for f in range(0, hidden, 2 * chunk):
            grad = dot_tn(left, dpre_scr[:, f : f + 2 * chunk]).astype(BF16)
            gin[pair, 0, :, f : f + 2 * chunk] = grad[:in_rows]
            gin[pair, 1, :, f : f + 2 * chunk] = grad[in_rows:]
        near_copies(pair)[1].start()
    for pair in range(pairs):
        left = act_scr[:, 2 * pair * out_rows : 2 * (pair + 1) * out_rows]
        grad = dot_tn(left, dmade_all).astype(BF16)
        gout[pair, 0] = grad[:out_rows]
        gout[pair, 1] = grad[out_rows:]
        near_copies(pair)[0].start()
    for pair in range(pairs):
        near_copies(pair)[1].wait_recv()
        gin[pair, core] = (gin[pair, core].astype(F32) + gin_near[pair].astype(F32)).astype(BF16)
    for copy in first_copies(0):
        copy.start()

    @pl.loop(0, peers)
    def _(k):
        where = pl.ds(pl.multiple_of(k * capacity, 16), capacity)
        sent[k] = dot(act_scr[where], w_out[...]).astype(BF16)

    made_copy = pltpu.make_async_copy(sent, made_ref, load_sem.at[0])
    made_copy.start()
    for pair in range(pairs):
        near_copies(pair)[0].wait_recv()
        gout[pair, core] = (gout[pair, core].astype(F32) + gout_near[pair].astype(F32)).astype(BF16)
    for copy in first_copies(1):
        copy.start()

    dmid_ref[...] = jnp.zeros_like(dmid_ref)

    def collect(k, shares, block, share_row):
        base = (turn_index(expert, k, peers) * capacity).astype(F32)
        number = lax.broadcasted_iota(jnp.int32, (tokens, lanes), 1).astype(F32) + base
        picks = [cols_ref[:, i : i + 1] == number for i in range(2)]
        both = jnp.where(picks[0] | picks[1], 1.0, 0.0)[:, :capacity].astype(BF16)
        dmid_ref[...] += dot(both, block)
        return tuple(
            shares[i] + jnp.sum(jnp.where(picks[i], share_row, 0.0), axis=1, keepdims=True)
            for i in range(2)
        )

    zero = jnp.zeros((tokens, 1), F32)
    shares = collect(0, (zero, zero), dsent[0], share[0, 0:1])

    def gather_step(k, shares):
        for copy in returns(k):
            copy.wait()
        return collect(k, shares, back[k], share_back[k, 0:1])

    shares = lax.fori_loop(1, peers, gather_step, shares)
    total = shares[0] + shares[1]
    dchosen = [shares[i] - gates_ref[:, i : i + 1] * total for i in range(2)]
    elane = lax.broadcasted_iota(jnp.int32, (tokens, router_ref.shape[0]), 1).astype(F32)
    dlogits = sum(
        jnp.where(cols_ref[:, 2 + i : 3 + i] == elane, dchosen[i], 0.0) for i in range(2)
    )
    dh2 = dmid_ref[...] + split_dot(dlogits, router_ref[...], dot)
    mid = mid_ref[...]
    r = lax.rsqrt(jnp.mean(mid * mid, axis=1, keepdims=True) + EPSILON)
    u = dh2 * gain
    mean = jnp.mean(u * mid, axis=1, keepdims=True)
    cot = jnp.concatenate([zp_ref[...], zc_ref[...]], axis=0).astype(F32)
    dmid = cot + r * u - (r * r * r) * mid * mean
    dmid_ref[...] = dmid
    branch = dmid.astype(BF16)
    feats = da_ref.shape[1]

    def da_view(k):
        return act_scr.at[pl.ds(k * feats, feats), pl.ds(0, tokens)]

    def da_copy(k):
        target = flip(me, k)
        return remote(
            da_view(k), da_ref.at[me], d_send.at[k], d_recv.at[k], context=target
        )

    da_own = pltpu.make_async_copy(da_view(0), da_ref.at[me], d_send.at[0])
    for k in (3, 2, 1, 0):
        first = pl.multiple_of(flip(me, k) * feats, 64)
        block = dot_nt(wo_ref[pl.ds(first, feats)], branch).astype(BF16)
        act_scr[k * feats : (k + 1) * feats, :tokens] = block
        if k:
            da_copy(k).start()
        else:
            da_own.start()
    gsmall_ref[0:1] = jnp.sum(dh2 * mid * r, axis=0, keepdims=True)
    gsmall_ref[1:] = split_dot(dlogits, h2_scr[...], dot_tn)
    columns = slice(tokens, tokens + width)
    act_scr[:width, columns] = dot(at_ref[...], branch).astype(BF16)
    gwo_copy = pltpu.make_async_copy(
        act_scr.at[pl.ds(0, width), pl.ds(tokens, width)], gwo_ref, out_sem.at[0]
    )
    gwo_copy.start()
    stores = []
    for n, (left_ref, right_ref) in enumerate(((gin_ref, ginr_ref), (gout_ref, goutr_ref))):
        total, y_land, x_land, size = totals[n]
        left, right = pl.ds(0, size), pl.ds(size, size)
        for i in range(groups):
            y_first(n, i).wait_recv()
            own = total.at[2 * i + high, core, :, left]
            own[...] = (own[...].astype(F32) + y_land[i].astype(F32)).astype(BF16)
            stores.append(
                pltpu.make_async_copy(own, left_ref.at[i], out_sem.at[1 + len(stores)])
            )
            stores[-1].start()
        for y in range(2):
            own = total.at[2 * group + y, core, :, right]
            value = own[...].astype(F32)
            for k in range(1, groups):
                x_first(n, k, y).wait_recv()
                value = value + x_land[k - 1, y].astype(F32)
            own[...] = value.astype(BF16)
            stores.append(
                pltpu.make_async_copy(own, right_ref.at[y], out_sem.at[1 + len(stores)])
            )
            stores[-1].start()
    gwo_copy.wait()
    da_own.wait()
    for k in (1, 2, 3):
        da_copy(k).wait()
    made_copy.wait()
    for pair in range(pairs):
        for copy in near_copies(pair):
            copy.wait_send()
    for n in range(2):
        for copy in first_copies(n):
            copy.wait_send()
    for copy in stores:
        copy.wait()


def experts_layer(peers, pairs, spread, capacity, *args):
    at, xp, xc, wo, gain, router, cols, rows, zp, zc, w_in, w_out, dz = args
    tokens, width = cols.shape[0], gain.shape[0]
    hidden = w_in.shape[2]
    slots = peers * capacity
    in_rows, out_rows = width // (2 * pairs), hidden // (2 * pairs)
    lanes = -(-capacity // 128) * 128
    dma = pltpu.SemaphoreType.DMA
    anywhere = pl.BlockSpec(memory_space=pl.ANY)
    inside = pl.BlockSpec(memory_space=VMEM)
    return pl.pallas_call(
        functools.partial(experts_kernel, peers, pairs, capacity),
        in_specs=[inside] * 10 + [anywhere] * 3,
        out_specs=(inside,) * 3 + (anywhere, inside) + (anywhere,) * 6,
        out_shape=(
            jax.ShapeDtypeStruct((tokens, width), F32),
            jax.ShapeDtypeStruct((tokens, 128), F32),
            jax.ShapeDtypeStruct((tokens, width), F32),
            jax.ShapeDtypeStruct((width, width), BF16),
            jax.ShapeDtypeStruct((1 + router.shape[0], width), F32),
            jax.ShapeDtypeStruct((peers, capacity, width), BF16),
            jax.ShapeDtypeStruct((pairs // 2, in_rows, hidden // 2), BF16),
            jax.ShapeDtypeStruct((2, in_rows, hidden // 2), BF16),
            jax.ShapeDtypeStruct((pairs // 2, out_rows, width // 2), BF16),
            jax.ShapeDtypeStruct((2, out_rows, width // 2), BF16),
            jax.ShapeDtypeStruct((spread, width // spread, tokens), BF16),
        ),
        scratch_shapes=[
            VMEM((width, hidden), BF16),
            VMEM((hidden, width), BF16),
            VMEM((peers, capacity, width + 128), BF16),
            VMEM((peers, capacity, width), BF16),
            VMEM((peers, capacity, width), BF16),
            VMEM((slots, hidden), BF16),
            VMEM((slots, hidden), BF16),
            VMEM((peers, capacity, width), BF16),
            VMEM((peers, capacity, width), BF16),
            VMEM((peers, 8, lanes), F32),
            VMEM((peers, 8, lanes), F32),
            VMEM((tokens, width), BF16),
            VMEM((pairs, 2, in_rows, hidden), BF16),
            VMEM((pairs, 2, out_rows, width), BF16),
            VMEM((pairs, in_rows, hidden), BF16),
            VMEM((pairs, out_rows, width), BF16),
            VMEM((pairs // 2, in_rows, hidden // 2), BF16),
            VMEM((max(pairs // 2 - 1, 1), 2, in_rows, hidden // 2), BF16),
            VMEM((pairs // 2, out_rows, width // 2), BF16),
            VMEM((max(pairs // 2 - 1, 1), 2, out_rows, width // 2), BF16),
            dma((3,)),
            dma((peers,)),
            dma((peers,)),
            dma((peers,)),
            dma((peers,)),
            dma((peers,)),
            dma((peers,)),
            dma((2, pairs)),
            dma((2, pairs)),
            dma((2, 3, pairs // 2)),
            dma((2, 3, pairs // 2)),
            dma((spread,)),
            dma((spread,)),
            dma((5 + pairs,)),
        ],
        compiler_params=pltpu.CompilerParams(
            vmem_limit_bytes=63 * MIB, collective_id=1, has_side_effects=True
        ),
        name="experts",
    )(*args)


def rear_kernel(
    lay,
    heads,
    groups,
    peers,
    da_ref,
    e_ref,
    qkvn_ref,
    qkvt_ref,
    ot_ref,
    rl_ref,
    h1_ref,
    w_ref,
    buckets_ref,
    gsmall_ref,
    gwo_ref,
    made_ref,
    gin_ref,
    ginr_ref,
    gout_ref,
    goutr_ref,
    dh_ref,
    small_ref,
    bias_ref,
    back_ref,
    gin_far_ref,
    ginr_far_ref,
    gout_far_ref,
    goutr_far_ref,
    dh_far_ref,
    sums_ref,
    ds_scr,
    dot_scr,
    do_scr,
    dt_scr,
    dh_scr,
    dh_near,
    wo_near,
    wo_far,
    wo_send,
    shares,
    x_land,
    share_land,
    total_scr,
    small_scr,
    small_land,
    bias_scr,
    bias_land,
    made_sem,
    exp_sem,
    wo_sem,
    dh_sem,
    half_send,
    half_recv,
    rs_send,
    rs_recv,
    z_send,
    z_recv,
    y_sem,
    x_send,
    x_recv,
    c_send,
    c_recv,
    small_send,
    small_recv,
    bias_send,
    bias_recv,
):
    h = pl.program_id(0)
    me = lax.axis_index("context")
    expert = lax.axis_index("expert")
    group = lax.axis_index("dp")
    near, across, far = flip(me, 1), flip(me, 2), flip(me, 3)
    high = me // 2
    feats = heads * HD
    hrow = pl.multiple_of(h * HD, HD)
    others = range(1, groups)

    def made_copy(k):
        return remote(
            made_ref.at[k],
            back_ref.at[k],
            made_sem.at[0, k],
            made_sem.at[1, k],
            expert=flip(expert, k),
        )


    grads = ((gin_ref, ginr_ref, gin_far_ref, ginr_far_ref), (gout_ref, goutr_ref, gout_far_ref, goutr_far_ref))

    def second_copies(n):
        left, right, left_far, right_far = grads[n]
        copies = [
            remote(
                right.at[1 - high], right_far, exp_sem.at[n, 0, 0], exp_sem.at[n, 1, 0], context=across
            )
        ]
        for k in others:
            target = flip(group, k)
            copies.append(
                remote(
                    left.at[target],
                    left_far.at[k - 1],
                    exp_sem.at[n, 0, k],
                    exp_sem.at[n, 1, k],
                    dp=target,
                )
            )
        return copies

    wo_first = [
        remote(
            gwo_ref.at[slab],
            wo_near.at[i],
            wo_sem.at[0, i],
            wo_sem.at[1, i],
            context=near,
        )
        for i, slab in enumerate((near, far))
    ]
    wo_second = remote(wo_send, wo_far, wo_sem.at[0, 2], wo_sem.at[1, 2], context=across)
    dh_first = [
        remote(dh_scr.at[k], dh_near.at[i], dh_sem.at[0, i], dh_sem.at[1, i], context=near)
        for i, k in enumerate((1, 3))
    ]
    dh_second = remote(
        dh_scr.at[2], dh_far_ref, dh_sem.at[0, 2], dh_sem.at[1, 2], context=across
    )

    def half_copy(part, k):
        target = flip(group, k)
        return remote(
            shares.at[part, target],
            x_land.at[part, k],
            half_send.at[part, k],
            half_recv.at[part, k],
            dp=target,
        )

    def scatter_copy(part, k):
        target = flip(expert, k)
        return remote(
            shares.at[part, group, target],
            share_land.at[part, k],
            rs_send.at[part, k],
            rs_recv.at[part, k],
            expert=target,
        )

    def scatter(part, value):
        rows, width = value.shape[0] // peers, value.shape[1] // groups
        value = value.astype(BF16)
        for i in range(groups):
            for j in range(peers):
                shares[part, i, j] = value[
                    j * rows : (j + 1) * rows, i * width : (i + 1) * width
                ]
        for k in others:
            half_copy(part, k).start()

    def pass_on(part):
        total = shares[part, group].astype(F32)
        for k in others:
            half_copy(part, k).wait_recv()
            total = total + x_land[part, k].astype(F32)
        shares[part, group] = total.astype(BF16)
        for k in reversed(range(1, peers)):
            scatter_copy(part, k).start()

    def spread_copy(part, k):
        return remote(
            total_scr.at[part],
            sums_ref.at[part, group, me, expert],
            z_send.at[part, k],
            z_recv.at[part, k],
            expert=flip(expert, k),
        )

    def spread_own(part):
        return pltpu.make_async_copy(
            total_scr.at[part], sums_ref.at[part, group, me, expert], z_send.at[part, 0]
        )

    def collect(part):
        total = shares[part, group, expert].astype(F32)
        for k in range(1, peers):
            scatter_copy(part, k).wait_recv()
            total = total + share_land[part, k].astype(F32)
        total_scr[part] = total.astype(BF16)
        for k in reversed(range(1, peers)):
            spread_copy(part, k).start()
        spread_own(part).start()

    def y_copy(part):
        view = sums_ref.at[part, group, me]
        return remote(view, view, y_sem.at[0, part], y_sem.at[1, part], context=across)

    def gathered(part):
        for k in range(1, peers):
            spread_copy(part, k).wait_recv()
        spread_own(part).wait()
        y_copy(part).start()

    def x_copy(part, k, i):
        view = sums_ref.at[part, group, (me, across)[i]]
        return remote(
            view, view, x_send.at[part, k, i], x_recv.at[part, k, i], dp=flip(group, k)
        )

    def core_copy(part, k, i):
        view = sums_ref.at[part, flip(group, k), (me, across)[i]]
        return remote(view, view, c_send.at[part, k, i], c_recv.at[part, k, i], context=near)

    stages = [("dp", group, groups), ("expert", expert, peers), ("context", me, lay.spread)]
    offsets = [0, groups, groups + peers]

    def small_copies(stage, k):
        axis, index, _ = stages[stage]
        spot = offsets[stage] + k
        where = {axis: flip(index, k)}
        return (
            remote(
                small_scr.at[stage],
                small_land.at[spot],
                small_send.at[spot],
                small_recv.at[spot],
                **where,
            ),
            remote(
                bias_scr.at[stage],
                bias_land.at[spot],
                bias_send.at[spot],
                bias_recv.at[spot],
                **where,
            ),
        )

    def small_start(stage):
        for k in range(1, stages[stage][2]):
            for copy in small_copies(stage, k):
                copy.start()

    def small_sum(stage):
        small, bias = small_scr[stage], bias_scr[stage]
        for k in range(1, stages[stage][2]):
            for copy in small_copies(stage, k):
                copy.wait_recv()
            small = small + small_land[offsets[stage] + k]
            bias = bias + bias_land[offsets[stage] + k]
        return small, bias

    @pl.when(h == 0)
    def _():
        greet(
            [{"context": t} for t in (near, across, far)]
            + [{"dp": flip(group, k)} for k in others]
            + [{"expert": flip(expert, k)} for k in range(1, peers)]
        )
        for copy in wo_first:
            copy.start()
        for n in range(2):
            for copy in second_copies(n):
                copy.start()
        for k in reversed(range(1, peers)):
            if k != 2:
                made_copy(k).start()
        bias_scr[0] = jnp.zeros_like(bias_scr[0])
        small_scr[0] = jnp.zeros_like(small_scr[0])
        small_scr[0, : gsmall_ref.shape[0]] = gsmall_ref[...]

    deltas = []
    for q in range(lay.blocks):
        cols = slice(q * BK, (q + 1) * BK)
        for c, start, at, size in lay.pieces[q]:
            where = q * BK + at
            dot_scr[:, where : where + size] = da_ref[c, pl.ds(hrow, HD), start : start + size]
        raw = dot_scr[:, cols].astype(F32)
        inverse = rl_ref[0, :, cols]
        deltas.append(
            inverse * jnp.sum(raw * ot_ref[pl.ds(hrow, HD), cols], axis=0, keepdims=True)
        )
        scaled = raw * inverse
        dot_scr[:, cols] = scaled.astype(BF16)
        do_scr[cols] = scaled.T.astype(BF16)
    krow = pl.multiple_of(feats + h * HD, HD)
    vrow = pl.multiple_of(2 * feats + h * HD, HD)
    for q in range(lay.blocks):
        cols = slice(q * BK, (q + 1) * BK)
        dq = 0.0
        for k in lay.keys[q]:
            t = lay.tile[(q, k)]
            rows = slice(k * BK, (k + 1) * BK)
            dp = dot(qkvn_ref[2 * heads + h, rows], dot_scr[:, cols])
            ds = (e_ref[0, t].astype(F32) * (dp - deltas[q])).astype(BF16)
            ds_scr[h, t] = ds
            dq = dq + dot(qkvt_ref[pl.ds(krow, HD), rows], ds)
        dt_scr[pl.ds(hrow, HD), cols] = (dq * HD**-0.5).astype(BF16)

    @pl.when(h == heads - 1)
    def _():
        collect(0)
        wo_second.wait_recv()
        scatter(
            heads,
            gwo_ref[me].astype(F32) + wo_near[0].astype(F32) + wo_far[...].astype(F32),
        )

    @pl.when(h == 1)
    def _():
        for copy in wo_first:
            copy.wait_recv()
        wo_send[...] = (gwo_ref[across].astype(F32) + wo_near[1].astype(F32)).astype(BF16)
        wo_second.start()

    for k in range(lay.blocks):
        rows = slice(k * BK, (k + 1) * BK)
        dk, dv = 0.0, 0.0
        for q in range(lay.blocks):
            if k in lay.keys[q]:
                t = lay.tile[(q, k)]
                cols = slice(q * BK, (q + 1) * BK)
                dk = dk + dot(ds_scr[h, t], qkvn_ref[h, cols])
                dv = dv + dot(e_ref[0, t], do_scr[cols])
        dt_scr[pl.ds(krow, HD), rows] = dk.T.astype(BF16)
        dt_scr[pl.ds(vrow, HD), rows] = dv.T.astype(BF16)

    for head in range(1, heads):

        @pl.when(h == head)
        def _():
            pass_on(head - 1)

    @pl.when(h == heads - 1)
    def _():
        gathered(0)

    d_all = jnp.concatenate(
        [dt_scr[pl.ds(row, HD)] for row in (hrow, krow, vrow)], axis=0
    )
    grad = dot(d_all, h1_ref[...])
    for head in range(heads):

        @pl.when(h == head)
        def _():
            scatter(head, grad)

    def distances(head):
        column = lax.broadcasted_iota(jnp.int32, bias_scr.shape[1:], 1) == me * heads + head
        span = buckets_ref.shape[0]
        number = lax.broadcasted_iota(jnp.int32, (bias_scr.shape[1], span), 0)
        pieces = [jnp.zeros((1, BK), F32) for _ in range(lay.distances + 1)]
        for d in range(lay.distances):
            tile = 0.0
            for (q, k), t in lay.tile.items():
                if lay.distance(q, k) == d:
                    tile = tile + ds_scr[head, t].astype(F32)
            sums = diagonal_sums(tile)
            pieces[d + 1] = pieces[d + 1] + sums[:, :BK]
            pieces[d] = pieces[d] + sums[:, BK:]
        by_distance = jnp.concatenate(pieces[1:], axis=1)
        hot = buckets_ref[...].reshape(1, span) == number
        summed = jnp.sum(jnp.where(hot, by_distance, 0.0), axis=1, keepdims=True)
        bias_scr[0] += jnp.where(column, summed, 0.0)

    def spread_x(part):
        y_copy(part).wait_recv()
        for k in others:
            for i in range(2):
                x_copy(part, k, i).start()
        for i in range(2):
            core_copy(part, 0, i).start()

    def spread_core(part):
        for k in others:
            for i in range(2):
                x_copy(part, k, i).wait_recv()
                core_copy(part, k, i).start()

    @pl.when(h == heads - 1)
    def _():
        half = lay.prompt_rows
        for k in (1, 3, 2, 0):
            c = flip(me, k)
            parts = [dt_scr[:, pl.ds(pl.multiple_of(c * half, 128), half)]]
            for j in range(lay.cont_count):
                first = lay.spread * (half + j * lay.cont_rows) + c * lay.cont_rows
                parts.append(dt_scr[:, pl.ds(pl.multiple_of(first, 128), lay.cont_rows)])
            block = jnp.concatenate(parts, axis=1).T
            dh_scr[k] = dot_nt(block, w_ref[...]).astype(BF16)
            if k == 1:
                dh_first[0].start()
            if k == 3:
                dh_first[1].start()
        last, wo = heads - 1, heads
        pass_on(wo)
        collect(1)
        spread_x(0)
        for copy in dh_first:
            copy.wait_recv()
        dh_scr[2] = (dh_scr[2].astype(F32) + dh_near[1].astype(F32)).astype(BF16)
        dh_second.start()
        dh_ref[...] = dh_scr[0].astype(F32) + dh_near[0].astype(F32)
        pass_on(last)
        distances(0)
        gathered(1)
        collect(wo)
        collect(last)
        made_copy(2).start()
        for head in range(1, heads):
            distances(head)
        small_start(0)
        spread_core(0)
        spread_x(1)
        gathered(wo)
        gathered(last)
        small, bias = small_sum(0)
        small_scr[1], bias_scr[1] = small, bias
        small_start(1)
        spread_core(1)
        spread_x(wo)
        spread_x(last)
        small, bias = small_sum(1)
        small_scr[2], bias_scr[2] = small, bias
        small_start(2)
        spread_core(wo)
        spread_core(last)
        small, bias = small_sum(2)
        small_ref[...] = small
        bias_ref[...] = bias
        for part in range(heads + 1):
            for k in range(groups):
                for i in range(2):
                    core_copy(part, k, i).wait()
            for k in others:
                half_copy(part, k).wait_send()
                for i in range(2):
                    x_copy(part, k, i).wait_send()
            y_copy(part).wait_send()
            for k in range(1, peers):
                spread_copy(part, k).wait_send()
                scatter_copy(part, k).wait_send()
        for stage in range(3):
            for k in range(1, stages[stage][2]):
                for copy in small_copies(stage, k):
                    copy.wait_send()
        for copy in wo_first:
            copy.wait_send()
        wo_second.wait_send()
        for copy in dh_first:
            copy.wait_send()
        dh_second.wait()
        for n in range(2):
            for copy in second_copies(n):
                copy.wait()
        for k in range(1, peers):
            made_copy(k).wait()


def rear(lay, heads, groups, peers, *args):
    da, e, qkvn, qkvt, ot, rl, h1, w, buckets, gsmall, gwo, made, gin, ginr, gout, goutr = args
    width = h1.shape[1]
    feats = heads * HD
    parts = heads + 1
    small_rows = -(-gsmall.shape[0] // 8) * 8
    rows, lanes = feats // peers, width // groups
    dma = pltpu.SemaphoreType.DMA
    anywhere = pl.BlockSpec(memory_space=pl.ANY)
    links = groups + peers + lay.spread

    def once(array):
        return pl.BlockSpec(
            array.shape, lambda h: (0,) * len(array.shape), pipeline_mode=pl.Buffered(1)
        )

    def result(shape, dtype):
        return jax.ShapeDtypeStruct(shape, dtype)

    kept = (
        result((lay.tokens, width), F32),
        result((small_rows, width), F32),
        result((BUCKETS, 128), F32),
    )
    return pl.pallas_call(
        functools.partial(rear_kernel, lay, heads, groups, peers),
        grid=(heads,),
        in_specs=[
            once(da),
            pl.BlockSpec((1, lay.tiles, BK, BK), lambda h: (h, 0, 0, 0)),
            once(qkvn),
            once(qkvt),
            once(ot),
            pl.BlockSpec((1, 1, lay.total), lambda h: (h, 0, 0)),
            once(h1),
            once(w),
            once(buckets),
            once(gsmall),
            once(gwo),
        ]
        + [anywhere] * 5,
        out_specs=tuple(once(k) for k in kept) + (anywhere,) * 7,
        out_shape=kept
        + (
            result(made.shape, BF16),
            result((max(groups - 1, 1), *gin.shape[1:]), BF16),
            result(ginr.shape[1:], BF16),
            result((max(groups - 1, 1), *gout.shape[1:]), BF16),
            result(goutr.shape[1:], BF16),
            result((lay.tokens, width), BF16),
            result((parts, groups, lay.spread, peers, rows, lanes), BF16),
        ),
        scratch_shapes=[
            VMEM((heads, lay.tiles, BK, BK), BF16),
            VMEM((HD, lay.total), BF16),
            VMEM((lay.total, HD), BF16),
            VMEM((3 * feats, lay.total), BF16),
            VMEM((4, lay.tokens, width), BF16),
            VMEM((2, lay.tokens, width), BF16),
            VMEM((2, feats, width), BF16),
            VMEM((feats, width), BF16),
            VMEM((feats, width), BF16),
            VMEM((parts, groups, peers, rows, lanes), BF16),
            VMEM((parts, groups, peers, rows, lanes), BF16),
            VMEM((parts, peers, rows, lanes), BF16),
            VMEM((parts, rows, lanes), BF16),
            VMEM((3, small_rows, width), F32),
            VMEM((links, small_rows, width), F32),
            VMEM((3, BUCKETS, 128), F32),
            VMEM((links, BUCKETS, 128), F32),
            dma((2, peers)),
            dma((2, 2, groups)),
            dma((2, 3)),
            dma((2, 3)),
            dma((parts, groups)),
            dma((parts, groups)),
            dma((parts, peers)),
            dma((parts, peers)),
            dma((parts, peers)),
            dma((parts, peers)),
            dma((2, parts)),
            dma((parts, groups, 2)),
            dma((parts, groups, 2)),
            dma((parts, groups, 2)),
            dma((parts, groups, 2)),
            dma((links,)),
            dma((links,)),
            dma((links,)),
            dma((links,)),
        ],
        compiler_params=pltpu.CompilerParams(
            vmem_limit_bytes=63 * MIB, collective_id=2, has_side_effects=True
        ),
        name="rear",
    )(*args)


def finish_kernel(lay, heads, groups, peers, capacity, count, *refs):
    names = FINISH_LOADED + FINISH_KEPT
    source = dict(zip(names, refs))
    refs = refs[len(names) :]
    target = dict(zip(FINISH_STORED, refs))
    gbias_ref, ggain_ref, ggain2_ref, grouter_ref = refs[len(FINISH_STORED) : count]
    refs = refs[count:]
    held = dict(zip(FINISH_LOADED + FINISH_STORED, refs))
    turn_scr, in_sem, out_sem = refs[len(held) :]
    group, high = lax.axis_index("dp"), lax.axis_index("context") // 2
    expert = lax.axis_index("expert")
    own = {"made": 0, "gin": group, "ginr": high, "gout": group, "goutr": high}
    loads = {}
    for n, name in enumerate(FINISH_LOADED):
        view = source[name].at[own[name]] if name in own else source[name]
        loads[name] = pltpu.make_async_copy(view, held[name], in_sem.at[n])
        loads[name].start()
    stores = {
        name: pltpu.make_async_copy(held[name], target[name], out_sem.at[n])
        for n, name in enumerate(FINISH_STORED)
    }

    def take(name):
        loads[name].wait()
        return held[name]

    def give(name, value):
        held[name][...] = value
        stores[name].start()

    half = lay.prompt_rows
    tokens = lay.tokens
    feats = heads * HD
    width = source["gain"].shape[0]
    gain = source["gain"][...].reshape(1, width)
    cols, gates = source["cols"], source["gates"]
    for side in ("", "r"):
        for name in ("gin", "gout"):
            total = take(name + side)[...].astype(F32)
            far = take(name + side + "_far")
            if side:
                total = total + far[...].astype(F32)
            else:
                for k in range(groups - 1):
                    total = total + far[k].astype(F32)
            spot = held[name + "_out"]
            size = total.shape[1]
            if side:
                spot[:, size:] = total
                stores[name + "_out"].start()
            else:
                spot[:, :size] = total

    out = take("mid")[...]
    take("made")
    take("back")
    for k in range(peers):
        base = (flip(expert, k) * capacity).astype(F32)
        number = lax.broadcasted_iota(jnp.int32, (tokens, capacity), 1).astype(F32) + base
        block = held["back"][k] if k else held["made"][...]
        for i in range(2):
            pick = jnp.where(cols[:, i : i + 1] == number, 1.0, 0.0).astype(BF16)
            out = out + gates[:, i : i + 1] * dot(pick, block)
    give("outp", out[:half].astype(BF16))
    give("outc", out[half:].astype(BF16))

    x = jnp.concatenate([take("xp")[...], take("xc")[...]], axis=0).astype(F32)
    dh1 = take("dh")[...] + take("dh_far")[...].astype(F32)
    r = lax.rsqrt(jnp.mean(x * x, axis=1, keepdims=True) + EPSILON)
    w = dh1 * gain
    mean = jnp.mean(w * x, axis=1, keepdims=True)
    dx = take("dmid")[...] + r * w - (r * r * r) * x * mean
    give("dxp", dx[:half])
    give("dxc", dx[half:])

    small_ref, bias_ref = source["small"], source["bias"]
    ggain2_ref[...] = small_ref[0:1].reshape(ggain2_ref.shape)
    grouter_ref[...] = small_ref[1 : 1 + grouter_ref.shape[0]]
    pad = jnp.concatenate([bias_ref[...], jnp.zeros((128 - BUCKETS, 128), F32)], axis=0)
    gbias_ref[...] = pad.T[: gbias_ref.shape[0], :BUCKETS]

    sums = take("sums")
    lanes = sums.shape[5]
    gwo = held["gwo"]
    for c in range(lay.spread):
        for i in range(groups):
            gwo[c * feats : (c + 1) * feats, i * lanes : (i + 1) * lanes] = (
                sums[heads, i, c].reshape(feats, lanes).astype(F32)
            )
    stores["gwo"].start()
    gained = 0.0
    for n, name in enumerate("qkv"):
        for c in range(lay.spread):
            for head in range(heads):
                to = c * feats + head * HD
                for i in range(groups):
                    block = sums[head, i, c].reshape(feats, lanes)
                    turn_scr[to : to + HD, i * lanes : (i + 1) * lanes] = block[
                        n * HD : (n + 1) * HD
                    ]
        grad = turn_scr[...].T.astype(F32)
        give("g" + name, grad)
        weight = take("w" + name)[...].astype(F32)
        gained = gained + jnp.sum(grad * weight, axis=1, keepdims=True)
    gained = jnp.broadcast_to(gained, (width, 128)).T[0:1]
    ggain_ref[...] = (gained / gain).reshape(ggain_ref.shape)
    for copy in stores.values():
        copy.wait()


FINISH_LOADED = [
    "gin",
    "gin_far",
    "gout",
    "gout_far",
    "ginr",
    "ginr_far",
    "goutr",
    "goutr_far",
    "mid",
    "made",
    "back",
    "xp",
    "xc",
    "dh",
    "dh_far",
    "dmid",
    "sums",
    "wq",
    "wk",
    "wv",
]
FINISH_KEPT = [
    "cols",
    "gates",
    "gain",
    "small",
    "bias",
]
FINISH_STORED = [
    "gin_out",
    "gout_out",
    "outp",
    "outc",
    "dxp",
    "dxc",
    "gwo",
    "gq",
    "gk",
    "gv",
]


def finish(lay, heads, groups, peers, capacity, experts, head_count, given):
    width = given["xp"].shape[1]
    rest = lay.tokens - lay.prompt_rows

    def result(shape, dtype=F32):
        return jax.ShapeDtypeStruct(shape, dtype)

    def loaded(name):
        shape = given[name].shape
        if name in ("made", "gin", "ginr", "gout", "goutr"):
            shape = shape[1:]
        return VMEM(shape, given[name].dtype)

    in_rows, in_lanes = given["gin"].shape[1:]
    out_rows, out_lanes = given["gout"].shape[1:]
    stored = (
        result((in_rows, 2 * in_lanes)),
        result((out_rows, 2 * out_lanes)),
        result((lay.prompt_rows, width), BF16),
        result((rest, width), BF16),
        result((lay.prompt_rows, width)),
        result((rest, width)),
        result((width, width)),
        result((width, width)),
        result((width, width)),
        result((width, width)),
    )
    kept = (
        result((head_count, BUCKETS)),
        result((width,)),
        result((width,)),
        result((experts, width)),
    )
    anywhere = pl.BlockSpec(memory_space=pl.ANY)
    inside = pl.BlockSpec(memory_space=VMEM)
    dma = pltpu.SemaphoreType.DMA
    return pl.pallas_call(
        functools.partial(
            finish_kernel, lay, heads, groups, peers, capacity, len(stored) + len(kept)
        ),
        in_specs=[anywhere] * len(FINISH_LOADED) + [inside] * len(FINISH_KEPT),
        out_specs=(anywhere,) * len(stored) + (inside,) * len(kept),
        out_shape=stored + kept,
        scratch_shapes=[loaded(name) for name in FINISH_LOADED]
        + [VMEM(s.shape, s.dtype) for s in stored]
        + [
            VMEM((width, width), BF16),
            dma((len(FINISH_LOADED),)),
            dma((len(stored),)),
        ],
        compiler_params=pltpu.CompilerParams(vmem_limit_bytes=60 * MIB),
        name="finish",
    )(*[given[name] for name in FINISH_LOADED + FINISH_KEPT])


def body(
    prompt_in,
    cont_in,
    prompt_route,
    cont_route,
    order,
    buckets,
    attn_gain,
    w_query,
    w_key,
    w_value,
    w_attn_out,
    rel_bias,
    ffn_gain,
    router,
    w_in,
    w_out,
    prompt_cot,
    cont_cot,
):
    prompt_rows = prompt_in.shape[1]
    cont_count = cont_in.shape[1]
    cont_rows = cont_in.shape[2]
    width = prompt_in.shape[2]
    spread = lax.axis_size("context")
    peers = lax.axis_size("expert")
    groups = lax.axis_size("dp")
    lay = Layout(spread, prompt_rows, cont_count, cont_rows)
    tokens = lay.tokens
    head_count = rel_bias.shape[1]
    heads = head_count // spread
    experts = peers * w_in.shape[0]
    capacity = 9 * tokens * 2 // (8 * experts)
    rest = cont_count * cont_rows
    xp, xc = prompt_in.reshape(prompt_rows, width), cont_in.reshape(rest, width)
    zp, zc = prompt_cot.reshape(prompt_rows, width), cont_cot.reshape(rest, width)
    router_t, bias_t = router.T, rel_bias.T
    h1, qkvn, qkvt, e, ot, rl, weights, cols, rows, at, dz_slots = front(
        lay,
        heads,
        peers,
        capacity,
        xp,
        xc,
        prompt_route[0].T,
        cont_route[0].swapaxes(1, 2),
        order.reshape(1, tokens),
        buckets,
        attn_gain,
        w_query,
        w_key,
        w_value,
        bias_t,
        zp,
        zc,
    )
    pairs = groups * spread // 2
    mid, gates, dmid, g_wo, g_small, made, gin, ginr, gout, goutr, dattn_t = experts_layer(
        peers,
        pairs,
        spread,
        capacity,
        at.reshape(width, tokens),
        xp,
        xc,
        w_attn_out,
        ffn_gain,
        router_t,
        cols,
        rows,
        zp,
        zc,
        w_in,
        w_out,
        dz_slots,
    )
    dh, small, bias, back, gin_far, ginr_far, gout_far, goutr_far, dh_far, sums = rear(
        lay,
        heads,
        groups,
        peers,
        dattn_t,
        e,
        qkvn,
        qkvt,
        ot,
        rl,
        h1,
        weights,
        buckets,
        g_small,
        g_wo.reshape(spread, width // spread, width),
        made,
        gin,
        ginr,
        gout,
        goutr,
    )
    given = dict(
        gin=gin, gin_far=gin_far, ginr=ginr, ginr_far=ginr_far,
        gout=gout, gout_far=gout_far, goutr=goutr, goutr_far=goutr_far,
        mid=mid, made=made, back=back, xp=xp, xc=xc, dh=dh, dh_far=dh_far, dmid=dmid,
        sums=sums, wq=w_query, wk=w_key, wv=w_value,
        cols=cols, gates=gates, gain=attn_gain, small=small, bias=bias,
    )
    outs = finish(lay, heads, groups, peers, capacity, experts, head_count, given)
    g_in, g_out, outp, outc, dxp, dxc, g_wo, g_q, g_k, g_v, g_bias, g_gain, g_gain2, g_router = outs
    return (
        outp[None],
        outc.reshape(1, cont_count, cont_rows, width),
        dxp[None],
        dxc.reshape(1, cont_count, cont_rows, width),
        g_gain,
        g_q,
        g_k,
        g_v,
        g_wo,
        g_bias.T,
        g_gain2,
        g_router.T,
        g_in[None],
        g_out[None],
    )


def solution(mesh):
    split = P(("dp", "expert"), "context", None)
    split_cont = P(("dp", "expert"), None, "context", None)
    whole = P()
    expert = P("expert", None, None)
    grad = P("expert", ("dp", "context"), None)
    return jax.shard_map(
        body,
        mesh=mesh,
        in_specs=(split, split_cont, split, split_cont, split)
        + (whole,) * 9
        + (expert, expert, split, split_cont),
        out_specs=(split, split_cont, split, split_cont) + (whole,) * 8 + (grad, grad),
        check_vma=False,
    )
```

```python
import functools

import jax
import jax.numpy as jnp
from jax import lax
from jax.experimental import pallas as pl
from jax.experimental.pallas import tpu as pltpu
from jax.sharding import PartitionSpec as P

HD = 64
BK = 256
BUCKETS = 32
EPSILON = 1e-06
MASKED = -1e30
F32 = jnp.float32
BF16 = jnp.bfloat16
VMEM = pltpu.VMEM
MESH = pl.DeviceIdType.MESH
MIB = 1 << 20


def dot(a, b):
    return lax.dot_general(a, b, (((1,), (0,)), ((), ())), preferred_element_type=F32)


def dot_nt(a, b):
    return lax.dot_general(a, b, (((1,), (1,)), ((), ())), preferred_element_type=F32)


def dot_tn(a, b):
    return lax.dot_general(a, b, (((0,), (0,)), ((), ())), preferred_element_type=F32)


def split_dot(a, b, op):
    high = a.astype(BF16)
    low = (a - high.astype(F32)).astype(BF16)
    return op(high, b) + op(low, b)


def full(shape):
    return pl.BlockSpec(shape, lambda *_: (0,) * len(shape))


class Layout:
    def __init__(self, spread, prompt_rows, cont_count, cont_rows):
        assert prompt_rows == BK and BK % cont_rows == 0
        self.spread = spread
        self.prompt_rows = prompt_rows
        self.cont_count = cont_count
        self.cont_rows = cont_rows
        self.tokens = prompt_rows + cont_count * cont_rows
        self.per_cont = spread * cont_rows // BK
        self.blocks = spread + cont_count * self.per_cont
        self.total = self.blocks * BK
        self.keys, self.place, self.pieces = [], [], []
        for p in range(spread):
            self.keys.append(list(range(p + 1)))
            self.place.append(p)
            self.pieces.append([(p, 0, 0, BK)])
        each = BK // cont_rows
        for j in range(cont_count):
            for m in range(self.per_cont):
                first = spread + j * self.per_cont
                self.keys.append(list(range(spread)) + list(range(first, first + m + 1)))
                self.place.append(spread + m)
                self.pieces.append(
                    [
                        (m * each + n, prompt_rows + j * cont_rows, n * cont_rows, cont_rows)
                        for n in range(each)
                    ]
                )
        self.tile = {}
        for q in range(self.blocks):
            for k in self.keys[q]:
                self.tile[(q, k)] = len(self.tile)
        self.tiles = len(self.tile)
        self.distances = spread + self.per_cont

    def distance(self, q, k):
        return self.place[q] - self.place[k]


def flip(index, mask):
    bit = 1
    while bit <= mask:
        if mask & bit:
            index = index + bit * (1 - 2 * ((index // bit) % 2))
        bit *= 2
    return index


def remote(src, dst, send, recv, **where):
    return pltpu.make_async_remote_copy(
        src_ref=src,
        dst_ref=dst,
        send_sem=send,
        recv_sem=recv,
        device_id=where,
        device_id_type=MESH,
    )


def greet(partners):
    barrier = pltpu.get_barrier_semaphore()
    for where in partners:
        pl.semaphore_signal(barrier, inc=1, device_id=where, device_id_type=MESH)
    pl.semaphore_wait(barrier, len(partners))


def make_plan(capacity, routes, order_row):
    tokens = routes.shape[0]
    side = (tokens, tokens)
    lane = lax.broadcasted_iota(jnp.int32, side, 1).astype(F32)
    sub = lax.broadcasted_iota(jnp.int32, side, 0)
    rank_col = jnp.sum(jnp.where(order_row == sub, lane, 0.0), axis=1, keepdims=True)
    rank_row = jnp.broadcast_to(rank_col, (tokens, 128)).T[0:1]
    before = jnp.where(rank_row < rank_col, 1.0, 0.0).astype(BF16)
    expert_lane = lax.broadcasted_iota(jnp.int32, (tokens, 128), 1).astype(F32)
    hots = [jnp.where(routes[:, i : i + 1] == expert_lane, 1.0, 0.0) for i in range(2)]
    counts = [dot(before, hot.astype(BF16)) for hot in hots]
    counts[1] = counts[1] + jnp.sum(hots[0], axis=0, keepdims=True)
    cols = jnp.zeros((tokens, 128), F32)
    for i in range(2):
        pos = jnp.sum(hots[i] * counts[i], axis=1, keepdims=True)
        route = routes[:, i : i + 1]
        slot = jnp.where(pos < capacity, route * capacity + pos, -1.0)
        cols = jnp.where(expert_lane == i, slot, cols)
        cols = jnp.where(expert_lane == 2 + i, route, cols)
    return cols, cols.T[0:8], hots


def toeplitz_tile(table_row, d):
    line = jnp.concatenate(
        [table_row[:, (d + 1) * BK : (d + 2) * BK], table_row[:, d * BK : (d + 1) * BK]], axis=1
    )
    tile = jnp.broadcast_to(line, (8, 2 * BK))
    row = lax.broadcasted_iota(jnp.int32, (8, 2 * BK), 0)
    for bit in (1, 2, 4):
        tile = jnp.where((row & bit) > 0, pltpu.roll(tile, bit, 1), tile)
    height = 8
    while height < BK:
        tile = jnp.concatenate([tile, pltpu.roll(tile, height, 1)], axis=0)
        height *= 2
    tile = tile[:, :BK]
    if d == 0:
        key = lax.broadcasted_iota(jnp.int32, (BK, BK), 0)
        query = lax.broadcasted_iota(jnp.int32, (BK, BK), 1)
        tile = jnp.where(query >= key, tile, MASKED)
    return tile


def diagonal_sums(tile):
    tile = jnp.concatenate([tile, jnp.zeros((BK, BK), F32)], axis=1)
    height = BK
    while height > 8:
        height //= 2
        tile = tile[:height] + pltpu.roll(tile[height:], 2 * BK - height, 1)
    row = lax.broadcasted_iota(jnp.int32, (8, 2 * BK), 0)
    for bit in (1, 2, 4):
        tile = jnp.where((row & bit) > 0, pltpu.roll(tile, 2 * BK - bit, 1), tile)
    return jnp.sum(tile, axis=0, keepdims=True)


def front_kernel(
    lay,
    heads,
    peers,
    capacity,
    xp_ref,
    xc_ref,
    rp_ref,
    rc_ref,
    order_ref,
    buckets_ref,
    gain_ref,
    wq_ref,
    wk_ref,
    wv_ref,
    bias_ref,
    zp_ref,
    zc_ref,
    h1_ref,
    qkvn_ref,
    qkvt_ref,
    e_ref,
    ot_ref,
    rl_ref,
    w_ref,
    cols_ref,
    rows_ref,
    at_ref,
    dz_ref,
    x_all,
    at_scr,
    dz_scr,
    s_scr,
    bias_scr,
    x_send,
    x_recv,
    a_send,
    a_recv,
    z_send,
    z_recv,
    own_sem,
):
    h = pl.program_id(0)
    me = lax.axis_index("context")
    expert = lax.axis_index("expert")
    feats = heads * HD
    half = lay.prompt_rows
    near, across, far = flip(me, 1), flip(me, 2), flip(me, 3)
    width = gain_ref.shape[0]
    gain = gain_ref[...].reshape(1, width)

    def x_copy(slot, part, index, target):
        view = x_all.at[slot, pl.ds(part * half, half)]
        return remote(view, view, x_send.at[index], x_recv.at[index], context=target)

    def z_copy(k):
        return remote(
            dz_scr.at[k], dz_ref.at[k], z_send.at[k], z_recv.at[k], expert=flip(expert, k)
        )

    def a_copy(k, head):
        target = flip(me, k)
        src = at_scr.at[target, pl.ds(head * HD, HD)]
        dst = at_ref.at[me, pl.ds(head * HD, HD)]
        return remote(src, dst, a_send.at[head, k], a_recv.at[head, k], context=target)

    def a_own(head):
        return pltpu.make_async_copy(
            at_scr.at[me, pl.ds(head * HD, HD)],
            at_ref.at[me, pl.ds(head * HD, HD)],
            a_send.at[head, 0],
        )

    z_own = pltpu.make_async_copy(dz_scr.at[0], dz_ref.at[0], own_sem)

    def project(slot):
        x = x_all[slot].astype(F32)
        r = lax.rsqrt(jnp.mean(x * x, axis=1, keepdims=True) + EPSILON)
        normed = (x * r * gain).astype(BF16)
        y = dot(normed, w_ref[...])
        scale = jnp.where(lax.broadcasted_iota(jnp.int32, y.shape, 1) < feats, HD**-0.5, 1.0)
        y = (y.astype(BF16).astype(F32) * scale).astype(BF16)
        yt = y.T
        spots = [(0, pl.multiple_of(slot * half, 128), half)]
        for j in range(lay.cont_count):
            first = lay.spread * half + j * lay.spread * lay.cont_rows
            spots.append(
                (
                    half + j * lay.cont_rows,
                    pl.multiple_of(first + slot * lay.cont_rows, 128),
                    lay.cont_rows,
                )
            )
        for start, to, size in spots:
            h1_ref[pl.ds(to, size)] = normed[start : start + size]
            qkvt_ref[:, pl.ds(to, size)] = yt[:, start : start + size]
            for i in range(3 * heads):
                qkvn_ref[i, pl.ds(to, size)] = y[start : start + size, i * HD : (i + 1) * HD]

    @pl.when(h == 0)
    def _():
        greet(
            [{"context": t} for t in (near, across, far)]
            + [{"expert": flip(expert, k)} for k in range(1, peers)]
        )
        x_all[me, :half] = xp_ref[...]
        x_all[me, half:] = xc_ref[...]
        for part in range(2):
            x_copy(me, part, part, across).start()
        for part in range(2):
            x_copy(me, part, 2 + part, near).start()
        tokens = lay.tokens
        routes = jnp.concatenate(
            [rp_ref[...]] + [rc_ref[j] for j in range(lay.cont_count)], axis=1
        ).astype(F32)
        routes = jnp.concatenate([routes, jnp.zeros((126, tokens), F32)], axis=0).T
        cols, rows, hots = make_plan(capacity, routes, order_ref[...])
        cols_ref[...] = cols
        rows_ref[...] = rows
        dz = jnp.concatenate([zp_ref[...], zc_ref[...]], axis=0)
        for k in list(range(1, peers)) + [0]:
            base = flip(expert, k) * capacity
            number = (lax.broadcasted_iota(jnp.int32, (capacity, tokens), 0) + base).astype(F32)
            first = jnp.where(rows[0:1] == number, 1.0, 0.0)
            second = jnp.where(rows[1:2] == number, 1.0, 0.0)
            dz_scr[k, :, :width] = dot((first + second).astype(BF16), dz).astype(BF16)
            other = dot(first.astype(BF16), hots[1].astype(BF16))
            other = other + dot(second.astype(BF16), hots[0].astype(BF16))
            dz_scr[k, :, width:] = other.astype(BF16)
            if k:
                z_copy(k).start()
            else:
                z_own.start()
        for c in range(lay.spread):

            @pl.when(me == c)
            def _():
                for i, ref in enumerate((wq_ref, wk_ref, wv_ref)):
                    w_ref[:, i * feats : (i + 1) * feats] = ref[:, c * feats : (c + 1) * feats]

        project(me)
        for part in range(2):
            x_copy(near, part, 2 + part, near).wait_recv()
        project(near)
        for part in range(2):
            x_copy(across, part, part, across).wait_recv()
            x_copy(across, part, 4 + part, near).start()
        project(across)
        for part in range(2):
            x_copy(far, part, 4 + part, near).wait_recv()
        project(far)
        for part in range(2):
            x_copy(me, part, part, across).wait_send()
            x_copy(me, part, 2 + part, near).wait_send()
            x_copy(across, part, 4 + part, near).wait_send()

    pick = lax.broadcasted_iota(jnp.int32, bias_ref.shape, 0) == me * heads + h
    bias_row = jnp.sum(jnp.where(pick, bias_ref[...], 0.0), axis=0, keepdims=True)
    bias_row = jnp.concatenate([bias_row, jnp.zeros((1, 128 - BUCKETS), F32)], axis=1)
    column = jnp.broadcast_to(bias_row, (128, 128)).T[:BUCKETS, 0:1]
    span = buckets_ref.shape[0]
    number = lax.broadcasted_iota(jnp.int32, (BUCKETS, span), 0)
    table_row = jnp.sum(
        jnp.where(buckets_ref[...].reshape(1, span) == number, column, 0.0), axis=0, keepdims=True
    )
    table_row = jnp.concatenate([jnp.zeros((1, BK), F32), table_row], axis=1)
    for d in range(lay.distances):
        bias_scr[d] = toeplitz_tile(table_row, d)
    hrow = pl.multiple_of(h * HD, HD)
    vrow = pl.multiple_of(2 * feats + h * HD, HD)
    for q in range(lay.blocks):
        qt = qkvt_ref[pl.ds(hrow, HD), q * BK : (q + 1) * BK]
        top = None
        for n, k in enumerate(lay.keys[q]):
            s = dot(qkvn_ref[heads + h, k * BK : (k + 1) * BK], qt) + bias_scr[lay.distance(q, k)]
            s_scr[n] = s
            m = jnp.max(s, axis=0, keepdims=True)
            top = m if top is None else jnp.maximum(top, m)
        total, out = 0.0, 0.0
        for n, k in enumerate(lay.keys[q]):
            e = jnp.exp(s_scr[n] - top)
            total = total + jnp.sum(e, axis=0, keepdims=True)
            e = e.astype(BF16)
            e_ref[0, lay.tile[(q, k)]] = e
            out = out + dot(qkvt_ref[pl.ds(vrow, HD), k * BK : (k + 1) * BK], e)
        inverse = 1.0 / total
        rl_ref[0, :, q * BK : (q + 1) * BK] = inverse
        out = out * inverse
        ot_ref[pl.ds(hrow, HD), q * BK : (q + 1) * BK] = out
        for c, start, at, size in lay.pieces[q]:
            at_scr[c, pl.ds(hrow, HD), start : start + size] = out[:, at : at + size].astype(BF16)

    for k in (3, 2, 1):
        a_copy(k, h).start()
    a_own(h).start()

    @pl.when(h == heads - 1)
    def _():
        for head in range(heads):
            a_own(head).wait()
            for k in (1, 2, 3):
                a_copy(k, head).wait()
        z_own.wait()
        for k in range(1, peers):
            z_copy(k).wait()


def front(lay, heads, peers, capacity, *args):
    width = args[0].shape[1]
    feats = heads * HD
    dma = pltpu.SemaphoreType.DMA
    anywhere = pl.BlockSpec(memory_space=pl.ANY)
    return pl.pallas_call(
        functools.partial(front_kernel, lay, heads, peers, capacity),
        grid=(heads,),
        in_specs=[full(a.shape) for a in args],
        out_specs=(
            full((lay.total, width)),
            full((3 * heads, lay.total, HD)),
            full((3 * feats, lay.total)),
            pl.BlockSpec((1, lay.tiles, BK, BK), lambda h: (h, 0, 0, 0)),
            full((feats, lay.total)),
            pl.BlockSpec((1, 1, lay.total), lambda h: (h, 0, 0)),
            full((width, 3 * feats)),
            full((lay.tokens, 128)),
            full((8, lay.tokens)),
            anywhere,
            anywhere,
        ),
        out_shape=(
            jax.ShapeDtypeStruct((lay.total, width), BF16),
            jax.ShapeDtypeStruct((3 * heads, lay.total, HD), BF16),
            jax.ShapeDtypeStruct((3 * feats, lay.total), BF16),
            jax.ShapeDtypeStruct((heads, lay.tiles, BK, BK), BF16),
            jax.ShapeDtypeStruct((feats, lay.total), F32),
            jax.ShapeDtypeStruct((heads, 1, lay.total), F32),
            jax.ShapeDtypeStruct((width, 3 * feats), BF16),
            jax.ShapeDtypeStruct((lay.tokens, 128), F32),
            jax.ShapeDtypeStruct((8, lay.tokens), F32),
            jax.ShapeDtypeStruct((lay.spread, feats, lay.tokens), BF16),
            jax.ShapeDtypeStruct((peers, capacity, width + 128), BF16),
        ),
        scratch_shapes=[
            VMEM((lay.spread, lay.tokens, width), BF16),
            VMEM((lay.spread, feats, lay.tokens), BF16),
            VMEM((peers, capacity, width + 128), BF16),
            VMEM((max(len(k) for k in lay.keys), BK, BK), F32),
            VMEM((lay.distances, BK, BK), F32),
            dma((6,)),
            dma((6,)),
            dma((heads, 4)),
            dma((heads, 4)),
            dma((peers,)),
            dma((peers,)),
            dma,
        ],
        compiler_params=pltpu.CompilerParams(
            vmem_limit_bytes=60 * MIB, collective_id=0, has_side_effects=True
        ),
        name="front",
    )(*args)


def gelu_parts(u):
    slope = 0.7978845608028654
    cube = 0.044715
    square = u * u
    t = jnp.tanh(slope * u * (1.0 + cube * square))
    half = 0.5 * (1.0 + t)
    value = u * half
    grad = half + 0.5 * u * (1.0 - t * t) * (slope * (1.0 + 3.0 * cube * square))
    return value, grad


def turn_index(index, mask, size):
    bit = 1
    while bit < size:
        index = index + ((mask // bit) % 2) * bit * (1 - 2 * ((index // bit) % 2))
        bit *= 2
    return index


def experts_kernel(
    peers,
    pairs,
    capacity,
    at_ref,
    xp_ref,
    xc_ref,
    wo_ref,
    gain_ref,
    router_ref,
    cols_ref,
    rows_ref,
    zp_ref,
    zc_ref,
    w_in_ref,
    w_out_ref,
    dz_ref,
    mid_ref,
    gates_ref,
    dmid_ref,
    gwo_ref,
    gsmall_ref,
    made_ref,
    gin_ref,
    ginr_ref,
    gout_ref,
    goutr_ref,
    da_ref,
    w_in,
    w_out,
    dz,
    sent,
    arrived,
    act_scr,
    dpre_scr,
    dsent,
    back,
    share,
    share_back,
    h2_scr,
    gin,
    gout,
    gin_near,
    gout_near,
    gin_y,
    gin_x,
    gout_y,
    gout_x,
    load_sem,
    s_send,
    s_recv,
    r_send,
    r_recv,
    h_send,
    h_recv,
    p_send,
    p_recv,
    q_send,
    q_recv,
    d_send,
    d_recv,
    out_sem,
):
    me = lax.axis_index("context")
    expert = lax.axis_index("expert")
    core = me % 2
    near = flip(me, 1)
    tokens = cols_ref.shape[0]
    width = gain_ref.shape[0]
    gain = gain_ref[...].reshape(1, width)
    hidden = w_in_ref.shape[2]
    lanes = share.shape[2]
    chunk = 512
    loads = [
        pltpu.make_async_copy(dz_ref, dz, load_sem.at[0]),
        pltpu.make_async_copy(w_in_ref.at[0], w_in, load_sem.at[1]),
        pltpu.make_async_copy(w_out_ref.at[0], w_out, load_sem.at[2]),
    ]
    for copy in loads:
        copy.start()
    greet(
        [{"context": flip(me, k)} for k in (1, 2, 3)]
        + [{"expert": flip(expert, k)} for k in range(1, peers)]
        + [{"dp": flip(lax.axis_index("dp"), k)} for k in range(1, pairs // 2)]
    )

    def to_peer(k, src, dst, send, recv):
        target = turn_index(expert, k, peers)
        return remote(src.at[k], dst.at[k], send.at[k], recv.at[k], expert=target)

    def dispatch(k):
        return to_peer(k, sent, arrived, s_send, s_recv)

    def returns(k):
        return (
            to_peer(k, dsent, back, r_send, r_recv),
            to_peer(k, share, share_back, h_send, h_recv),
        )

    mid = jnp.concatenate([xp_ref[...], xc_ref[...]], axis=0).astype(F32)
    mid = mid + dot_tn(at_ref[...], wo_ref[...])
    mid_ref[...] = mid
    r = lax.rsqrt(jnp.mean(mid * mid, axis=1, keepdims=True) + EPSILON)
    h2_scr[...] = (mid * r * gain).astype(BF16)
    inner = (expert * (3 - expert)) // 2 if peers == 4 else 1
    for k in ([3, 1, 2] if peers == 4 else list(range(1, peers))) + [0]:
        base = flip(expert, k) * capacity
        number = (lax.broadcasted_iota(jnp.int32, (capacity, tokens), 0) + base).astype(F32)
        pick = (rows_ref[0:1] == number) | (rows_ref[1:2] == number)
        block = dot(jnp.where(pick, 1.0, 0.0).astype(BF16), h2_scr[...]).astype(BF16)
        if k:
            sent[k] = block
            if k < 3:
                dispatch(k).start()
            elif k == 3:

                @pl.when(inner == 0)
                def _():
                    dispatch(3).start()

        else:
            arrived[0] = block
    logits = dot_nt(h2_scr[...], router_ref[...])
    lane = lax.broadcasted_iota(jnp.int32, logits.shape, 1).astype(F32)
    hots = [cols_ref[:, 2 + i : 3 + i] == lane for i in range(2)]
    chosen = [jnp.sum(jnp.where(hot, logits, 0.0), axis=1, keepdims=True) for hot in hots]
    most = jnp.maximum(chosen[0], chosen[1])
    parts = [jnp.exp(c - most) for c in chosen]
    inverse = 1.0 / (parts[0] + parts[1])
    gates = [p * inverse for p in parts]
    wide = lax.broadcasted_iota(jnp.int32, (tokens, 128), 1)
    gates_ref[...] = jnp.where(wide == 0, gates[0], jnp.where(wide == 1, gates[1], 0.0))
    for copy in loads:
        copy.wait()

    def process(k):
        rows = arrived[k]
        scores = dot_nt(rows, router_ref[...])
        elane = lax.broadcasted_iota(jnp.int32, scores.shape, 1)
        own = jnp.sum(jnp.where(elane == expert, scores, 0.0), axis=1, keepdims=True)
        other_hot = dz[k, :, width : width + scores.shape[1]].astype(F32)
        other = jnp.sum(other_hot * scores, axis=1, keepdims=True)
        gate = 1.0 / (1.0 + jnp.exp(other - own))
        dmade = (gate * dz[k, :, :width].astype(F32)).astype(BF16)
        dz[k, :, :width] = dmade
        where = pl.ds(pl.multiple_of(k * capacity, 16), capacity)
        total, part = 0.0, 0.0
        for f in range(0, hidden, chunk):
            pre = dot(rows, w_in[:, f : f + chunk])
            dact = dot_nt(dmade, w_out[f : f + chunk])
            value, grad = gelu_parts(pre)
            act = value.astype(BF16)
            act_scr[where, f : f + chunk] = act
            dpre = (dact * grad).astype(BF16)
            dpre_scr[where, f : f + chunk] = dpre
            product = act.astype(F32) * dact
            for i in range(0, chunk, 128):
                part = part + product[:, i : i + 128]
            total = total + dot_nt(dpre, w_in[:, f : f + chunk])
        dsent[k] = total.astype(BF16)
        column = jnp.broadcast_to(jnp.sum(part, axis=1, keepdims=True), (capacity, 128))
        column = jnp.concatenate([column, jnp.zeros((lanes - capacity, 128), F32)], axis=0)
        share[k] = column.T[:8]

    process(0)

    @pl.loop(1, peers)
    def _(k):
        dispatch(k).wait_recv()

        @pl.when((k >= 2) & (k + 1 < peers) & ((k > 2) | (inner == 1)))
        def _():
            dispatch(k + 1).start()

        process(k)
        for copy in returns(k):
            copy.start()

    @pl.loop(1, peers)
    def _(k):
        dispatch(k).wait_send()

    def near_copies(pair):
        return (
            remote(
                gout.at[pair, 1 - core],
                gout_near.at[pair],
                p_send.at[0, pair],
                p_recv.at[0, pair],
                context=near,
            ),
            remote(
                gin.at[pair, 1 - core],
                gin_near.at[pair],
                p_send.at[1, pair],
                p_recv.at[1, pair],
                context=near,
            ),
        )

    slots = peers * capacity
    out_rows, in_rows = gout.shape[2], gin.shape[2]
    group = lax.axis_index("dp")
    high = me // 2
    across = flip(me, 2)
    groups = pairs // 2

    totals = ((gin, gin_y, gin_x, hidden // 2), (gout, gout_y, gout_x, width // 2))

    def y_first(n, i):
        total, land, _, half = totals[n]
        return remote(
            total.at[2 * i + 1 - high, core, :, pl.ds(0, half)],
            land.at[i],
            q_send.at[n, 0, i],
            q_recv.at[n, 0, i],
            context=across,
        )

    def x_first(n, k, y):
        total, _, land, half = totals[n]
        target = flip(group, k)
        return remote(
            total.at[2 * target + y, core, :, pl.ds(half, half)],
            land.at[k - 1, y],
            q_send.at[n, 1 + y, k],
            q_recv.at[n, 1 + y, k],
            dp=target,
        )

    def first_copies(n):
        copies = [y_first(n, i) for i in range(groups)]
        return copies + [x_first(n, k, y) for k in range(1, groups) for y in range(2)]

    dmade_all = dz[:, :, :width].reshape(slots, width)
    for pair in range(pairs):
        left = arrived[:, :, 2 * pair * in_rows : 2 * (pair + 1) * in_rows]
        left = left.reshape(slots, 2 * in_rows)
        for f in range(0, hidden, 2 * chunk):
            grad = dot_tn(left, dpre_scr[:, f : f + 2 * chunk]).astype(BF16)
            gin[pair, 0, :, f : f + 2 * chunk] = grad[:in_rows]
            gin[pair, 1, :, f : f + 2 * chunk] = grad[in_rows:]
        near_copies(pair)[1].start()
    for pair in range(pairs):
        left = act_scr[:, 2 * pair * out_rows : 2 * (pair + 1) * out_rows]
        grad = dot_tn(left, dmade_all).astype(BF16)
        gout[pair, 0] = grad[:out_rows]
        gout[pair, 1] = grad[out_rows:]
        near_copies(pair)[0].start()
    for pair in range(pairs):
        near_copies(pair)[1].wait_recv()
        gin[pair, core] = (gin[pair, core].astype(F32) + gin_near[pair].astype(F32)).astype(BF16)
    for copy in first_copies(0):
        copy.start()

    @pl.loop(0, peers)
    def _(k):
        where = pl.ds(pl.multiple_of(k * capacity, 16), capacity)
        sent[k] = dot(act_scr[where], w_out[...]).astype(BF16)

    made_copy = pltpu.make_async_copy(sent, made_ref, load_sem.at[0])
    made_copy.start()
    for pair in range(pairs):
        near_copies(pair)[0].wait_recv()
        gout[pair, core] = (gout[pair, core].astype(F32) + gout_near[pair].astype(F32)).astype(BF16)
    for copy in first_copies(1):
        copy.start()

    dmid_ref[...] = jnp.zeros_like(dmid_ref)

    def collect(k, shares, block, share_row):
        base = (turn_index(expert, k, peers) * capacity).astype(F32)
        number = lax.broadcasted_iota(jnp.int32, (tokens, lanes), 1).astype(F32) + base
        picks = [cols_ref[:, i : i + 1] == number for i in range(2)]
        both = jnp.where(picks[0] | picks[1], 1.0, 0.0)[:, :capacity].astype(BF16)
        dmid_ref[...] += dot(both, block)
        return tuple(
            shares[i] + jnp.sum(jnp.where(picks[i], share_row, 0.0), axis=1, keepdims=True)
            for i in range(2)
        )

    zero = jnp.zeros((tokens, 1), F32)
    shares = collect(0, (zero, zero), dsent[0], share[0, 0:1])

    def gather_step(k, shares):
        for copy in returns(k):
            copy.wait()
        return collect(k, shares, back[k], share_back[k, 0:1])

    shares = lax.fori_loop(1, peers, gather_step, shares)
    total = shares[0] + shares[1]
    dchosen = [shares[i] - gates_ref[:, i : i + 1] * total for i in range(2)]
    elane = lax.broadcasted_iota(jnp.int32, (tokens, router_ref.shape[0]), 1).astype(F32)
    dlogits = sum(
        jnp.where(cols_ref[:, 2 + i : 3 + i] == elane, dchosen[i], 0.0) for i in range(2)
    )
    dh2 = dmid_ref[...] + split_dot(dlogits, router_ref[...], dot)
    mid = mid_ref[...]
    r = lax.rsqrt(jnp.mean(mid * mid, axis=1, keepdims=True) + EPSILON)
    u = dh2 * gain
    mean = jnp.mean(u * mid, axis=1, keepdims=True)
    cot = jnp.concatenate([zp_ref[...], zc_ref[...]], axis=0).astype(F32)
    dmid = cot + r * u - (r * r * r) * mid * mean
    dmid_ref[...] = dmid
    branch = dmid.astype(BF16)
    feats = da_ref.shape[1]

    def da_view(k):
        return act_scr.at[pl.ds(k * feats, feats), pl.ds(0, tokens)]

    def da_copy(k):
        target = flip(me, k)
        return remote(
            da_view(k), da_ref.at[me], d_send.at[k], d_recv.at[k], context=target
        )

    da_own = pltpu.make_async_copy(da_view(0), da_ref.at[me], d_send.at[0])
    for k in (3, 2, 1, 0):
        first = pl.multiple_of(flip(me, k) * feats, 64)
        block = dot_nt(wo_ref[pl.ds(first, feats)], branch).astype(BF16)
        act_scr[k * feats : (k + 1) * feats, :tokens] = block
        if k:
            da_copy(k).start()
        else:
            da_own.start()
    gsmall_ref[0:1] = jnp.sum(dh2 * mid * r, axis=0, keepdims=True)
    gsmall_ref[1:] = split_dot(dlogits, h2_scr[...], dot_tn)
    columns = slice(tokens, tokens + width)
    act_scr[:width, columns] = dot(at_ref[...], branch).astype(BF16)
    gwo_copy = pltpu.make_async_copy(
        act_scr.at[pl.ds(0, width), pl.ds(tokens, width)], gwo_ref, out_sem.at[0]
    )
    gwo_copy.start()
    stores = []
    for n, (left_ref, right_ref) in enumerate(((gin_ref, ginr_ref), (gout_ref, goutr_ref))):
        total, y_land, x_land, size = totals[n]
        left, right = pl.ds(0, size), pl.ds(size, size)
        for i in range(groups):
            y_first(n, i).wait_recv()
            own = total.at[2 * i + high, core, :, left]
            own[...] = (own[...].astype(F32) + y_land[i].astype(F32)).astype(BF16)
            stores.append(
                pltpu.make_async_copy(own, left_ref.at[i], out_sem.at[1 + len(stores)])
            )
            stores[-1].start()
        for y in range(2):
            own = total.at[2 * group + y, core, :, right]
            value = own[...].astype(F32)
            for k in range(1, groups):
                x_first(n, k, y).wait_recv()
                value = value + x_land[k - 1, y].astype(F32)
            own[...] = value.astype(BF16)
            stores.append(
                pltpu.make_async_copy(own, right_ref.at[y], out_sem.at[1 + len(stores)])
            )
            stores[-1].start()
    gwo_copy.wait()
    da_own.wait()
    for k in (1, 2, 3):
        da_copy(k).wait()
    made_copy.wait()
    for pair in range(pairs):
        for copy in near_copies(pair):
            copy.wait_send()
    for n in range(2):
        for copy in first_copies(n):
            copy.wait_send()
    for copy in stores:
        copy.wait()


def experts_layer(peers, pairs, spread, capacity, *args):
    at, xp, xc, wo, gain, router, cols, rows, zp, zc, w_in, w_out, dz = args
    tokens, width = cols.shape[0], gain.shape[0]
    hidden = w_in.shape[2]
    slots = peers * capacity
    in_rows, out_rows = width // (2 * pairs), hidden // (2 * pairs)
    lanes = -(-capacity // 128) * 128
    dma = pltpu.SemaphoreType.DMA
    anywhere = pl.BlockSpec(memory_space=pl.ANY)
    inside = pl.BlockSpec(memory_space=VMEM)
    return pl.pallas_call(
        functools.partial(experts_kernel, peers, pairs, capacity),
        in_specs=[inside] * 10 + [anywhere] * 3,
        out_specs=(inside,) * 3 + (anywhere, inside) + (anywhere,) * 6,
        out_shape=(
            jax.ShapeDtypeStruct((tokens, width), F32),
            jax.ShapeDtypeStruct((tokens, 128), F32),
            jax.ShapeDtypeStruct((tokens, width), F32),
            jax.ShapeDtypeStruct((width, width), BF16),
            jax.ShapeDtypeStruct((1 + router.shape[0], width), F32),
            jax.ShapeDtypeStruct((peers, capacity, width), BF16),
            jax.ShapeDtypeStruct((pairs // 2, in_rows, hidden // 2), BF16),
            jax.ShapeDtypeStruct((2, in_rows, hidden // 2), BF16),
            jax.ShapeDtypeStruct((pairs // 2, out_rows, width // 2), BF16),
            jax.ShapeDtypeStruct((2, out_rows, width // 2), BF16),
            jax.ShapeDtypeStruct((spread, width // spread, tokens), BF16),
        ),
        scratch_shapes=[
            VMEM((width, hidden), BF16),
            VMEM((hidden, width), BF16),
            VMEM((peers, capacity, width + 128), BF16),
            VMEM((peers, capacity, width), BF16),
            VMEM((peers, capacity, width), BF16),
            VMEM((slots, hidden), BF16),
            VMEM((slots, hidden), BF16),
            VMEM((peers, capacity, width), BF16),
            VMEM((peers, capacity, width), BF16),
            VMEM((peers, 8, lanes), F32),
            VMEM((peers, 8, lanes), F32),
            VMEM((tokens, width), BF16),
            VMEM((pairs, 2, in_rows, hidden), BF16),
            VMEM((pairs, 2, out_rows, width), BF16),
            VMEM((pairs, in_rows, hidden), BF16),
            VMEM((pairs, out_rows, width), BF16),
            VMEM((pairs // 2, in_rows, hidden // 2), BF16),
            VMEM((max(pairs // 2 - 1, 1), 2, in_rows, hidden // 2), BF16),
            VMEM((pairs // 2, out_rows, width // 2), BF16),
            VMEM((max(pairs // 2 - 1, 1), 2, out_rows, width // 2), BF16),
            dma((3,)),
            dma((peers,)),
            dma((peers,)),
            dma((peers,)),
            dma((peers,)),
            dma((peers,)),
            dma((peers,)),
            dma((2, pairs)),
            dma((2, pairs)),
            dma((2, 3, pairs // 2)),
            dma((2, 3, pairs // 2)),
            dma((spread,)),
            dma((spread,)),
            dma((5 + pairs,)),
        ],
        compiler_params=pltpu.CompilerParams(
            vmem_limit_bytes=63 * MIB, collective_id=1, has_side_effects=True
        ),
        name="experts",
    )(*args)


def rear_kernel(
    lay,
    heads,
    groups,
    peers,
    da_ref,
    e_ref,
    qkvn_ref,
    qkvt_ref,
    ot_ref,
    rl_ref,
    h1_ref,
    w_ref,
    buckets_ref,
    gsmall_ref,
    gwo_ref,
    made_ref,
    gin_ref,
    ginr_ref,
    gout_ref,
    goutr_ref,
    dh_ref,
    small_ref,
    bias_ref,
    back_ref,
    gin_far_ref,
    ginr_far_ref,
    gout_far_ref,
    goutr_far_ref,
    dh_far_ref,
    sums_ref,
    ds_scr,
    dot_scr,
    do_scr,
    dt_scr,
    dh_scr,
    dh_near,
    wo_near,
    wo_far,
    wo_send,
    shares,
    x_land,
    share_land,
    total_scr,
    small_scr,
    small_land,
    bias_scr,
    bias_land,
    made_sem,
    exp_sem,
    wo_sem,
    dh_sem,
    half_send,
    half_recv,
    rs_send,
    rs_recv,
    z_send,
    z_recv,
    y_sem,
    x_send,
    x_recv,
    c_send,
    c_recv,
    small_send,
    small_recv,
    bias_send,
    bias_recv,
):
    h = pl.program_id(0)
    me = lax.axis_index("context")
    expert = lax.axis_index("expert")
    group = lax.axis_index("dp")
    near, across, far = flip(me, 1), flip(me, 2), flip(me, 3)
    high = me // 2
    feats = heads * HD
    hrow = pl.multiple_of(h * HD, HD)
    others = range(1, groups)

    def made_copy(k):
        return remote(
            made_ref.at[k],
            back_ref.at[k],
            made_sem.at[0, k],
            made_sem.at[1, k],
            expert=flip(expert, k),
        )


    grads = ((gin_ref, ginr_ref, gin_far_ref, ginr_far_ref), (gout_ref, goutr_ref, gout_far_ref, goutr_far_ref))

    def second_copies(n):
        left, right, left_far, right_far = grads[n]
        copies = [
            remote(
                right.at[1 - high], right_far, exp_sem.at[n, 0, 0], exp_sem.at[n, 1, 0], context=across
            )
        ]
        for k in others:
            target = flip(group, k)
            copies.append(
                remote(
                    left.at[target],
                    left_far.at[k - 1],
                    exp_sem.at[n, 0, k],
                    exp_sem.at[n, 1, k],
                    dp=target,
                )
            )
        return copies

    wo_first = [
        remote(
            gwo_ref.at[slab],
            wo_near.at[i],
            wo_sem.at[0, i],
            wo_sem.at[1, i],
            context=near,
        )
        for i, slab in enumerate((near, far))
    ]
    wo_second = remote(wo_send, wo_far, wo_sem.at[0, 2], wo_sem.at[1, 2], context=across)
    dh_first = [
        remote(dh_scr.at[k], dh_near.at[i], dh_sem.at[0, i], dh_sem.at[1, i], context=near)
        for i, k in enumerate((1, 3))
    ]
    dh_second = remote(
        dh_scr.at[2], dh_far_ref, dh_sem.at[0, 2], dh_sem.at[1, 2], context=across
    )

    def half_copy(part, k):
        target = flip(group, k)
        return remote(
            shares.at[part, target],
            x_land.at[part, k],
            half_send.at[part, k],
            half_recv.at[part, k],
            dp=target,
        )

    def scatter_copy(part, k):
        target = flip(expert, k)
        return remote(
            shares.at[part, group, target],
            share_land.at[part, k],
            rs_send.at[part, k],
            rs_recv.at[part, k],
            expert=target,
        )

    def scatter(part, value):
        rows, width = value.shape[0] // peers, value.shape[1] // groups
        value = value.astype(BF16)
        for i in range(groups):
            for j in range(peers):
                shares[part, i, j] = value[
                    j * rows : (j + 1) * rows, i * width : (i + 1) * width
                ]
        for k in others:
            half_copy(part, k).start()

    def pass_on(part):
        total = shares[part, group].astype(F32)
        for k in others:
            half_copy(part, k).wait_recv()
            total = total + x_land[part, k].astype(F32)
        shares[part, group] = total.astype(BF16)
        for k in reversed(range(1, peers)):
            scatter_copy(part, k).start()

    def spread_copy(part, k):
        return remote(
            total_scr.at[part],
            sums_ref.at[part, group, me, expert],
            z_send.at[part, k],
            z_recv.at[part, k],
            expert=flip(expert, k),
        )

    def spread_own(part):
        return pltpu.make_async_copy(
            total_scr.at[part], sums_ref.at[part, group, me, expert], z_send.at[part, 0]
        )

    def collect(part):
        total = shares[part, group, expert].astype(F32)
        for k in range(1, peers):
            scatter_copy(part, k).wait_recv()
            total = total + share_land[part, k].astype(F32)
        total_scr[part] = total.astype(BF16)
        for k in reversed(range(1, peers)):
            spread_copy(part, k).start()
        spread_own(part).start()

    def y_copy(part):
        view = sums_ref.at[part, group, me]
        return remote(view, view, y_sem.at[0, part], y_sem.at[1, part], context=across)

    def gathered(part):
        for k in range(1, peers):
            spread_copy(part, k).wait_recv()
        spread_own(part).wait()
        y_copy(part).start()

    def x_copy(part, k, i):
        view = sums_ref.at[part, group, (me, across)[i]]
        return remote(
            view, view, x_send.at[part, k, i], x_recv.at[part, k, i], dp=flip(group, k)
        )

    def core_copy(part, k, i):
        view = sums_ref.at[part, flip(group, k), (me, across)[i]]
        return remote(view, view, c_send.at[part, k, i], c_recv.at[part, k, i], context=near)

    stages = [("dp", group, groups), ("expert", expert, peers), ("context", me, lay.spread)]
    offsets = [0, groups, groups + peers]

    def small_copies(stage, k):
        axis, index, _ = stages[stage]
        spot = offsets[stage] + k
        where = {axis: flip(index, k)}
        return (
            remote(
                small_scr.at[stage],
                small_land.at[spot],
                small_send.at[spot],
                small_recv.at[spot],
                **where,
            ),
            remote(
                bias_scr.at[stage],
                bias_land.at[spot],
                bias_send.at[spot],
                bias_recv.at[spot],
                **where,
            ),
        )

    def small_start(stage):
        for k in range(1, stages[stage][2]):
            for copy in small_copies(stage, k):
                copy.start()

    def small_sum(stage):
        small, bias = small_scr[stage], bias_scr[stage]
        for k in range(1, stages[stage][2]):
            for copy in small_copies(stage, k):
                copy.wait_recv()
            small = small + small_land[offsets[stage] + k]
            bias = bias + bias_land[offsets[stage] + k]
        return small, bias

    @pl.when(h == 0)
    def _():
        greet(
            [{"context": t} for t in (near, across, far)]
            + [{"dp": flip(group, k)} for k in others]
            + [{"expert": flip(expert, k)} for k in range(1, peers)]
        )
        for copy in wo_first:
            copy.start()
        for n in range(2):
            for copy in second_copies(n):
                copy.start()
        for k in reversed(range(1, peers)):
            if k != 2:
                made_copy(k).start()
        bias_scr[0] = jnp.zeros_like(bias_scr[0])
        small_scr[0] = jnp.zeros_like(small_scr[0])
        small_scr[0, : gsmall_ref.shape[0]] = gsmall_ref[...]

    deltas = []
    for q in range(lay.blocks):
        cols = slice(q * BK, (q + 1) * BK)
        for c, start, at, size in lay.pieces[q]:
            where = q * BK + at
            dot_scr[:, where : where + size] = da_ref[c, pl.ds(hrow, HD), start : start + size]
        raw = dot_scr[:, cols].astype(F32)
        inverse = rl_ref[0, :, cols]
        deltas.append(
            inverse * jnp.sum(raw * ot_ref[pl.ds(hrow, HD), cols], axis=0, keepdims=True)
        )
        scaled = raw * inverse
        dot_scr[:, cols] = scaled.astype(BF16)
        do_scr[cols] = scaled.T.astype(BF16)
    krow = pl.multiple_of(feats + h * HD, HD)
    vrow = pl.multiple_of(2 * feats + h * HD, HD)
    for q in range(lay.blocks):
        cols = slice(q * BK, (q + 1) * BK)
        dq = 0.0
        for k in lay.keys[q]:
            t = lay.tile[(q, k)]
            rows = slice(k * BK, (k + 1) * BK)
            dp = dot(qkvn_ref[2 * heads + h, rows], dot_scr[:, cols])
            ds = (e_ref[0, t].astype(F32) * (dp - deltas[q])).astype(BF16)
            ds_scr[h, t] = ds
            dq = dq + dot(qkvt_ref[pl.ds(krow, HD), rows], ds)
        dt_scr[pl.ds(hrow, HD), cols] = (dq * HD**-0.5).astype(BF16)

    @pl.when(h == heads - 1)
    def _():
        wo_second.wait_recv()
        scatter(
            heads,
            gwo_ref[me].astype(F32) + wo_near[0].astype(F32) + wo_far[...].astype(F32),
        )

    @pl.when(h == 1)
    def _():
        for copy in wo_first:
            copy.wait_recv()
        wo_send[...] = (gwo_ref[across].astype(F32) + wo_near[1].astype(F32)).astype(BF16)
        wo_second.start()

    for k in range(lay.blocks):
        rows = slice(k * BK, (k + 1) * BK)
        dk, dv = 0.0, 0.0
        for q in range(lay.blocks):
            if k in lay.keys[q]:
                t = lay.tile[(q, k)]
                cols = slice(q * BK, (q + 1) * BK)
                dk = dk + dot(ds_scr[h, t], qkvn_ref[h, cols])
                dv = dv + dot(e_ref[0, t], do_scr[cols])
        dt_scr[pl.ds(krow, HD), rows] = dk.T.astype(BF16)
        dt_scr[pl.ds(vrow, HD), rows] = dv.T.astype(BF16)

    for head in range(1, heads):

        @pl.when(h == head)
        def _():
            pass_on(head - 1)

    @pl.when(h == heads - 1)
    def _():
        collect(0)

    d_all = jnp.concatenate(
        [dt_scr[pl.ds(row, HD)] for row in (hrow, krow, vrow)], axis=0
    )
    grad = dot(d_all, h1_ref[...])
    for head in range(heads):

        @pl.when(h == head)
        def _():
            scatter(head, grad)

    def distances(head):
        column = lax.broadcasted_iota(jnp.int32, bias_scr.shape[1:], 1) == me * heads + head
        span = buckets_ref.shape[0]
        number = lax.broadcasted_iota(jnp.int32, (bias_scr.shape[1], span), 0)
        pieces = [jnp.zeros((1, BK), F32) for _ in range(lay.distances + 1)]
        for d in range(lay.distances):
            tile = 0.0
            for (q, k), t in lay.tile.items():
                if lay.distance(q, k) == d:
                    tile = tile + ds_scr[head, t].astype(F32)
            sums = diagonal_sums(tile)
            pieces[d + 1] = pieces[d + 1] + sums[:, :BK]
            pieces[d] = pieces[d] + sums[:, BK:]
        by_distance = jnp.concatenate(pieces[1:], axis=1)
        hot = buckets_ref[...].reshape(1, span) == number
        summed = jnp.sum(jnp.where(hot, by_distance, 0.0), axis=1, keepdims=True)
        bias_scr[0] += jnp.where(column, summed, 0.0)

    def spread_x(part):
        y_copy(part).wait_recv()
        for k in others:
            for i in range(2):
                x_copy(part, k, i).start()
        for i in range(2):
            core_copy(part, 0, i).start()

    def spread_core(part):
        for k in others:
            for i in range(2):
                x_copy(part, k, i).wait_recv()
                core_copy(part, k, i).start()

    @pl.when(h == heads - 1)
    def _():
        half = lay.prompt_rows
        for k in (1, 3, 2, 0):
            c = flip(me, k)
            parts = [dt_scr[:, pl.ds(pl.multiple_of(c * half, 128), half)]]
            for j in range(lay.cont_count):
                first = lay.spread * (half + j * lay.cont_rows) + c * lay.cont_rows
                parts.append(dt_scr[:, pl.ds(pl.multiple_of(first, 128), lay.cont_rows)])
            block = jnp.concatenate(parts, axis=1).T
            dh_scr[k] = dot_nt(block, w_ref[...]).astype(BF16)
            if k == 1:
                dh_first[0].start()
            if k == 3:
                dh_first[1].start()
        last, wo = heads - 1, heads
        pass_on(wo)
        collect(1)
        gathered(0)
        for copy in dh_first:
            copy.wait_recv()
        dh_scr[2] = (dh_scr[2].astype(F32) + dh_near[1].astype(F32)).astype(BF16)
        dh_second.start()
        dh_ref[...] = dh_scr[0].astype(F32) + dh_near[0].astype(F32)
        pass_on(last)
        distances(0)
        spread_x(0)
        gathered(1)
        collect(wo)
        collect(last)
        made_copy(2).start()
        for head in range(1, heads):
            distances(head)
        small_start(0)
        spread_core(0)
        spread_x(1)
        gathered(wo)
        gathered(last)
        small, bias = small_sum(0)
        small_scr[1], bias_scr[1] = small, bias
        small_start(1)
        spread_core(1)
        spread_x(wo)
        spread_x(last)
        small, bias = small_sum(1)
        small_scr[2], bias_scr[2] = small, bias
        small_start(2)
        spread_core(wo)
        spread_core(last)
        small, bias = small_sum(2)
        small_ref[...] = small
        bias_ref[...] = bias
        for part in range(heads + 1):
            for k in range(groups):
                for i in range(2):
                    core_copy(part, k, i).wait()
            for k in others:
                half_copy(part, k).wait_send()
                for i in range(2):
                    x_copy(part, k, i).wait_send()
            y_copy(part).wait_send()
            for k in range(1, peers):
                spread_copy(part, k).wait_send()
                scatter_copy(part, k).wait_send()
        for stage in range(3):
            for k in range(1, stages[stage][2]):
                for copy in small_copies(stage, k):
                    copy.wait_send()
        for copy in wo_first:
            copy.wait_send()
        wo_second.wait_send()
        for copy in dh_first:
            copy.wait_send()
        dh_second.wait()
        for n in range(2):
            for copy in second_copies(n):
                copy.wait()
        for k in range(1, peers):
            made_copy(k).wait()


def rear(lay, heads, groups, peers, *args):
    da, e, qkvn, qkvt, ot, rl, h1, w, buckets, gsmall, gwo, made, gin, ginr, gout, goutr = args
    width = h1.shape[1]
    feats = heads * HD
    parts = heads + 1
    small_rows = -(-gsmall.shape[0] // 8) * 8
    rows, lanes = feats // peers, width // groups
    dma = pltpu.SemaphoreType.DMA
    anywhere = pl.BlockSpec(memory_space=pl.ANY)
    links = groups + peers + lay.spread

    def once(array):
        return pl.BlockSpec(
            array.shape, lambda h: (0,) * len(array.shape), pipeline_mode=pl.Buffered(1)
        )

    def result(shape, dtype):
        return jax.ShapeDtypeStruct(shape, dtype)

    kept = (
        result((lay.tokens, width), F32),
        result((small_rows, width), F32),
        result((BUCKETS, 128), F32),
    )
    return pl.pallas_call(
        functools.partial(rear_kernel, lay, heads, groups, peers),
        grid=(heads,),
        in_specs=[
            once(da),
            pl.BlockSpec((1, lay.tiles, BK, BK), lambda h: (h, 0, 0, 0)),
            once(qkvn),
            once(qkvt),
            once(ot),
            pl.BlockSpec((1, 1, lay.total), lambda h: (h, 0, 0)),
            once(h1),
            once(w),
            once(buckets),
            once(gsmall),
            once(gwo),
        ]
        + [anywhere] * 5,
        out_specs=tuple(once(k) for k in kept) + (anywhere,) * 7,
        out_shape=kept
        + (
            result(made.shape, BF16),
            result((max(groups - 1, 1), *gin.shape[1:]), BF16),
            result(ginr.shape[1:], BF16),
            result((max(groups - 1, 1), *gout.shape[1:]), BF16),
            result(goutr.shape[1:], BF16),
            result((lay.tokens, width), BF16),
            result((parts, groups, lay.spread, peers, rows, lanes), BF16),
        ),
        scratch_shapes=[
            VMEM((heads, lay.tiles, BK, BK), BF16),
            VMEM((HD, lay.total), BF16),
            VMEM((lay.total, HD), BF16),
            VMEM((3 * feats, lay.total), BF16),
            VMEM((4, lay.tokens, width), BF16),
            VMEM((2, lay.tokens, width), BF16),
            VMEM((2, feats, width), BF16),
            VMEM((feats, width), BF16),
            VMEM((feats, width), BF16),
            VMEM((parts, groups, peers, rows, lanes), BF16),
            VMEM((parts, groups, peers, rows, lanes), BF16),
            VMEM((parts, peers, rows, lanes), BF16),
            VMEM((parts, rows, lanes), BF16),
            VMEM((3, small_rows, width), F32),
            VMEM((links, small_rows, width), F32),
            VMEM((3, BUCKETS, 128), F32),
            VMEM((links, BUCKETS, 128), F32),
            dma((2, peers)),
            dma((2, 2, groups)),
            dma((2, 3)),
            dma((2, 3)),
            dma((parts, groups)),
            dma((parts, groups)),
            dma((parts, peers)),
            dma((parts, peers)),
            dma((parts, peers)),
            dma((parts, peers)),
            dma((2, parts)),
            dma((parts, groups, 2)),
            dma((parts, groups, 2)),
            dma((parts, groups, 2)),
            dma((parts, groups, 2)),
            dma((links,)),
            dma((links,)),
            dma((links,)),
            dma((links,)),
        ],
        compiler_params=pltpu.CompilerParams(
            vmem_limit_bytes=63 * MIB, collective_id=2, has_side_effects=True
        ),
        name="rear",
    )(*args)


def finish_kernel(lay, heads, groups, peers, capacity, count, *refs):
    names = FINISH_LOADED + FINISH_KEPT
    source = dict(zip(names, refs))
    refs = refs[len(names) :]
    target = dict(zip(FINISH_STORED, refs))
    gbias_ref, ggain_ref, ggain2_ref, grouter_ref = refs[len(FINISH_STORED) : count]
    refs = refs[count:]
    names = [name for name in FINISH_LOADED if name not in ("made", "back")]
    held = dict(zip(names + FINISH_STORED, refs))
    made_scr, turn_scr, in_sem, out_sem = refs[len(held) :]
    held["made"], held["back"] = made_scr.at[0], made_scr.at[pl.ds(1, peers - 1)]
    group, high = lax.axis_index("dp"), lax.axis_index("context") // 2
    expert = lax.axis_index("expert")
    own = {"made": 0, "gin": group, "ginr": high, "gout": group, "goutr": high}
    loads = {}
    for n, name in enumerate(FINISH_LOADED):
        view = source[name].at[own[name]] if name in own else source[name]
        if name == "back":
            view = view.at[pl.ds(1, peers - 1)]
        loads[name] = pltpu.make_async_copy(view, held[name], in_sem.at[n])
        loads[name].start()
    stores = {
        name: pltpu.make_async_copy(held[name], target[name], out_sem.at[n])
        for n, name in enumerate(FINISH_STORED)
    }

    def take(name):
        loads[name].wait()
        return held[name]

    def give(name, value):
        held[name][...] = value
        stores[name].start()

    half = lay.prompt_rows
    tokens = lay.tokens
    feats = heads * HD
    width = source["gain"].shape[0]
    gain = source["gain"][...].reshape(1, width)
    cols, gates = source["cols"], source["gates"]
    for side in ("", "r"):
        for name in ("gin", "gout"):
            total = take(name + side)[...].astype(F32)
            far = take(name + side + "_far")
            if side:
                total = total + far[...].astype(F32)
            else:
                for k in range(groups - 1):
                    total = total + far[k].astype(F32)
            spot = held[name + "_out"]
            size = total.shape[1]
            if side:
                spot[:, size:] = total
                stores[name + "_out"].start()
            else:
                spot[:, :size] = total

    out = take("mid")[...]
    take("made")
    take("back")
    slots = peers * capacity
    lane = lax.broadcasted_iota(jnp.int32, (1, slots), 1)
    number = lane
    for k in range(peers):
        shift = (flip(expert, k) - k) * capacity
        inside = (lane >= k * capacity) & (lane < (k + 1) * capacity)
        number = number + jnp.where(inside, shift, 0)
    number = number.astype(F32)
    blocks = made_scr[...].reshape(slots, width)
    for i in range(2):
        pick = jnp.where(cols[:, i : i + 1] == number, 1.0, 0.0).astype(BF16)
        out = out + gates[:, i : i + 1] * dot(pick, blocks)
    give("outp", out[:half].astype(BF16))
    give("outc", out[half:].astype(BF16))

    x = jnp.concatenate([take("xp")[...], take("xc")[...]], axis=0).astype(F32)
    dh1 = take("dh")[...] + take("dh_far")[...].astype(F32)
    r = lax.rsqrt(jnp.mean(x * x, axis=1, keepdims=True) + EPSILON)
    w = dh1 * gain
    mean = jnp.mean(w * x, axis=1, keepdims=True)
    dx = take("dmid")[...] + r * w - (r * r * r) * x * mean
    give("dxp", dx[:half])
    give("dxc", dx[half:])

    small_ref, bias_ref = source["small"], source["bias"]
    ggain2_ref[...] = small_ref[0:1].reshape(ggain2_ref.shape)
    grouter_ref[...] = small_ref[1 : 1 + grouter_ref.shape[0]]
    pad = jnp.concatenate([bias_ref[...], jnp.zeros((128 - BUCKETS, 128), F32)], axis=0)
    gbias_ref[...] = pad.T[: gbias_ref.shape[0], :BUCKETS]

    sums = take("sums")
    lanes = sums.shape[5]
    gwo = held["gwo"]
    for c in range(lay.spread):
        for i in range(groups):
            gwo[c * feats : (c + 1) * feats, i * lanes : (i + 1) * lanes] = (
                sums[heads, i, c].reshape(feats, lanes).astype(F32)
            )
    stores["gwo"].start()
    gained = 0.0
    for n, name in enumerate("qkv"):
        for c in range(lay.spread):
            for head in range(heads):
                to = c * feats + head * HD
                for i in range(groups):
                    block = sums[head, i, c].reshape(feats, lanes)
                    turn_scr[to : to + HD, i * lanes : (i + 1) * lanes] = block[
                        n * HD : (n + 1) * HD
                    ]
        grad = turn_scr[...].T.astype(F32)
        give("g" + name, grad)
        weight = take("w" + name)[...].astype(F32)
        gained = gained + jnp.sum(grad * weight, axis=1, keepdims=True)
    gained = jnp.broadcast_to(gained, (width, 128)).T[0:1]
    ggain_ref[...] = (gained / gain).reshape(ggain_ref.shape)
    for copy in stores.values():
        copy.wait()


FINISH_LOADED = [
    "gin",
    "gin_far",
    "gout",
    "gout_far",
    "ginr",
    "ginr_far",
    "goutr",
    "goutr_far",
    "mid",
    "made",
    "back",
    "xp",
    "xc",
    "dh",
    "dh_far",
    "dmid",
    "sums",
    "wq",
    "wk",
    "wv",
]
FINISH_KEPT = [
    "cols",
    "gates",
    "gain",
    "small",
    "bias",
]
FINISH_STORED = [
    "gin_out",
    "gout_out",
    "outp",
    "outc",
    "dxp",
    "dxc",
    "gwo",
    "gq",
    "gk",
    "gv",
]


def finish(lay, heads, groups, peers, capacity, experts, head_count, given):
    width = given["xp"].shape[1]
    rest = lay.tokens - lay.prompt_rows

    def result(shape, dtype=F32):
        return jax.ShapeDtypeStruct(shape, dtype)

    def loaded(name):
        shape = given[name].shape
        if name in ("made", "gin", "ginr", "gout", "goutr"):
            shape = shape[1:]
        return VMEM(shape, given[name].dtype)

    in_rows, in_lanes = given["gin"].shape[1:]
    out_rows, out_lanes = given["gout"].shape[1:]
    stored = (
        result((in_rows, 2 * in_lanes)),
        result((out_rows, 2 * out_lanes)),
        result((lay.prompt_rows, width), BF16),
        result((rest, width), BF16),
        result((lay.prompt_rows, width)),
        result((rest, width)),
        result((width, width)),
        result((width, width)),
        result((width, width)),
        result((width, width)),
    )
    kept = (
        result((head_count, BUCKETS)),
        result((width,)),
        result((width,)),
        result((experts, width)),
    )
    anywhere = pl.BlockSpec(memory_space=pl.ANY)
    inside = pl.BlockSpec(memory_space=VMEM)
    dma = pltpu.SemaphoreType.DMA
    return pl.pallas_call(
        functools.partial(
            finish_kernel, lay, heads, groups, peers, capacity, len(stored) + len(kept)
        ),
        in_specs=[anywhere] * len(FINISH_LOADED) + [inside] * len(FINISH_KEPT),
        out_specs=(anywhere,) * len(stored) + (inside,) * len(kept),
        out_shape=stored + kept,
        scratch_shapes=[loaded(name) for name in FINISH_LOADED if name not in ("made", "back")]
        + [VMEM(s.shape, s.dtype) for s in stored]
        + [
            VMEM(given["back"].shape, BF16),
            VMEM((width, width), BF16),
            dma((len(FINISH_LOADED),)),
            dma((len(stored),)),
        ],
        compiler_params=pltpu.CompilerParams(vmem_limit_bytes=60 * MIB),
        name="finish",
    )(*[given[name] for name in FINISH_LOADED + FINISH_KEPT])


def body(
    prompt_in,
    cont_in,
    prompt_route,
    cont_route,
    order,
    buckets,
    attn_gain,
    w_query,
    w_key,
    w_value,
    w_attn_out,
    rel_bias,
    ffn_gain,
    router,
    w_in,
    w_out,
    prompt_cot,
    cont_cot,
):
    prompt_rows = prompt_in.shape[1]
    cont_count = cont_in.shape[1]
    cont_rows = cont_in.shape[2]
    width = prompt_in.shape[2]
    spread = lax.axis_size("context")
    peers = lax.axis_size("expert")
    groups = lax.axis_size("dp")
    lay = Layout(spread, prompt_rows, cont_count, cont_rows)
    tokens = lay.tokens
    head_count = rel_bias.shape[1]
    heads = head_count // spread
    experts = peers * w_in.shape[0]
    capacity = 9 * tokens * 2 // (8 * experts)
    rest = cont_count * cont_rows
    xp, xc = prompt_in.reshape(prompt_rows, width), cont_in.reshape(rest, width)
    zp, zc = prompt_cot.reshape(prompt_rows, width), cont_cot.reshape(rest, width)
    router_t, bias_t = router.T, rel_bias.T
    h1, qkvn, qkvt, e, ot, rl, weights, cols, rows, at, dz_slots = front(
        lay,
        heads,
        peers,
        capacity,
        xp,
        xc,
        prompt_route[0].T,
        cont_route[0].swapaxes(1, 2),
        order.reshape(1, tokens),
        buckets,
        attn_gain,
        w_query,
        w_key,
        w_value,
        bias_t,
        zp,
        zc,
    )
    pairs = groups * spread // 2
    mid, gates, dmid, g_wo, g_small, made, gin, ginr, gout, goutr, dattn_t = experts_layer(
        peers,
        pairs,
        spread,
        capacity,
        at.reshape(width, tokens),
        xp,
        xc,
        w_attn_out,
        ffn_gain,
        router_t,
        cols,
        rows,
        zp,
        zc,
        w_in,
        w_out,
        dz_slots,
    )
    dh, small, bias, back, gin_far, ginr_far, gout_far, goutr_far, dh_far, sums = rear(
        lay,
        heads,
        groups,
        peers,
        dattn_t,
        e,
        qkvn,
        qkvt,
        ot,
        rl,
        h1,
        weights,
        buckets,
        g_small,
        g_wo.reshape(spread, width // spread, width),
        made,
        gin,
        ginr,
        gout,
        goutr,
    )
    given = dict(
        gin=gin, gin_far=gin_far, ginr=ginr, ginr_far=ginr_far,
        gout=gout, gout_far=gout_far, goutr=goutr, goutr_far=goutr_far,
        mid=mid, made=made, back=back, xp=xp, xc=xc, dh=dh, dh_far=dh_far, dmid=dmid,
        sums=sums, wq=w_query, wk=w_key, wv=w_value,
        cols=cols, gates=gates, gain=attn_gain, small=small, bias=bias,
    )
    outs = finish(lay, heads, groups, peers, capacity, experts, head_count, given)
    g_in, g_out, outp, outc, dxp, dxc, g_wo, g_q, g_k, g_v, g_bias, g_gain, g_gain2, g_router = outs
    return (
        outp[None],
        outc.reshape(1, cont_count, cont_rows, width),
        dxp[None],
        dxc.reshape(1, cont_count, cont_rows, width),
        g_gain,
        g_q,
        g_k,
        g_v,
        g_wo,
        g_bias.T,
        g_gain2,
        g_router.T,
        g_in[None],
        g_out[None],
    )


def solution(mesh):
    split = P(("dp", "expert"), "context", None)
    split_cont = P(("dp", "expert"), None, "context", None)
    whole = P()
    expert = P("expert", None, None)
    grad = P("expert", ("dp", "context"), None)
    return jax.shard_map(
        body,
        mesh=mesh,
        in_specs=(split, split_cont, split, split_cont, split)
        + (whole,) * 9
        + (expert, expert, split, split_cont),
        out_specs=(split, split_cont, split, split_cont) + (whole,) * 8 + (grad, grad),
        check_vma=False,
    )
```

```python
import functools

import jax
import jax.numpy as jnp
from jax import lax
from jax.experimental import pallas as pl
from jax.experimental.pallas import tpu as pltpu
from jax.sharding import PartitionSpec as P

HD = 64
BK = 256
BUCKETS = 32
EPSILON = 1e-06
MASKED = -1e30
F32 = jnp.float32
BF16 = jnp.bfloat16
VMEM = pltpu.VMEM
MESH = pl.DeviceIdType.MESH
MIB = 1 << 20


def dot(a, b):
    return lax.dot_general(a, b, (((1,), (0,)), ((), ())), preferred_element_type=F32)


def dot_nt(a, b):
    return lax.dot_general(a, b, (((1,), (1,)), ((), ())), preferred_element_type=F32)


def dot_tn(a, b):
    return lax.dot_general(a, b, (((0,), (0,)), ((), ())), preferred_element_type=F32)


def split_dot(a, b, op):
    high = a.astype(BF16)
    low = (a - high.astype(F32)).astype(BF16)
    return op(high, b) + op(low, b)


def full(shape):
    return pl.BlockSpec(shape, lambda *_: (0,) * len(shape))


class Layout:
    def __init__(self, spread, prompt_rows, cont_count, cont_rows):
        assert prompt_rows == BK and BK % cont_rows == 0
        self.spread = spread
        self.prompt_rows = prompt_rows
        self.cont_count = cont_count
        self.cont_rows = cont_rows
        self.tokens = prompt_rows + cont_count * cont_rows
        self.per_cont = spread * cont_rows // BK
        self.blocks = spread + cont_count * self.per_cont
        self.total = self.blocks * BK
        self.keys, self.place, self.pieces = [], [], []
        for p in range(spread):
            self.keys.append(list(range(p + 1)))
            self.place.append(p)
            self.pieces.append([(p, 0, 0, BK)])
        each = BK // cont_rows
        for j in range(cont_count):
            for m in range(self.per_cont):
                first = spread + j * self.per_cont
                self.keys.append(list(range(spread)) + list(range(first, first + m + 1)))
                self.place.append(spread + m)
                self.pieces.append(
                    [
                        (m * each + n, prompt_rows + j * cont_rows, n * cont_rows, cont_rows)
                        for n in range(each)
                    ]
                )
        self.tile = {}
        for q in range(self.blocks):
            for k in self.keys[q]:
                self.tile[(q, k)] = len(self.tile)
        self.tiles = len(self.tile)
        self.distances = spread + self.per_cont

    def distance(self, q, k):
        return self.place[q] - self.place[k]


def flip(index, mask):
    bit = 1
    while bit <= mask:
        if mask & bit:
            index = index + bit * (1 - 2 * ((index // bit) % 2))
        bit *= 2
    return index


def remote(src, dst, send, recv, **where):
    return pltpu.make_async_remote_copy(
        src_ref=src,
        dst_ref=dst,
        send_sem=send,
        recv_sem=recv,
        device_id=where,
        device_id_type=MESH,
    )


def greet(partners):
    barrier = pltpu.get_barrier_semaphore()
    for where in partners:
        pl.semaphore_signal(barrier, inc=1, device_id=where, device_id_type=MESH)
    pl.semaphore_wait(barrier, len(partners))


def make_plan(capacity, routes, order_row):
    tokens = routes.shape[0]
    side = (tokens, tokens)
    lane = lax.broadcasted_iota(jnp.int32, side, 1).astype(F32)
    sub = lax.broadcasted_iota(jnp.int32, side, 0)
    rank_col = jnp.sum(jnp.where(order_row == sub, lane, 0.0), axis=1, keepdims=True)
    rank_row = jnp.broadcast_to(rank_col, (tokens, 128)).T[0:1]
    before = jnp.where(rank_row < rank_col, 1.0, 0.0).astype(BF16)
    expert_lane = lax.broadcasted_iota(jnp.int32, (tokens, 128), 1).astype(F32)
    hots = [jnp.where(routes[:, i : i + 1] == expert_lane, 1.0, 0.0) for i in range(2)]
    counts = [dot(before, hot.astype(BF16)) for hot in hots]
    counts[1] = counts[1] + jnp.sum(hots[0], axis=0, keepdims=True)
    cols = jnp.zeros((tokens, 128), F32)
    for i in range(2):
        pos = jnp.sum(hots[i] * counts[i], axis=1, keepdims=True)
        route = routes[:, i : i + 1]
        slot = jnp.where(pos < capacity, route * capacity + pos, -1.0)
        cols = jnp.where(expert_lane == i, slot, cols)
        cols = jnp.where(expert_lane == 2 + i, route, cols)
    return cols, cols.T[0:8], hots


def toeplitz_tile(table_row, d):
    line = jnp.concatenate(
        [table_row[:, (d + 1) * BK : (d + 2) * BK], table_row[:, d * BK : (d + 1) * BK]], axis=1
    )
    tile = jnp.broadcast_to(line, (8, 2 * BK))
    row = lax.broadcasted_iota(jnp.int32, (8, 2 * BK), 0)
    for bit in (1, 2, 4):
        tile = jnp.where((row & bit) > 0, pltpu.roll(tile, bit, 1), tile)
    height = 8
    while height < BK:
        tile = jnp.concatenate([tile, pltpu.roll(tile, height, 1)], axis=0)
        height *= 2
    tile = tile[:, :BK]
    if d == 0:
        key = lax.broadcasted_iota(jnp.int32, (BK, BK), 0)
        query = lax.broadcasted_iota(jnp.int32, (BK, BK), 1)
        tile = jnp.where(query >= key, tile, MASKED)
    return tile


def diagonal_sums(tile):
    tile = jnp.concatenate([tile, jnp.zeros((BK, BK), F32)], axis=1)
    height = BK
    while height > 8:
        height //= 2
        tile = tile[:height] + pltpu.roll(tile[height:], 2 * BK - height, 1)
    row = lax.broadcasted_iota(jnp.int32, (8, 2 * BK), 0)
    for bit in (1, 2, 4):
        tile = jnp.where((row & bit) > 0, pltpu.roll(tile, 2 * BK - bit, 1), tile)
    return jnp.sum(tile, axis=0, keepdims=True)


def front_kernel(
    lay,
    heads,
    peers,
    capacity,
    xp_ref,
    xc_ref,
    rp_ref,
    rc_ref,
    order_ref,
    buckets_ref,
    gain_ref,
    wq_ref,
    wk_ref,
    wv_ref,
    bias_ref,
    zp_ref,
    zc_ref,
    h1_ref,
    qkvn_ref,
    qkvt_ref,
    e_ref,
    ot_ref,
    rl_ref,
    w_ref,
    cols_ref,
    rows_ref,
    at_ref,
    dz_ref,
    x_all,
    at_scr,
    dz_scr,
    s_scr,
    bias_scr,
    x_send,
    x_recv,
    a_send,
    a_recv,
    z_send,
    z_recv,
    own_sem,
):
    h = pl.program_id(0)
    me = lax.axis_index("context")
    expert = lax.axis_index("expert")
    feats = heads * HD
    half = lay.prompt_rows
    near, across, far = flip(me, 1), flip(me, 2), flip(me, 3)
    width = gain_ref.shape[0]
    gain = gain_ref[...].reshape(1, width)

    def x_copy(slot, part, index, target):
        view = x_all.at[slot, pl.ds(part * half, half)]
        return remote(view, view, x_send.at[index], x_recv.at[index], context=target)

    def z_copy(k):
        return remote(
            dz_scr.at[k], dz_ref.at[k], z_send.at[k], z_recv.at[k], expert=flip(expert, k)
        )

    def a_copy(k, head):
        target = flip(me, k)
        src = at_scr.at[target, pl.ds(head * HD, HD)]
        dst = at_ref.at[me, pl.ds(head * HD, HD)]
        return remote(src, dst, a_send.at[head, k], a_recv.at[head, k], context=target)

    def a_own(head):
        return pltpu.make_async_copy(
            at_scr.at[me, pl.ds(head * HD, HD)],
            at_ref.at[me, pl.ds(head * HD, HD)],
            a_send.at[head, 0],
        )

    z_own = pltpu.make_async_copy(dz_scr.at[0], dz_ref.at[0], own_sem)

    def project(slot):
        x = x_all[slot].astype(F32)
        r = lax.rsqrt(jnp.mean(x * x, axis=1, keepdims=True) + EPSILON)
        normed = (x * r * gain).astype(BF16)
        y = dot(normed, w_ref[...])
        scale = jnp.where(lax.broadcasted_iota(jnp.int32, y.shape, 1) < feats, HD**-0.5, 1.0)
        y = (y.astype(BF16).astype(F32) * scale).astype(BF16)
        yt = y.T
        spots = [(0, pl.multiple_of(slot * half, 128), half)]
        for j in range(lay.cont_count):
            first = lay.spread * half + j * lay.spread * lay.cont_rows
            spots.append(
                (
                    half + j * lay.cont_rows,
                    pl.multiple_of(first + slot * lay.cont_rows, 128),
                    lay.cont_rows,
                )
            )
        for start, to, size in spots:
            h1_ref[pl.ds(to, size)] = normed[start : start + size]
            qkvt_ref[:, pl.ds(to, size)] = yt[:, start : start + size]
            for i in range(3 * heads):
                qkvn_ref[i, pl.ds(to, size)] = y[start : start + size, i * HD : (i + 1) * HD]

    @pl.when(h == 0)
    def _():
        greet(
            [{"context": t} for t in (near, across, far)]
            + [{"expert": flip(expert, k)} for k in range(1, peers)]
        )
        x_all[me, :half] = xp_ref[...]
        x_all[me, half:] = xc_ref[...]
        for part in range(2):
            x_copy(me, part, part, across).start()
        for part in range(2):
            x_copy(me, part, 2 + part, near).start()
        tokens = lay.tokens
        routes = jnp.concatenate(
            [rp_ref[...]] + [rc_ref[j] for j in range(lay.cont_count)], axis=1
        ).astype(F32)
        routes = jnp.concatenate([routes, jnp.zeros((126, tokens), F32)], axis=0).T
        cols, rows, hots = make_plan(capacity, routes, order_ref[...])
        cols_ref[...] = cols
        rows_ref[...] = rows
        dz = jnp.concatenate([zp_ref[...], zc_ref[...]], axis=0)
        for k in list(range(1, peers)) + [0]:
            base = flip(expert, k) * capacity
            number = (lax.broadcasted_iota(jnp.int32, (capacity, tokens), 0) + base).astype(F32)
            first = jnp.where(rows[0:1] == number, 1.0, 0.0)
            second = jnp.where(rows[1:2] == number, 1.0, 0.0)
            dz_scr[k, :, :width] = dot((first + second).astype(BF16), dz).astype(BF16)
            other = dot(first.astype(BF16), hots[1].astype(BF16))
            other = other + dot(second.astype(BF16), hots[0].astype(BF16))
            dz_scr[k, :, width:] = other.astype(BF16)
            if k:
                z_copy(k).start()
            else:
                z_own.start()
        for c in range(lay.spread):

            @pl.when(me == c)
            def _():
                for i, ref in enumerate((wq_ref, wk_ref, wv_ref)):
                    w_ref[:, i * feats : (i + 1) * feats] = ref[:, c * feats : (c + 1) * feats]

        project(me)
        for part in range(2):
            x_copy(near, part, 2 + part, near).wait_recv()
        project(near)
        for part in range(2):
            x_copy(across, part, part, across).wait_recv()
            x_copy(across, part, 4 + part, near).start()
        project(across)
        for part in range(2):
            x_copy(far, part, 4 + part, near).wait_recv()
        project(far)
        for part in range(2):
            x_copy(me, part, part, across).wait_send()
            x_copy(me, part, 2 + part, near).wait_send()
            x_copy(across, part, 4 + part, near).wait_send()

    pick = lax.broadcasted_iota(jnp.int32, bias_ref.shape, 0) == me * heads + h
    bias_row = jnp.sum(jnp.where(pick, bias_ref[...], 0.0), axis=0, keepdims=True)
    bias_row = jnp.concatenate([bias_row, jnp.zeros((1, 128 - BUCKETS), F32)], axis=1)
    column = jnp.broadcast_to(bias_row, (128, 128)).T[:BUCKETS, 0:1]
    span = buckets_ref.shape[0]
    number = lax.broadcasted_iota(jnp.int32, (BUCKETS, span), 0)
    table_row = jnp.sum(
        jnp.where(buckets_ref[...].reshape(1, span) == number, column, 0.0), axis=0, keepdims=True
    )
    table_row = jnp.concatenate([jnp.zeros((1, BK), F32), table_row], axis=1)
    for d in range(lay.distances):
        bias_scr[d] = toeplitz_tile(table_row, d)
    hrow = pl.multiple_of(h * HD, HD)
    vrow = pl.multiple_of(2 * feats + h * HD, HD)
    for q in range(lay.blocks):
        qt = qkvt_ref[pl.ds(hrow, HD), q * BK : (q + 1) * BK]
        top = None
        for n, k in enumerate(lay.keys[q]):
            s = dot(qkvn_ref[heads + h, k * BK : (k + 1) * BK], qt) + bias_scr[lay.distance(q, k)]
            s_scr[n] = s
            m = jnp.max(s, axis=0, keepdims=True)
            top = m if top is None else jnp.maximum(top, m)
        total, out = 0.0, 0.0
        for n, k in enumerate(lay.keys[q]):
            e = jnp.exp(s_scr[n] - top)
            total = total + jnp.sum(e, axis=0, keepdims=True)
            e = e.astype(BF16)
            e_ref[0, lay.tile[(q, k)]] = e
            out = out + dot(qkvt_ref[pl.ds(vrow, HD), k * BK : (k + 1) * BK], e)
        inverse = 1.0 / total
        rl_ref[0, :, q * BK : (q + 1) * BK] = inverse
        out = out * inverse
        ot_ref[pl.ds(hrow, HD), q * BK : (q + 1) * BK] = out
        for c, start, at, size in lay.pieces[q]:
            at_scr[c, pl.ds(hrow, HD), start : start + size] = out[:, at : at + size].astype(BF16)

    for k in (3, 2, 1):
        a_copy(k, h).start()
    a_own(h).start()

    @pl.when(h == heads - 1)
    def _():
        for head in range(heads):
            a_own(head).wait()
            for k in (1, 2, 3):
                a_copy(k, head).wait()
        z_own.wait()
        for k in range(1, peers):
            z_copy(k).wait()


def front(lay, heads, peers, capacity, *args):
    width = args[0].shape[1]
    feats = heads * HD
    dma = pltpu.SemaphoreType.DMA
    anywhere = pl.BlockSpec(memory_space=pl.ANY)
    return pl.pallas_call(
        functools.partial(front_kernel, lay, heads, peers, capacity),
        grid=(heads,),
        in_specs=[full(a.shape) for a in args],
        out_specs=(
            full((lay.total, width)),
            full((3 * heads, lay.total, HD)),
            full((3 * feats, lay.total)),
            pl.BlockSpec((1, lay.tiles, BK, BK), lambda h: (h, 0, 0, 0)),
            full((feats, lay.total)),
            pl.BlockSpec((1, 1, lay.total), lambda h: (h, 0, 0)),
            full((width, 3 * feats)),
            full((lay.tokens, 128)),
            full((8, lay.tokens)),
            anywhere,
            anywhere,
        ),
        out_shape=(
            jax.ShapeDtypeStruct((lay.total, width), BF16),
            jax.ShapeDtypeStruct((3 * heads, lay.total, HD), BF16),
            jax.ShapeDtypeStruct((3 * feats, lay.total), BF16),
            jax.ShapeDtypeStruct((heads, lay.tiles, BK, BK), BF16),
            jax.ShapeDtypeStruct((feats, lay.total), F32),
            jax.ShapeDtypeStruct((heads, 1, lay.total), F32),
            jax.ShapeDtypeStruct((width, 3 * feats), BF16),
            jax.ShapeDtypeStruct((lay.tokens, 128), F32),
            jax.ShapeDtypeStruct((8, lay.tokens), F32),
            jax.ShapeDtypeStruct((lay.spread, feats, lay.tokens), BF16),
            jax.ShapeDtypeStruct((peers, capacity, width + 128), BF16),
        ),
        scratch_shapes=[
            VMEM((lay.spread, lay.tokens, width), BF16),
            VMEM((lay.spread, feats, lay.tokens), BF16),
            VMEM((peers, capacity, width + 128), BF16),
            VMEM((max(len(k) for k in lay.keys), BK, BK), F32),
            VMEM((lay.distances, BK, BK), F32),
            dma((6,)),
            dma((6,)),
            dma((heads, 4)),
            dma((heads, 4)),
            dma((peers,)),
            dma((peers,)),
            dma,
        ],
        compiler_params=pltpu.CompilerParams(
            vmem_limit_bytes=60 * MIB, collective_id=0, has_side_effects=True
        ),
        name="front",
    )(*args)


def gelu_parts(u):
    slope = 0.7978845608028654
    cube = 0.044715
    square = u * u
    t = jnp.tanh(slope * u * (1.0 + cube * square))
    half = 0.5 * (1.0 + t)
    value = u * half
    grad = half + 0.5 * u * (1.0 - t * t) * (slope * (1.0 + 3.0 * cube * square))
    return value, grad


def turn_index(index, mask, size):
    bit = 1
    while bit < size:
        index = index + ((mask // bit) % 2) * bit * (1 - 2 * ((index // bit) % 2))
        bit *= 2
    return index


def experts_kernel(
    peers,
    pairs,
    capacity,
    at_ref,
    xp_ref,
    xc_ref,
    wo_ref,
    gain_ref,
    router_ref,
    cols_ref,
    rows_ref,
    zp_ref,
    zc_ref,
    w_in_ref,
    w_out_ref,
    dz_ref,
    mid_ref,
    gates_ref,
    dmid_ref,
    gwo_ref,
    gsmall_ref,
    made_ref,
    gin_ref,
    ginr_ref,
    gout_ref,
    goutr_ref,
    da_ref,
    w_in,
    w_out,
    dz,
    sent,
    arrived,
    act_scr,
    dpre_scr,
    dsent,
    back,
    share,
    share_back,
    h2_scr,
    gin,
    gout,
    gin_near,
    gout_near,
    gin_y,
    gin_x,
    gout_y,
    gout_x,
    load_sem,
    s_send,
    s_recv,
    r_send,
    r_recv,
    h_send,
    h_recv,
    p_send,
    p_recv,
    q_send,
    q_recv,
    d_send,
    d_recv,
    out_sem,
):
    me = lax.axis_index("context")
    expert = lax.axis_index("expert")
    core = me % 2
    near = flip(me, 1)
    tokens = cols_ref.shape[0]
    width = gain_ref.shape[0]
    gain = gain_ref[...].reshape(1, width)
    hidden = w_in_ref.shape[2]
    lanes = share.shape[2]
    chunk = 512
    loads = [
        pltpu.make_async_copy(dz_ref, dz, load_sem.at[0]),
        pltpu.make_async_copy(w_in_ref.at[0], w_in, load_sem.at[1]),
        pltpu.make_async_copy(w_out_ref.at[0], w_out, load_sem.at[2]),
    ]
    for copy in loads:
        copy.start()
    greet(
        [{"context": flip(me, k)} for k in (1, 2, 3)]
        + [{"expert": flip(expert, k)} for k in range(1, peers)]
        + [{"dp": flip(lax.axis_index("dp"), k)} for k in range(1, pairs // 2)]
    )

    def to_peer(k, src, dst, send, recv):
        target = turn_index(expert, k, peers)
        return remote(src.at[k], dst.at[k], send.at[k], recv.at[k], expert=target)

    def dispatch(k):
        return to_peer(k, sent, arrived, s_send, s_recv)

    def returns(k):
        return (
            to_peer(k, dsent, back, r_send, r_recv),
            to_peer(k, share, share_back, h_send, h_recv),
        )

    mid = jnp.concatenate([xp_ref[...], xc_ref[...]], axis=0).astype(F32)
    mid = mid + dot_tn(at_ref[...], wo_ref[...])
    mid_ref[...] = mid
    r = lax.rsqrt(jnp.mean(mid * mid, axis=1, keepdims=True) + EPSILON)
    h2_scr[...] = (mid * r * gain).astype(BF16)
    inner = (expert * (3 - expert)) // 2 if peers == 4 else 1
    for k in ([3, 1, 2] if peers == 4 else list(range(1, peers))) + [0]:
        base = flip(expert, k) * capacity
        number = (lax.broadcasted_iota(jnp.int32, (capacity, tokens), 0) + base).astype(F32)
        pick = (rows_ref[0:1] == number) | (rows_ref[1:2] == number)
        block = dot(jnp.where(pick, 1.0, 0.0).astype(BF16), h2_scr[...]).astype(BF16)
        if k:
            sent[k] = block
            if k < 3:
                dispatch(k).start()
            elif k == 3:

                @pl.when(inner == 0)
                def _():
                    dispatch(3).start()

        else:
            arrived[0] = block
    logits = dot_nt(h2_scr[...], router_ref[...])
    lane = lax.broadcasted_iota(jnp.int32, logits.shape, 1).astype(F32)
    hots = [cols_ref[:, 2 + i : 3 + i] == lane for i in range(2)]
    chosen = [jnp.sum(jnp.where(hot, logits, 0.0), axis=1, keepdims=True) for hot in hots]
    most = jnp.maximum(chosen[0], chosen[1])
    parts = [jnp.exp(c - most) for c in chosen]
    inverse = 1.0 / (parts[0] + parts[1])
    gates = [p * inverse for p in parts]
    wide = lax.broadcasted_iota(jnp.int32, (tokens, 128), 1)
    gates_ref[...] = jnp.where(wide == 0, gates[0], jnp.where(wide == 1, gates[1], 0.0))
    for copy in loads:
        copy.wait()

    def process(k):
        rows = arrived[k]
        scores = dot_nt(rows, router_ref[...])
        elane = lax.broadcasted_iota(jnp.int32, scores.shape, 1)
        own = jnp.sum(jnp.where(elane == expert, scores, 0.0), axis=1, keepdims=True)
        other_hot = dz[k, :, width : width + scores.shape[1]].astype(F32)
        other = jnp.sum(other_hot * scores, axis=1, keepdims=True)
        gate = 1.0 / (1.0 + jnp.exp(other - own))
        dmade = (gate * dz[k, :, :width].astype(F32)).astype(BF16)
        dz[k, :, :width] = dmade
        where = pl.ds(pl.multiple_of(k * capacity, 16), capacity)
        total, part = 0.0, 0.0
        for f in range(0, hidden, chunk):
            pre = dot(rows, w_in[:, f : f + chunk])
            dact = dot_nt(dmade, w_out[f : f + chunk])
            value, grad = gelu_parts(pre)
            act = value.astype(BF16)
            act_scr[where, f : f + chunk] = act
            dpre = (dact * grad).astype(BF16)
            dpre_scr[where, f : f + chunk] = dpre
            product = act.astype(F32) * dact
            for i in range(0, chunk, 128):
                part = part + product[:, i : i + 128]
            total = total + dot_nt(dpre, w_in[:, f : f + chunk])
        dsent[k] = total.astype(BF16)
        column = jnp.broadcast_to(jnp.sum(part, axis=1, keepdims=True), (capacity, 128))
        column = jnp.concatenate([column, jnp.zeros((lanes - capacity, 128), F32)], axis=0)
        share[k] = column.T[:8]

    process(0)

    @pl.loop(1, peers)
    def _(k):
        dispatch(k).wait_recv()

        @pl.when((k >= 2) & (k + 1 < peers) & ((k > 2) | (inner == 1)))
        def _():
            dispatch(k + 1).start()

        process(k)
        for copy in returns(k):
            copy.start()

    @pl.loop(1, peers)
    def _(k):
        dispatch(k).wait_send()

    def near_copies(pair):
        return (
            remote(
                gout.at[pair, 1 - core],
                gout_near.at[pair],
                p_send.at[0, pair],
                p_recv.at[0, pair],
                context=near,
            ),
            remote(
                gin.at[pair, 1 - core],
                gin_near.at[pair],
                p_send.at[1, pair],
                p_recv.at[1, pair],
                context=near,
            ),
        )

    slots = peers * capacity
    out_rows, in_rows = gout.shape[2], gin.shape[2]
    group = lax.axis_index("dp")
    high = me // 2
    across = flip(me, 2)
    groups = pairs // 2

    totals = ((gin, gin_y, gin_x, hidden // 2), (gout, gout_y, gout_x, width // 2))

    def y_first(n, i):
        total, land, _, half = totals[n]
        return remote(
            total.at[2 * i + 1 - high, core, :, pl.ds(0, half)],
            land.at[i],
            q_send.at[n, 0, i],
            q_recv.at[n, 0, i],
            context=across,
        )

    def x_first(n, k, y):
        total, _, land, half = totals[n]
        target = flip(group, k)
        return remote(
            total.at[2 * target + y, core, :, pl.ds(half, half)],
            land.at[k - 1, y],
            q_send.at[n, 1 + y, k],
            q_recv.at[n, 1 + y, k],
            dp=target,
        )

    def first_copies(n):
        copies = [y_first(n, i) for i in range(groups)]
        return copies + [x_first(n, k, y) for k in range(1, groups) for y in range(2)]

    dmade_all = dz[:, :, :width].reshape(slots, width)
    for pair in range(pairs):
        left = arrived[:, :, 2 * pair * in_rows : 2 * (pair + 1) * in_rows]
        left = left.reshape(slots, 2 * in_rows)
        for f in range(0, hidden, 2 * chunk):
            grad = dot_tn(left, dpre_scr[:, f : f + 2 * chunk]).astype(BF16)
            gin[pair, 0, :, f : f + 2 * chunk] = grad[:in_rows]
            gin[pair, 1, :, f : f + 2 * chunk] = grad[in_rows:]
        near_copies(pair)[1].start()
    for pair in range(pairs):
        left = act_scr[:, 2 * pair * out_rows : 2 * (pair + 1) * out_rows]
        grad = dot_tn(left, dmade_all).astype(BF16)
        gout[pair, 0] = grad[:out_rows]
        gout[pair, 1] = grad[out_rows:]
        near_copies(pair)[0].start()
    for pair in range(pairs):
        near_copies(pair)[1].wait_recv()
        gin[pair, core] = (gin[pair, core].astype(F32) + gin_near[pair].astype(F32)).astype(BF16)
    for copy in first_copies(0):
        copy.start()

    for pair in range(pairs):
        near_copies(pair)[0].wait_recv()
        gout[pair, core] = (gout[pair, core].astype(F32) + gout_near[pair].astype(F32)).astype(BF16)
    for copy in first_copies(1):
        copy.start()

    dmid_ref[...] = jnp.zeros_like(dmid_ref)

    def collect(k, shares, block, share_row):
        base = (turn_index(expert, k, peers) * capacity).astype(F32)
        number = lax.broadcasted_iota(jnp.int32, (tokens, lanes), 1).astype(F32) + base
        picks = [cols_ref[:, i : i + 1] == number for i in range(2)]
        both = jnp.where(picks[0] | picks[1], 1.0, 0.0)[:, :capacity].astype(BF16)
        dmid_ref[...] += dot(both, block)
        return tuple(
            shares[i] + jnp.sum(jnp.where(picks[i], share_row, 0.0), axis=1, keepdims=True)
            for i in range(2)
        )

    zero = jnp.zeros((tokens, 1), F32)
    shares = collect(0, (zero, zero), dsent[0], share[0, 0:1])

    def gather_step(k, shares):
        for copy in returns(k):
            copy.wait()
        return collect(k, shares, back[k], share_back[k, 0:1])

    shares = lax.fori_loop(1, peers, gather_step, shares)
    total = shares[0] + shares[1]
    dchosen = [shares[i] - gates_ref[:, i : i + 1] * total for i in range(2)]
    elane = lax.broadcasted_iota(jnp.int32, (tokens, router_ref.shape[0]), 1).astype(F32)
    dlogits = sum(
        jnp.where(cols_ref[:, 2 + i : 3 + i] == elane, dchosen[i], 0.0) for i in range(2)
    )
    dh2 = dmid_ref[...] + split_dot(dlogits, router_ref[...], dot)
    mid = mid_ref[...]
    r = lax.rsqrt(jnp.mean(mid * mid, axis=1, keepdims=True) + EPSILON)
    u = dh2 * gain
    mean = jnp.mean(u * mid, axis=1, keepdims=True)
    cot = jnp.concatenate([zp_ref[...], zc_ref[...]], axis=0).astype(F32)
    dmid = cot + r * u - (r * r * r) * mid * mean
    dmid_ref[...] = dmid
    branch = dmid.astype(BF16)
    feats = da_ref.shape[1]

    def da_view(k):
        return dpre_scr.at[pl.ds(k * feats, feats), pl.ds(0, tokens)]

    def da_copy(k):
        target = flip(me, k)
        return remote(
            da_view(k), da_ref.at[me], d_send.at[k], d_recv.at[k], context=target
        )

    da_own = pltpu.make_async_copy(da_view(0), da_ref.at[me], d_send.at[0])
    for k in (3, 2, 1, 0):
        first = pl.multiple_of(flip(me, k) * feats, 64)
        block = dot_nt(wo_ref[pl.ds(first, feats)], branch).astype(BF16)
        dpre_scr[k * feats : (k + 1) * feats, :tokens] = block
        if k:
            da_copy(k).start()
        else:
            da_own.start()
    gsmall_ref[0:1] = jnp.sum(dh2 * mid * r, axis=0, keepdims=True)
    gsmall_ref[1:] = split_dot(dlogits, h2_scr[...], dot_tn)
    columns = slice(tokens, tokens + width)
    dpre_scr[:width, columns] = dot(at_ref[...], branch).astype(BF16)
    gwo_copy = pltpu.make_async_copy(
        dpre_scr.at[pl.ds(0, width), pl.ds(tokens, width)], gwo_ref, out_sem.at[0]
    )
    gwo_copy.start()
    @pl.loop(0, peers)
    def _(k):
        where = pl.ds(pl.multiple_of(k * capacity, 16), capacity)
        sent[k] = dot(act_scr[where], w_out[...]).astype(BF16)

    made_copy = pltpu.make_async_copy(sent, made_ref, load_sem.at[0])
    made_copy.start()
    stores = []
    for n, (left_ref, right_ref) in enumerate(((gin_ref, ginr_ref), (gout_ref, goutr_ref))):
        total, y_land, x_land, size = totals[n]
        left, right = pl.ds(0, size), pl.ds(size, size)
        for i in range(groups):
            y_first(n, i).wait_recv()
            own = total.at[2 * i + high, core, :, left]
            own[...] = (own[...].astype(F32) + y_land[i].astype(F32)).astype(BF16)
            stores.append(
                pltpu.make_async_copy(own, left_ref.at[i], out_sem.at[1 + len(stores)])
            )
            stores[-1].start()
        for y in range(2):
            own = total.at[2 * group + y, core, :, right]
            value = own[...].astype(F32)
            for k in range(1, groups):
                x_first(n, k, y).wait_recv()
                value = value + x_land[k - 1, y].astype(F32)
            own[...] = value.astype(BF16)
            stores.append(
                pltpu.make_async_copy(own, right_ref.at[y], out_sem.at[1 + len(stores)])
            )
            stores[-1].start()
    gwo_copy.wait()
    da_own.wait()
    for k in (1, 2, 3):
        da_copy(k).wait()
    made_copy.wait()
    for pair in range(pairs):
        for copy in near_copies(pair):
            copy.wait_send()
    for n in range(2):
        for copy in first_copies(n):
            copy.wait_send()
    for copy in stores:
        copy.wait()


def experts_layer(peers, pairs, spread, capacity, *args):
    at, xp, xc, wo, gain, router, cols, rows, zp, zc, w_in, w_out, dz = args
    tokens, width = cols.shape[0], gain.shape[0]
    hidden = w_in.shape[2]
    slots = peers * capacity
    in_rows, out_rows = width // (2 * pairs), hidden // (2 * pairs)
    lanes = -(-capacity // 128) * 128
    dma = pltpu.SemaphoreType.DMA
    anywhere = pl.BlockSpec(memory_space=pl.ANY)
    inside = pl.BlockSpec(memory_space=VMEM)
    return pl.pallas_call(
        functools.partial(experts_kernel, peers, pairs, capacity),
        in_specs=[inside] * 10 + [anywhere] * 3,
        out_specs=(inside,) * 3 + (anywhere, inside) + (anywhere,) * 6,
        out_shape=(
            jax.ShapeDtypeStruct((tokens, width), F32),
            jax.ShapeDtypeStruct((tokens, 128), F32),
            jax.ShapeDtypeStruct((tokens, width), F32),
            jax.ShapeDtypeStruct((width, width), BF16),
            jax.ShapeDtypeStruct((1 + router.shape[0], width), F32),
            jax.ShapeDtypeStruct((peers, capacity, width), BF16),
            jax.ShapeDtypeStruct((pairs // 2, in_rows, hidden // 2), BF16),
            jax.ShapeDtypeStruct((2, in_rows, hidden // 2), BF16),
            jax.ShapeDtypeStruct((pairs // 2, out_rows, width // 2), BF16),
            jax.ShapeDtypeStruct((2, out_rows, width // 2), BF16),
            jax.ShapeDtypeStruct((spread, width // spread, tokens), BF16),
        ),
        scratch_shapes=[
            VMEM((width, hidden), BF16),
            VMEM((hidden, width), BF16),
            VMEM((peers, capacity, width + 128), BF16),
            VMEM((peers, capacity, width), BF16),
            VMEM((peers, capacity, width), BF16),
            VMEM((slots, hidden), BF16),
            VMEM((slots, hidden), BF16),
            VMEM((peers, capacity, width), BF16),
            VMEM((peers, capacity, width), BF16),
            VMEM((peers, 8, lanes), F32),
            VMEM((peers, 8, lanes), F32),
            VMEM((tokens, width), BF16),
            VMEM((pairs, 2, in_rows, hidden), BF16),
            VMEM((pairs, 2, out_rows, width), BF16),
            VMEM((pairs, in_rows, hidden), BF16),
            VMEM((pairs, out_rows, width), BF16),
            VMEM((pairs // 2, in_rows, hidden // 2), BF16),
            VMEM((max(pairs // 2 - 1, 1), 2, in_rows, hidden // 2), BF16),
            VMEM((pairs // 2, out_rows, width // 2), BF16),
            VMEM((max(pairs // 2 - 1, 1), 2, out_rows, width // 2), BF16),
            dma((3,)),
            dma((peers,)),
            dma((peers,)),
            dma((peers,)),
            dma((peers,)),
            dma((peers,)),
            dma((peers,)),
            dma((2, pairs)),
            dma((2, pairs)),
            dma((2, 3, pairs // 2)),
            dma((2, 3, pairs // 2)),
            dma((spread,)),
            dma((spread,)),
            dma((5 + pairs,)),
        ],
        compiler_params=pltpu.CompilerParams(
            vmem_limit_bytes=63 * MIB, collective_id=1, has_side_effects=True
        ),
        name="experts",
    )(*args)


def rear_kernel(
    lay,
    heads,
    groups,
    peers,
    da_ref,
    e_ref,
    qkvn_ref,
    qkvt_ref,
    ot_ref,
    rl_ref,
    h1_ref,
    w_ref,
    buckets_ref,
    gsmall_ref,
    gwo_ref,
    made_ref,
    gin_ref,
    ginr_ref,
    gout_ref,
    goutr_ref,
    dh_ref,
    small_ref,
    bias_ref,
    back_ref,
    gin_far_ref,
    ginr_far_ref,
    gout_far_ref,
    goutr_far_ref,
    dh_far_ref,
    sums_ref,
    ds_scr,
    dot_scr,
    do_scr,
    dt_scr,
    dh_scr,
    dh_near,
    wo_near,
    wo_far,
    wo_send,
    shares,
    x_land,
    share_land,
    total_scr,
    small_scr,
    small_land,
    bias_scr,
    bias_land,
    made_sem,
    exp_sem,
    wo_sem,
    dh_sem,
    half_send,
    half_recv,
    rs_send,
    rs_recv,
    z_send,
    z_recv,
    y_sem,
    x_send,
    x_recv,
    c_send,
    c_recv,
    small_send,
    small_recv,
    bias_send,
    bias_recv,
):
    h = pl.program_id(0)
    me = lax.axis_index("context")
    expert = lax.axis_index("expert")
    group = lax.axis_index("dp")
    near, across, far = flip(me, 1), flip(me, 2), flip(me, 3)
    high = me // 2
    feats = heads * HD
    hrow = pl.multiple_of(h * HD, HD)
    others = range(1, groups)

    def made_copy(k):
        return remote(
            made_ref.at[k],
            back_ref.at[k],
            made_sem.at[0, k],
            made_sem.at[1, k],
            expert=flip(expert, k),
        )


    grads = ((gin_ref, ginr_ref, gin_far_ref, ginr_far_ref), (gout_ref, goutr_ref, gout_far_ref, goutr_far_ref))

    def second_copies(n):
        left, right, left_far, right_far = grads[n]
        copies = [
            remote(
                right.at[1 - high], right_far, exp_sem.at[n, 0, 0], exp_sem.at[n, 1, 0], context=across
            )
        ]
        for k in others:
            target = flip(group, k)
            copies.append(
                remote(
                    left.at[target],
                    left_far.at[k - 1],
                    exp_sem.at[n, 0, k],
                    exp_sem.at[n, 1, k],
                    dp=target,
                )
            )
        return copies

    wo_first = [
        remote(
            gwo_ref.at[slab],
            wo_near.at[i],
            wo_sem.at[0, i],
            wo_sem.at[1, i],
            context=near,
        )
        for i, slab in enumerate((near, far))
    ]
    wo_second = remote(wo_send, wo_far, wo_sem.at[0, 2], wo_sem.at[1, 2], context=across)
    dh_first = [
        remote(dh_scr.at[k], dh_near.at[i], dh_sem.at[0, i], dh_sem.at[1, i], context=near)
        for i, k in enumerate((1, 3))
    ]
    dh_second = remote(
        dh_scr.at[2], dh_far_ref, dh_sem.at[0, 2], dh_sem.at[1, 2], context=across
    )

    def half_copy(part, k):
        target = flip(group, k)
        return remote(
            shares.at[part, target],
            x_land.at[part, k],
            half_send.at[part, k],
            half_recv.at[part, k],
            dp=target,
        )

    def scatter_copy(part, k):
        target = flip(expert, k)
        return remote(
            shares.at[part, group, target],
            share_land.at[part, k],
            rs_send.at[part, k],
            rs_recv.at[part, k],
            expert=target,
        )

    def scatter(part, value):
        rows, width = value.shape[0] // peers, value.shape[1] // groups
        value = value.astype(BF16)
        for i in range(groups):
            for j in range(peers):
                shares[part, i, j] = value[
                    j * rows : (j + 1) * rows, i * width : (i + 1) * width
                ]
        for k in others:
            half_copy(part, k).start()

    def pass_on(part):
        total = shares[part, group].astype(F32)
        for k in others:
            half_copy(part, k).wait_recv()
            total = total + x_land[part, k].astype(F32)
        shares[part, group] = total.astype(BF16)
        for k in reversed(range(1, peers)):
            scatter_copy(part, k).start()

    def spread_copy(part, k):
        return remote(
            total_scr.at[part],
            sums_ref.at[part, group, me, expert],
            z_send.at[part, k],
            z_recv.at[part, k],
            expert=flip(expert, k),
        )

    def spread_own(part):
        return pltpu.make_async_copy(
            total_scr.at[part], sums_ref.at[part, group, me, expert], z_send.at[part, 0]
        )

    def collect(part):
        total = shares[part, group, expert].astype(F32)
        for k in range(1, peers):
            scatter_copy(part, k).wait_recv()
            total = total + share_land[part, k].astype(F32)
        total_scr[part] = total.astype(BF16)
        for k in reversed(range(1, peers)):
            spread_copy(part, k).start()
        spread_own(part).start()

    def y_copy(part):
        view = sums_ref.at[part, group, me]
        return remote(view, view, y_sem.at[0, part], y_sem.at[1, part], context=across)

    def gathered(part):
        for k in range(1, peers):
            spread_copy(part, k).wait_recv()
        spread_own(part).wait()
        y_copy(part).start()

    def x_copy(part, k, i):
        view = sums_ref.at[part, group, (me, across)[i]]
        return remote(
            view, view, x_send.at[part, k, i], x_recv.at[part, k, i], dp=flip(group, k)
        )

    def core_copy(part, k, i):
        view = sums_ref.at[part, flip(group, k), (me, across)[i]]
        return remote(view, view, c_send.at[part, k, i], c_recv.at[part, k, i], context=near)

    stages = [("dp", group, groups), ("expert", expert, peers), ("context", me, lay.spread)]
    offsets = [0, groups, groups + peers]

    def small_copies(stage, k):
        axis, index, _ = stages[stage]
        spot = offsets[stage] + k
        where = {axis: flip(index, k)}
        return (
            remote(
                small_scr.at[stage],
                small_land.at[spot],
                small_send.at[spot],
                small_recv.at[spot],
                **where,
            ),
            remote(
                bias_scr.at[stage],
                bias_land.at[spot],
                bias_send.at[spot],
                bias_recv.at[spot],
                **where,
            ),
        )

    def small_start(stage):
        for k in range(1, stages[stage][2]):
            for copy in small_copies(stage, k):
                copy.start()

    def small_sum(stage):
        small, bias = small_scr[stage], bias_scr[stage]
        for k in range(1, stages[stage][2]):
            for copy in small_copies(stage, k):
                copy.wait_recv()
            small = small + small_land[offsets[stage] + k]
            bias = bias + bias_land[offsets[stage] + k]
        return small, bias

    @pl.when(h == 0)
    def _():
        greet(
            [{"context": t} for t in (near, across, far)]
            + [{"dp": flip(group, k)} for k in others]
            + [{"expert": flip(expert, k)} for k in range(1, peers)]
        )
        for copy in wo_first:
            copy.start()
        for n in range(2):
            for copy in second_copies(n):
                copy.start()
        for k in reversed(range(1, peers)):
            if k > 2:
                made_copy(k).start()
        bias_scr[0] = jnp.zeros_like(bias_scr[0])
        small_scr[0] = jnp.zeros_like(small_scr[0])
        small_scr[0, : gsmall_ref.shape[0]] = gsmall_ref[...]

    deltas = []
    for q in range(lay.blocks):
        cols = slice(q * BK, (q + 1) * BK)
        for c, start, at, size in lay.pieces[q]:
            where = q * BK + at
            dot_scr[:, where : where + size] = da_ref[c, pl.ds(hrow, HD), start : start + size]
        raw = dot_scr[:, cols].astype(F32)
        inverse = rl_ref[0, :, cols]
        deltas.append(
            inverse * jnp.sum(raw * ot_ref[pl.ds(hrow, HD), cols], axis=0, keepdims=True)
        )
        scaled = raw * inverse
        dot_scr[:, cols] = scaled.astype(BF16)
        do_scr[cols] = scaled.T.astype(BF16)
    krow = pl.multiple_of(feats + h * HD, HD)
    vrow = pl.multiple_of(2 * feats + h * HD, HD)
    for q in range(lay.blocks):
        cols = slice(q * BK, (q + 1) * BK)
        dq = 0.0
        for k in lay.keys[q]:
            t = lay.tile[(q, k)]
            rows = slice(k * BK, (k + 1) * BK)
            dp = dot(qkvn_ref[2 * heads + h, rows], dot_scr[:, cols])
            ds = (e_ref[0, t].astype(F32) * (dp - deltas[q])).astype(BF16)
            ds_scr[h, t] = ds
            dq = dq + dot(qkvt_ref[pl.ds(krow, HD), rows], ds)
        dt_scr[pl.ds(hrow, HD), cols] = (dq * HD**-0.5).astype(BF16)

    @pl.when(h == heads - 1)
    def _():
        wo_second.wait_recv()
        scatter(
            heads,
            gwo_ref[me].astype(F32) + wo_near[0].astype(F32) + wo_far[...].astype(F32),
        )

    @pl.when(h == 1)
    def _():
        for copy in wo_first:
            copy.wait_recv()
        wo_send[...] = (gwo_ref[across].astype(F32) + wo_near[1].astype(F32)).astype(BF16)
        wo_second.start()

    for k in range(lay.blocks):
        rows = slice(k * BK, (k + 1) * BK)
        dk, dv = 0.0, 0.0
        for q in range(lay.blocks):
            if k in lay.keys[q]:
                t = lay.tile[(q, k)]
                cols = slice(q * BK, (q + 1) * BK)
                dk = dk + dot(ds_scr[h, t], qkvn_ref[h, cols])
                dv = dv + dot(e_ref[0, t], do_scr[cols])
        dt_scr[pl.ds(krow, HD), rows] = dk.T.astype(BF16)
        dt_scr[pl.ds(vrow, HD), rows] = dv.T.astype(BF16)

    for head in range(1, heads):

        @pl.when(h == head)
        def _():
            pass_on(head - 1)

    @pl.when(h == heads - 1)
    def _():
        collect(0)

    d_all = jnp.concatenate(
        [dt_scr[pl.ds(row, HD)] for row in (hrow, krow, vrow)], axis=0
    )
    grad = dot(d_all, h1_ref[...])
    for head in range(heads):

        @pl.when(h == head)
        def _():
            scatter(head, grad)

    def distances(head):
        column = lax.broadcasted_iota(jnp.int32, bias_scr.shape[1:], 1) == me * heads + head
        span = buckets_ref.shape[0]
        number = lax.broadcasted_iota(jnp.int32, (bias_scr.shape[1], span), 0)
        pieces = [jnp.zeros((1, BK), F32) for _ in range(lay.distances + 1)]
        for d in range(lay.distances):
            tile = 0.0
            for (q, k), t in lay.tile.items():
                if lay.distance(q, k) == d:
                    tile = tile + ds_scr[head, t].astype(F32)
            sums = diagonal_sums(tile)
            pieces[d + 1] = pieces[d + 1] + sums[:, :BK]
            pieces[d] = pieces[d] + sums[:, BK:]
        by_distance = jnp.concatenate(pieces[1:], axis=1)
        hot = buckets_ref[...].reshape(1, span) == number
        summed = jnp.sum(jnp.where(hot, by_distance, 0.0), axis=1, keepdims=True)
        bias_scr[0] += jnp.where(column, summed, 0.0)

    def spread_x(part):
        y_copy(part).wait_recv()
        for k in others:
            for i in range(2):
                x_copy(part, k, i).start()
        for i in range(2):
            core_copy(part, 0, i).start()

    def spread_core(part):
        for k in others:
            for i in range(2):
                x_copy(part, k, i).wait_recv()
                core_copy(part, k, i).start()

    @pl.when(h == heads - 1)
    def _():
        half = lay.prompt_rows
        for k in (1, 3, 2, 0):
            c = flip(me, k)
            parts = [dt_scr[:, pl.ds(pl.multiple_of(c * half, 128), half)]]
            for j in range(lay.cont_count):
                first = lay.spread * (half + j * lay.cont_rows) + c * lay.cont_rows
                parts.append(dt_scr[:, pl.ds(pl.multiple_of(first, 128), lay.cont_rows)])
            block = jnp.concatenate(parts, axis=1).T
            dh_scr[k] = dot_nt(block, w_ref[...]).astype(BF16)
            if k == 1:
                dh_first[0].start()
            if k == 3:
                dh_first[1].start()
        last, wo = heads - 1, heads
        pass_on(wo)
        collect(1)
        gathered(0)
        for copy in dh_first:
            copy.wait_recv()
        dh_scr[2] = (dh_scr[2].astype(F32) + dh_near[1].astype(F32)).astype(BF16)
        dh_second.start()
        dh_ref[...] = dh_scr[0].astype(F32) + dh_near[0].astype(F32)
        pass_on(last)
        distances(0)
        spread_x(0)
        gathered(1)
        collect(wo)
        collect(last)
        made_copy(2).start()
        made_copy(1).start()
        for head in range(1, heads):
            distances(head)
        small_start(0)
        spread_core(0)
        spread_x(1)
        gathered(wo)
        gathered(last)
        small, bias = small_sum(0)
        small_scr[1], bias_scr[1] = small, bias
        small_start(1)
        spread_core(1)
        spread_x(wo)
        spread_x(last)
        small, bias = small_sum(1)
        small_scr[2], bias_scr[2] = small, bias
        small_start(2)
        spread_core(wo)
        spread_core(last)
        small, bias = small_sum(2)
        small_ref[...] = small
        bias_ref[...] = bias
        for part in range(heads + 1):
            for k in range(groups):
                for i in range(2):
                    core_copy(part, k, i).wait()
            for k in others:
                half_copy(part, k).wait_send()
                for i in range(2):
                    x_copy(part, k, i).wait_send()
            y_copy(part).wait_send()
            for k in range(1, peers):
                spread_copy(part, k).wait_send()
                scatter_copy(part, k).wait_send()
        for stage in range(3):
            for k in range(1, stages[stage][2]):
                for copy in small_copies(stage, k):
                    copy.wait_send()
        for copy in wo_first:
            copy.wait_send()
        wo_second.wait_send()
        for copy in dh_first:
            copy.wait_send()
        dh_second.wait()
        for n in range(2):
            for copy in second_copies(n):
                copy.wait()
        for k in range(1, peers):
            made_copy(k).wait()


def rear(lay, heads, groups, peers, *args):
    da, e, qkvn, qkvt, ot, rl, h1, w, buckets, gsmall, gwo, made, gin, ginr, gout, goutr = args
    width = h1.shape[1]
    feats = heads * HD
    parts = heads + 1
    small_rows = -(-gsmall.shape[0] // 8) * 8
    rows, lanes = feats // peers, width // groups
    dma = pltpu.SemaphoreType.DMA
    anywhere = pl.BlockSpec(memory_space=pl.ANY)
    links = groups + peers + lay.spread

    def once(array):
        return pl.BlockSpec(
            array.shape, lambda h: (0,) * len(array.shape), pipeline_mode=pl.Buffered(1)
        )

    def result(shape, dtype):
        return jax.ShapeDtypeStruct(shape, dtype)

    kept = (
        result((lay.tokens, width), F32),
        result((small_rows, width), F32),
        result((BUCKETS, 128), F32),
    )
    return pl.pallas_call(
        functools.partial(rear_kernel, lay, heads, groups, peers),
        grid=(heads,),
        in_specs=[
            once(da),
            pl.BlockSpec((1, lay.tiles, BK, BK), lambda h: (h, 0, 0, 0)),
            once(qkvn),
            once(qkvt),
            once(ot),
            pl.BlockSpec((1, 1, lay.total), lambda h: (h, 0, 0)),
            once(h1),
            once(w),
            once(buckets),
            once(gsmall),
            once(gwo),
        ]
        + [anywhere] * 5,
        out_specs=tuple(once(k) for k in kept) + (anywhere,) * 7,
        out_shape=kept
        + (
            result(made.shape, BF16),
            result((max(groups - 1, 1), *gin.shape[1:]), BF16),
            result(ginr.shape[1:], BF16),
            result((max(groups - 1, 1), *gout.shape[1:]), BF16),
            result(goutr.shape[1:], BF16),
            result((lay.tokens, width), BF16),
            result((parts, groups, lay.spread, peers, rows, lanes), BF16),
        ),
        scratch_shapes=[
            VMEM((heads, lay.tiles, BK, BK), BF16),
            VMEM((HD, lay.total), BF16),
            VMEM((lay.total, HD), BF16),
            VMEM((3 * feats, lay.total), BF16),
            VMEM((4, lay.tokens, width), BF16),
            VMEM((2, lay.tokens, width), BF16),
            VMEM((2, feats, width), BF16),
            VMEM((feats, width), BF16),
            VMEM((feats, width), BF16),
            VMEM((parts, groups, peers, rows, lanes), BF16),
            VMEM((parts, groups, peers, rows, lanes), BF16),
            VMEM((parts, peers, rows, lanes), BF16),
            VMEM((parts, rows, lanes), BF16),
            VMEM((3, small_rows, width), F32),
            VMEM((links, small_rows, width), F32),
            VMEM((3, BUCKETS, 128), F32),
            VMEM((links, BUCKETS, 128), F32),
            dma((2, peers)),
            dma((2, 2, groups)),
            dma((2, 3)),
            dma((2, 3)),
            dma((parts, groups)),
            dma((parts, groups)),
            dma((parts, peers)),
            dma((parts, peers)),
            dma((parts, peers)),
            dma((parts, peers)),
            dma((2, parts)),
            dma((parts, groups, 2)),
            dma((parts, groups, 2)),
            dma((parts, groups, 2)),
            dma((parts, groups, 2)),
            dma((links,)),
            dma((links,)),
            dma((links,)),
            dma((links,)),
        ],
        compiler_params=pltpu.CompilerParams(
            vmem_limit_bytes=63 * MIB, collective_id=2, has_side_effects=True
        ),
        name="rear",
    )(*args)


def finish_kernel(lay, heads, groups, peers, capacity, count, *refs):
    names = FINISH_LOADED + FINISH_KEPT
    source = dict(zip(names, refs))
    refs = refs[len(names) :]
    target = dict(zip(FINISH_STORED, refs))
    gbias_ref, ggain_ref, ggain2_ref, grouter_ref = refs[len(FINISH_STORED) : count]
    refs = refs[count:]
    names = [name for name in FINISH_LOADED if name not in ("made", "back")]
    held = dict(zip(names + FINISH_STORED, refs))
    made_scr, turn_scr, in_sem, out_sem = refs[len(held) :]
    held["made"], held["back"] = made_scr.at[0], made_scr.at[pl.ds(1, peers - 1)]
    group, high = lax.axis_index("dp"), lax.axis_index("context") // 2
    expert = lax.axis_index("expert")
    own = {"made": 0, "gin": group, "ginr": high, "gout": group, "goutr": high}
    loads = {}
    for n, name in enumerate(FINISH_LOADED):
        view = source[name].at[own[name]] if name in own else source[name]
        if name == "back":
            view = view.at[pl.ds(1, peers - 1)]
        loads[name] = pltpu.make_async_copy(view, held[name], in_sem.at[n])
        loads[name].start()
    stores = {
        name: pltpu.make_async_copy(held[name], target[name], out_sem.at[n])
        for n, name in enumerate(FINISH_STORED)
    }

    def take(name):
        loads[name].wait()
        return held[name]

    def give(name, value):
        held[name][...] = value
        stores[name].start()

    half = lay.prompt_rows
    tokens = lay.tokens
    feats = heads * HD
    width = source["gain"].shape[0]
    gain = source["gain"][...].reshape(1, width)
    cols, gates = source["cols"], source["gates"]
    for side in ("", "r"):
        for name in ("gin", "gout"):
            total = take(name + side)[...].astype(F32)
            far = take(name + side + "_far")
            if side:
                total = total + far[...].astype(F32)
            else:
                for k in range(groups - 1):
                    total = total + far[k].astype(F32)
            spot = held[name + "_out"]
            size = total.shape[1]
            if side:
                spot[:, size:] = total
                stores[name + "_out"].start()
            else:
                spot[:, :size] = total

    out = take("mid")[...]
    take("made")
    take("back")
    slots = peers * capacity
    lane = lax.broadcasted_iota(jnp.int32, (1, slots), 1)
    number = lane
    for k in range(peers):
        shift = (flip(expert, k) - k) * capacity
        inside = (lane >= k * capacity) & (lane < (k + 1) * capacity)
        number = number + jnp.where(inside, shift, 0)
    number = number.astype(F32)
    blocks = made_scr[...].reshape(slots, width)
    for i in range(2):
        pick = jnp.where(cols[:, i : i + 1] == number, 1.0, 0.0).astype(BF16)
        out = out + gates[:, i : i + 1] * dot(pick, blocks)
    give("outp", out[:half].astype(BF16))
    give("outc", out[half:].astype(BF16))

    x = jnp.concatenate([take("xp")[...], take("xc")[...]], axis=0).astype(F32)
    dh1 = take("dh")[...] + take("dh_far")[...].astype(F32)
    r = lax.rsqrt(jnp.mean(x * x, axis=1, keepdims=True) + EPSILON)
    w = dh1 * gain
    mean = jnp.mean(w * x, axis=1, keepdims=True)
    dx = take("dmid")[...] + r * w - (r * r * r) * x * mean
    give("dxp", dx[:half])
    give("dxc", dx[half:])

    small_ref, bias_ref = source["small"], source["bias"]
    ggain2_ref[...] = small_ref[0:1].reshape(ggain2_ref.shape)
    grouter_ref[...] = small_ref[1 : 1 + grouter_ref.shape[0]]
    pad = jnp.concatenate([bias_ref[...], jnp.zeros((128 - BUCKETS, 128), F32)], axis=0)
    gbias_ref[...] = pad.T[: gbias_ref.shape[0], :BUCKETS]

    sums = take("sums")
    lanes = sums.shape[5]
    gwo = held["gwo"]
    for c in range(lay.spread):
        for i in range(groups):
            gwo[c * feats : (c + 1) * feats, i * lanes : (i + 1) * lanes] = (
                sums[heads, i, c].reshape(feats, lanes).astype(F32)
            )
    stores["gwo"].start()
    gained = 0.0
    for n, name in enumerate("qkv"):
        for c in range(lay.spread):
            for head in range(heads):
                to = c * feats + head * HD
                for i in range(groups):
                    block = sums[head, i, c].reshape(feats, lanes)
                    turn_scr[to : to + HD, i * lanes : (i + 1) * lanes] = block[
                        n * HD : (n + 1) * HD
                    ]
        grad = turn_scr[...].T.astype(F32)
        give("g" + name, grad)
        weight = take("w" + name)[...].astype(F32)
        gained = gained + jnp.sum(grad * weight, axis=1, keepdims=True)
    gained = jnp.broadcast_to(gained, (width, 128)).T[0:1]
    ggain_ref[...] = (gained / gain).reshape(ggain_ref.shape)
    for copy in stores.values():
        copy.wait()


FINISH_LOADED = [
    "gin",
    "gin_far",
    "gout",
    "gout_far",
    "ginr",
    "ginr_far",
    "goutr",
    "goutr_far",
    "mid",
    "made",
    "back",
    "xp",
    "xc",
    "dh",
    "dh_far",
    "dmid",
    "sums",
    "wq",
    "wk",
    "wv",
]
FINISH_KEPT = [
    "cols",
    "gates",
    "gain",
    "small",
    "bias",
]
FINISH_STORED = [
    "gin_out",
    "gout_out",
    "outp",
    "outc",
    "dxp",
    "dxc",
    "gwo",
    "gq",
    "gk",
    "gv",
]


def finish(lay, heads, groups, peers, capacity, experts, head_count, given):
    width = given["xp"].shape[1]
    rest = lay.tokens - lay.prompt_rows

    def result(shape, dtype=F32):
        return jax.ShapeDtypeStruct(shape, dtype)

    def loaded(name):
        shape = given[name].shape
        if name in ("made", "gin", "ginr", "gout", "goutr"):
            shape = shape[1:]
        return VMEM(shape, given[name].dtype)

    in_rows, in_lanes = given["gin"].shape[1:]
    out_rows, out_lanes = given["gout"].shape[1:]
    stored = (
        result((in_rows, 2 * in_lanes)),
        result((out_rows, 2 * out_lanes)),
        result((lay.prompt_rows, width), BF16),
        result((rest, width), BF16),
        result((lay.prompt_rows, width)),
        result((rest, width)),
        result((width, width)),
        result((width, width)),
        result((width, width)),
        result((width, width)),
    )
    kept = (
        result((head_count, BUCKETS)),
        result((width,)),
        result((width,)),
        result((experts, width)),
    )
    anywhere = pl.BlockSpec(memory_space=pl.ANY)
    inside = pl.BlockSpec(memory_space=VMEM)
    dma = pltpu.SemaphoreType.DMA
    return pl.pallas_call(
        functools.partial(
            finish_kernel, lay, heads, groups, peers, capacity, len(stored) + len(kept)
        ),
        in_specs=[anywhere] * len(FINISH_LOADED) + [inside] * len(FINISH_KEPT),
        out_specs=(anywhere,) * len(stored) + (inside,) * len(kept),
        out_shape=stored + kept,
        scratch_shapes=[loaded(name) for name in FINISH_LOADED if name not in ("made", "back")]
        + [VMEM(s.shape, s.dtype) for s in stored]
        + [
            VMEM(given["back"].shape, BF16),
            VMEM((width, width), BF16),
            dma((len(FINISH_LOADED),)),
            dma((len(stored),)),
        ],
        compiler_params=pltpu.CompilerParams(vmem_limit_bytes=60 * MIB),
        name="finish",
    )(*[given[name] for name in FINISH_LOADED + FINISH_KEPT])


def body(
    prompt_in,
    cont_in,
    prompt_route,
    cont_route,
    order,
    buckets,
    attn_gain,
    w_query,
    w_key,
    w_value,
    w_attn_out,
    rel_bias,
    ffn_gain,
    router,
    w_in,
    w_out,
    prompt_cot,
    cont_cot,
):
    prompt_rows = prompt_in.shape[1]
    cont_count = cont_in.shape[1]
    cont_rows = cont_in.shape[2]
    width = prompt_in.shape[2]
    spread = lax.axis_size("context")
    peers = lax.axis_size("expert")
    groups = lax.axis_size("dp")
    lay = Layout(spread, prompt_rows, cont_count, cont_rows)
    tokens = lay.tokens
    head_count = rel_bias.shape[1]
    heads = head_count // spread
    experts = peers * w_in.shape[0]
    capacity = 9 * tokens * 2 // (8 * experts)
    rest = cont_count * cont_rows
    xp, xc = prompt_in.reshape(prompt_rows, width), cont_in.reshape(rest, width)
    zp, zc = prompt_cot.reshape(prompt_rows, width), cont_cot.reshape(rest, width)
    router_t, bias_t = router.T, rel_bias.T
    h1, qkvn, qkvt, e, ot, rl, weights, cols, rows, at, dz_slots = front(
        lay,
        heads,
        peers,
        capacity,
        xp,
        xc,
        prompt_route[0].T,
        cont_route[0].swapaxes(1, 2),
        order.reshape(1, tokens),
        buckets,
        attn_gain,
        w_query,
        w_key,
        w_value,
        bias_t,
        zp,
        zc,
    )
    pairs = groups * spread // 2
    mid, gates, dmid, g_wo, g_small, made, gin, ginr, gout, goutr, dattn_t = experts_layer(
        peers,
        pairs,
        spread,
        capacity,
        at.reshape(width, tokens),
        xp,
        xc,
        w_attn_out,
        ffn_gain,
        router_t,
        cols,
        rows,
        zp,
        zc,
        w_in,
        w_out,
        dz_slots,
    )
    dh, small, bias, back, gin_far, ginr_far, gout_far, goutr_far, dh_far, sums = rear(
        lay,
        heads,
        groups,
        peers,
        dattn_t,
        e,
        qkvn,
        qkvt,
        ot,
        rl,
        h1,
        weights,
        buckets,
        g_small,
        g_wo.reshape(spread, width // spread, width),
        made,
        gin,
        ginr,
        gout,
        goutr,
    )
    given = dict(
        gin=gin, gin_far=gin_far, ginr=ginr, ginr_far=ginr_far,
        gout=gout, gout_far=gout_far, goutr=goutr, goutr_far=goutr_far,
        mid=mid, made=made, back=back, xp=xp, xc=xc, dh=dh, dh_far=dh_far, dmid=dmid,
        sums=sums, wq=w_query, wk=w_key, wv=w_value,
        cols=cols, gates=gates, gain=attn_gain, small=small, bias=bias,
    )
    outs = finish(lay, heads, groups, peers, capacity, experts, head_count, given)
    g_in, g_out, outp, outc, dxp, dxc, g_wo, g_q, g_k, g_v, g_bias, g_gain, g_gain2, g_router = outs
    return (
        outp[None],
        outc.reshape(1, cont_count, cont_rows, width),
        dxp[None],
        dxc.reshape(1, cont_count, cont_rows, width),
        g_gain,
        g_q,
        g_k,
        g_v,
        g_wo,
        g_bias.T,
        g_gain2,
        g_router.T,
        g_in[None],
        g_out[None],
    )


def solution(mesh):
    split = P(("dp", "expert"), "context", None)
    split_cont = P(("dp", "expert"), None, "context", None)
    whole = P()
    expert = P("expert", None, None)
    grad = P("expert", ("dp", "context"), None)
    return jax.shard_map(
        body,
        mesh=mesh,
        in_specs=(split, split_cont, split, split_cont, split)
        + (whole,) * 9
        + (expert, expert, split, split_cont),
        out_specs=(split, split_cont, split, split_cont) + (whole,) * 8 + (grad, grad),
        check_vma=False,
    )
```
